256 devices in a mesh: batch: 2 (over z_hi), narrow: 8 (over x, core), wide: 16 (over z_lo, y).
Axes of the slice: x: 4, y: 4, z: 8 (z_hi: 2, z_lo: 4; z = z_hi * 4 + z_lo), core: 2. Of those that a mesh axis runs over, the one named last changes fastest.
Arguments:
- inputs: bfloat16 [2, 16384, 256], P('batch', ('narrow', 'wide')), may hold values from -6 to 6
- in_weight: bfloat16 [256, 768], replicated, may hold values from -0.375 to 0.375
- short_kernel: float32 [3, 768], replicated, may hold values from -3 to 3
- filter_one: float32 [16384, 256], P(('narrow', 'wide')), as said below
- filter_two: float32 [16384, 256], P(('narrow', 'wide')), as said below
- out_weight: bfloat16 [256, 256], replicated, may hold values from -0.375 to 0.375
- out_grad: bfloat16 [2, 16384, 256], P('batch', ('narrow', 'wide')), may hold values from -6 to 6
Outputs:
- outputs: bfloat16 [2, 16384, 256], P('batch', ('narrow', 'wide'))
- grad_inputs: bfloat16 [2, 16384, 256], P('batch', ('narrow', 'wide'))
- grad_in_weight: float32 [256, 768], replicated
- grad_short: float32 [3, 768], replicated
- grad_filter_one: float32 [16384, 256], P(('narrow', 'wide'))
- grad_filter_two: float32 [16384, 256], P(('narrow', 'wide'))
- grad_out_weight: float32 [256, 256], replicated
The draws below stay inside these ranges and needn't reach their ends.
Inputs may be any that keep to these rules, and one draw needn't show every extreme that they name: `filter_one`: A long filter's value at each position and channel. `filter_two`: A long filter's value at each position and channel.
All inputs are finite; a program needn't handle non-finite values.
Results may differ from the reference program's by a relative error of at most 0.005.
Values may be sent and summed in bfloat16 or wider, within the bound.
No kernel may reach another device: no remote copies, remote signals or barrier semaphores. Data moves between devices by JAX's collectives and lax.ppermute only.
A program may use at most 64 MiB of HBM per device.

```python
import math
import jax
import jax.numpy as jnp

D = 256
SEQ_LEN = 16384
BATCH = 2


def draw_filter_one(key, part):
    key = jax.random.fold_in(key, 11)
    noise_key, rate_key = jax.random.split(key)
    noise_values = jnp.clip(jax.random.normal(noise_key, (SEQ_LEN, D), jnp.float32), -4.0, 4.0)
    log_length = jax.random.uniform(rate_key, (D,), jnp.float32, math.log(20.0), math.log(SEQ_LEN * 128.0))
    decay_length = jnp.exp(log_length)
    position = jnp.arange(SEQ_LEN, dtype=jnp.float32)[:, None]
    envelope = jnp.exp(-position / decay_length[None, :])
    amplitude = jnp.sqrt(2.0 / jnp.minimum(decay_length, SEQ_LEN * 1.0))
    return noise_values * envelope * amplitude[None, :]


def draw_filter_two(key, part):
    key = jax.random.fold_in(key, 12)
    noise_key, rate_key = jax.random.split(key)
    noise_values = jnp.clip(jax.random.normal(noise_key, (SEQ_LEN, D), jnp.float32), -4.0, 4.0)
    log_length = jax.random.uniform(rate_key, (D,), jnp.float32, math.log(20.0), math.log(SEQ_LEN * 128.0))
    decay_length = jnp.exp(log_length)
    position = jnp.arange(SEQ_LEN, dtype=jnp.float32)[:, None]
    envelope = jnp.exp(-position / decay_length[None, :])
    amplitude = jnp.sqrt(2.0 / jnp.minimum(decay_length, SEQ_LEN * 1.0))
    return noise_values * envelope * amplitude[None, :]


def level_of(rng, dims, shards, least, high):
    level, own = 1.0, jax.random.fold_in(rng, 6)
    for dim, blocks in shards:
        draws = jnp.exp(jax.random.uniform(jax.random.fold_in(own, dim), (blocks,), jnp.float32, least / len(shards), high / len(shards)))
        level = level * jnp.repeat(draws, dims[dim] // blocks).reshape([-1 if axis == dim else 1 for axis in range(len(dims))])
    return level


def bell_draw(key, extent, spread, most, cuts=(), kind=jnp.bfloat16):
    entries = spread * jax.random.normal(key, extent, jnp.float32)
    if cuts:
        entries = entries * level_of(key, extent, cuts, -0.22, 0.18)
    return jnp.clip(entries, -most, most).astype(kind)


def setup_inputs(seed: int = 0) -> dict:
    splits = jax.random.split(jax.random.key(seed), 8)
    return {
        "inputs": bell_draw(splits[0], (BATCH, SEQ_LEN, D), 1.0, 6.0, ((0, 2), (1, 128))),
        "in_weight": bell_draw(splits[1], (D, 3 * D), D ** -0.5, 0.375),
        "short_kernel": bell_draw(splits[2], (3, 3 * D), 0.6, 3.0, (), jnp.float32),
        "filter_one": draw_filter_one(jax.random.fold_in(splits[7], 71), 0),
        "filter_two": draw_filter_two(jax.random.fold_in(splits[7], 71), 0),
        "out_weight": bell_draw(splits[5], (D, D), D ** -0.5, 0.375),
        "out_grad": bell_draw(splits[6], (BATCH, SEQ_LEN, D), 1.0, 6.0, ((0, 2), (1, 128))),
    }


def causal_convolve(kernel_rows, signal_rows):
    length = kernel_rows.shape[0]
    padded = 2 * length
    product = jnp.fft.rfft(kernel_rows, n=padded, axis=0) * jnp.fft.rfft(signal_rows, n=padded, axis=0)
    return jnp.fft.irfft(product, n=padded, axis=0)[:length].astype(jnp.float32)


def correlate(kernel_rows, signal_rows):
    length = kernel_rows.shape[0]
    padded = 2 * length
    product = jnp.conj(jnp.fft.rfft(kernel_rows, n=padded, axis=0)) * jnp.fft.rfft(signal_rows, n=padded, axis=0)
    return jnp.fft.irfft(product, n=padded, axis=0)[:length].astype(jnp.float32)


def reference(inputs, in_weight, short_kernel, filter_one, filter_two, out_weight, out_grad):
    model_width = out_weight.shape[0]
    grad_scale = 1.0 / (BATCH * SEQ_LEN) ** 0.5
    outputs_list = []
    grad_inputs_list = []
    sum_in = jnp.zeros((model_width, 3 * model_width), jnp.float32)
    sum_out = jnp.zeros((model_width, model_width), jnp.float32)
    sum_kernel = jnp.zeros((3, 3 * model_width), jnp.float32)
    sum_one = jnp.zeros((SEQ_LEN, model_width), jnp.float32)
    sum_two = jnp.zeros((SEQ_LEN, model_width), jnp.float32)
    for member in range(BATCH):
        sequence = inputs[member]
        projected = jnp.dot(sequence, in_weight, preferred_element_type=jnp.float32)
        lagged_one = jnp.pad(projected, ((1, 0), (0, 0)))[:-1]
        lagged_two = jnp.pad(projected, ((2, 0), (0, 0)))[:-2]
        mixed_all = short_kernel[0] * projected + short_kernel[1] * lagged_one + short_kernel[2] * lagged_two
        value_part = mixed_all[:, :model_width]
        gate_one = mixed_all[:, model_width:2 * model_width]
        gate_two = mixed_all[:, 2 * model_width:]
        conv_one = causal_convolve(filter_one, value_part)
        gated_one = gate_one * conv_one
        conv_two = causal_convolve(filter_two, gated_one)
        pre_out = (gate_two * conv_two).astype(jnp.bfloat16)
        outputs_list.append(jnp.dot(pre_out, out_weight, preferred_element_type=jnp.float32).astype(jnp.bfloat16))
        cotangent = out_grad[member]
        grad_pre = jnp.dot(cotangent, out_weight.T, preferred_element_type=jnp.float32)
        sum_out = sum_out + jnp.dot(pre_out.T, cotangent, preferred_element_type=jnp.float32)
        grad_two = grad_pre * conv_two
        grad_conv_two = grad_pre * gate_two
        grad_gated = correlate(filter_two, grad_conv_two)
        sum_two = sum_two + correlate(gated_one, grad_conv_two)
        grad_one = grad_gated * conv_one
        grad_conv_one = grad_gated * gate_one
        grad_value = correlate(filter_one, grad_conv_one)
        sum_one = sum_one + correlate(value_part, grad_conv_one)
        grad_mixed = jnp.concatenate([grad_value, grad_one, grad_two], 1)
        ahead_one = jnp.pad(grad_mixed, ((0, 1), (0, 0)))[1:]
        ahead_two = jnp.pad(grad_mixed, ((0, 2), (0, 0)))[2:]
        grad_proj = (short_kernel[0] * grad_mixed + short_kernel[1] * ahead_one + short_kernel[2] * ahead_two).astype(jnp.bfloat16)
        kernel_terms = jnp.stack([jnp.sum(grad_mixed * projected, 0), jnp.sum(grad_mixed * lagged_one, 0), jnp.sum(grad_mixed * lagged_two, 0)])
        sum_kernel = sum_kernel + kernel_terms
        sum_in = sum_in + jnp.dot(sequence.T, grad_proj, preferred_element_type=jnp.float32)
        grad_inputs_list.append(jnp.dot(grad_proj, in_weight.T, preferred_element_type=jnp.float32).astype(jnp.bfloat16))
    return (jnp.stack(outputs_list), jnp.stack(grad_inputs_list), sum_in * grad_scale, sum_kernel * grad_scale, sum_one * grad_scale, sum_two * grad_scale, sum_out * grad_scale)
```

```python
import math

import jax
import jax.numpy as jnp
import numpy as np
from jax import lax
from jax.experimental import pallas as pl
from jax.experimental.pallas import tpu as pltpu
from jax.sharding import PartitionSpec as P

everyone = ("batch", "narrow", "wide")
vmem_limit = 56 * 1024 * 1024


def two_terms(table):
    high = table.astype(np.float32).astype(jnp.bfloat16)
    low = (table - high.astype(np.float64)).astype(np.float32).astype(jnp.bfloat16)
    return high, low


def transform_tables(blocks, rows):
    length = 2 * blocks * rows
    outer = np.arange(blocks) + 0.5
    step = 2.0 * math.pi * np.outer(outer, np.arange(blocks)) / (2 * blocks)
    turn = 2.0 * math.pi * np.outer(outer, np.arange(rows)) / length
    inner = 2.0 * math.pi * np.outer(np.arange(rows), np.arange(rows)) / rows
    first = np.concatenate([np.cos(step), -np.sin(step)], 0)
    c, s = np.cos(inner), np.sin(inner)
    second = np.block([[c, -s], [s, c]])
    second_back = np.block([[c, s], [-s, c]])
    first_back = np.concatenate([np.cos(step).T, -np.sin(step).T], 1) * (2.0 / length)
    tables = []
    for table in (first, second, second_back, first_back):
        tables.extend(two_terms(table))
    tables.append(np.cos(turn).astype(np.float32))
    tables.append(np.sin(turn).astype(np.float32))
    return tables


def bf16_dot(a, b):
    return jnp.dot(a, b, preferred_element_type=jnp.float32)


def split(x):
    high = x.astype(jnp.bfloat16)
    low = (x - high.astype(jnp.float32)).astype(jnp.bfloat16)
    return high, low


def table_left(high, low, x):
    x_high, x_low = split(x)
    return bf16_dot(high, x_high) + bf16_dot(low, x_high) + bf16_dot(high, x_low)


def table_right(x, high, low):
    x_high, x_low = split(x)
    return bf16_dot(x_high, high) + bf16_dot(x_high, low) + bf16_dot(x_low, high)


def pack_kernel(seq_ref, in_weight_ref, one_ref, two_ref, out_weight_ref, grad_ref, out_ref, rows_ref):
    width = out_weight_ref.shape[0]
    slots = rows_ref.shape[0] // width
    contract_first = (((0,), (1,)), ((), ()))
    contract_last = (((1,), (1,)), ((), ()))
    seq = seq_ref[0]

    def put(index, x):
        rows_ref[pl.ds(index, width, stride=slots), :] = x

    def put_two(index, x):
        high = x.astype(jnp.bfloat16).astype(jnp.float32)
        put(index, high)
        put(index + 1, x - high)

    projected = [
        lax.dot_general(
            in_weight_ref[:, group * width : (group + 1) * width],
            seq,
            contract_first,
            preferred_element_type=jnp.float32,
        )
        for group in range(3)
    ]
    put(0, projected[0])
    put_two(1, projected[1])
    put_two(3, projected[2])
    put(
        5,
        lax.dot_general(
            out_weight_ref[...], grad_ref[0], contract_last, preferred_element_type=jnp.float32
        ),
    )
    chosen = jnp.where(lax.axis_index("batch") == 0, one_ref[...], two_ref[...])
    put_two(6, chosen.T)
    out_ref[...] = rows_ref[...].reshape(out_ref.shape).astype(jnp.bfloat16)


def convolve_kernel(
    in_ref,
    short_ref,
    first_high,
    first_low,
    second_high,
    second_low,
    second_back_high,
    second_back_low,
    first_back_high,
    first_back_low,
    turn_cos_ref,
    turn_sin_ref,
    out_ref,
    rows_ref,
    send_ref,
):
    sources, slots, rows = in_ref.shape
    blocks = sources // 2
    width = short_ref.shape[1] // 3
    scale = 1.0 / math.sqrt(sources * rows)
    turn_cos = turn_cos_ref[...]
    turn_sin = turn_sin_ref[...]
    lane = lax.broadcasted_iota(jnp.int32, (blocks, rows), 1)
    block = lax.broadcasted_iota(jnp.int32, (blocks, rows), 0)

    rows_ref[...] = in_ref[...].astype(jnp.float32).reshape(sources * slots, rows)

    def row(member, index):
        return rows_ref[pl.ds(member * blocks * slots + index, blocks, stride=slots), :]

    def later(x, distance):
        moved = pltpu.roll(x, distance, 1)
        carried = jnp.where(block == 0, 0.0, pltpu.roll(moved, 1, 0))
        return jnp.where(lane < distance, carried, moved)

    def earlier(x, distance):
        moved = pltpu.roll(x, rows - distance, 1)
        carried = jnp.where(block == blocks - 1, 0.0, pltpu.roll(moved, blocks - 1, 0))
        return jnp.where(lane >= rows - distance, carried, moved)

    def forward(signals):
        outer = table_left(first_high[...], first_low[...], jnp.concatenate(signals, 1))
        turned = []
        for i in range(len(signals)):
            re = outer[:blocks, i * rows : (i + 1) * rows]
            im = outer[blocks:, i * rows : (i + 1) * rows]
            turned.append(
                jnp.concatenate(
                    [re * turn_cos + im * turn_sin, im * turn_cos - re * turn_sin], 1
                )
            )
        inner = table_right(jnp.concatenate(turned, 0), second_high[...], second_low[...])
        return [
            (inner[i * blocks : (i + 1) * blocks, :rows], inner[i * blocks : (i + 1) * blocks, rows:])
            for i in range(len(signals))
        ]

    def backward(spectra):
        stacked = jnp.concatenate([jnp.concatenate(pair, 1) for pair in spectra], 0)
        inner = table_right(stacked, second_back_high[...], second_back_low[...])
        turned = []
        for i in range(len(spectra)):
            re = inner[i * blocks : (i + 1) * blocks, :rows]
            im = inner[i * blocks : (i + 1) * blocks, rows:]
            turned.append(
                jnp.concatenate(
                    [re * turn_cos - im * turn_sin, im * turn_cos + re * turn_sin], 0
                )
            )
        outer = table_left(first_back_high[...], first_back_low[...], jnp.concatenate(turned, 1))
        return [outer[:, i * rows : (i + 1) * rows] for i in range(len(spectra))]

    def times(a, b):
        return a[0] * b[0] - a[1] * b[1], a[0] * b[1] + a[1] * b[0]

    def conj_times(a, b):
        return a[0] * b[0] + a[1] * b[1], a[0] * b[1] - a[1] * b[0]

    def added(a, b):
        return a[0] + b[0], a[1] + b[1]

    mesh_place = (
        lax.axis_index("batch") * lax.axis_size("narrow") + lax.axis_index("narrow")
    ) * lax.axis_size("wide") + lax.axis_index("wide")
    short = short_ref[...]
    short_lane = lax.broadcasted_iota(jnp.int32, short.shape, 1)
    taps = []
    for group in range(3):
        column = jnp.sum(
            jnp.where(short_lane == mesh_place + group * width, short, 0.0), axis=1, keepdims=True
        )
        taps.append([column[tap : tap + 1, :] for tap in range(3)])

    projected, lagged_one, lagged_two, mixed, pre = [], [], [], [], []
    for member in range(2):
        now = [
            row(member, 0),
            row(member, 1) + row(member, 2),
            row(member, 3) + row(member, 4),
        ]
        one = [later(x, 1) for x in now]
        two = [later(x, 2) for x in now]
        projected.append(now)
        lagged_one.append(one)
        lagged_two.append(two)
        mixed.append(
            [
                taps[g][0] * now[g] + taps[g][1] * one[g] + taps[g][2] * two[g]
                for g in range(3)
            ]
        )
        pre.append(row(member, 5))
    members = range(2)
    grad_conv_two = [pre[m] * mixed[m][2] for m in members]
    spectra = forward(
        [row(m, 6) + row(m, 7) for m in members] + [mixed[m][0] for m in members] + grad_conv_two
    )
    one_spec, two_spec = spectra[0], spectra[1]
    value_spec, conv_two_spec = spectra[2:4], spectra[4:6]
    found = backward(
        [times(one_spec, value_spec[m]) for m in members]
        + [conj_times(two_spec, conv_two_spec[m]) for m in members]
    )
    conv_one, grad_gated = found[:2], found[2:]
    spectra = forward(
        [mixed[m][1] * conv_one[m] for m in members]
        + [mixed[m][1] * grad_gated[m] for m in members]
    )
    gated_spec, conv_one_spec = spectra[:2], spectra[2:]
    found = backward(
        [times(two_spec, gated_spec[m]) for m in members]
        + [conj_times(one_spec, conv_one_spec[m]) for m in members]
        + [
            added(*[conj_times(value_spec[m], conv_one_spec[m]) for m in members]),
            added(*[conj_times(gated_spec[m], conv_two_spec[m]) for m in members]),
        ]
    )
    conv_two, grad_value = found[:2], found[2:4]
    grad_filters = [found[4] * scale, found[5] * scale]

    def put(member, index, x):
        send_ref[pl.ds(member * blocks * slots + index, blocks, stride=slots), :] = x

    sums = [[0.0] * 3 for _ in range(3)]
    for m in members:
        put(m, 0, mixed[m][2] * conv_two[m])
        grads = [grad_value[m], grad_gated[m] * conv_one[m], pre[m] * conv_two[m]]
        for g in range(3):
            put(
                m,
                1 + g,
                taps[g][0] * grads[g]
                + taps[g][1] * earlier(grads[g], 1)
                + taps[g][2] * earlier(grads[g], 2),
            )
            for tap, lagged in enumerate((projected, lagged_one, lagged_two)):
                sums[g][tap] = sums[g][tap] + jnp.sum(
                    jnp.sum(grads[g] * lagged[m][g], axis=0, keepdims=True), axis=1, keepdims=True
                )
        put(m, 4, grad_filters[0])
        put(m, 5, grad_filters[1])
    sum_lane = lax.broadcasted_iota(jnp.int32, (1, rows), 1)
    line = jnp.zeros((1, rows), jnp.float32)
    for g in range(3):
        for tap in range(3):
            total = sums[g][tap] * scale
            high = total.astype(jnp.bfloat16).astype(jnp.float32)
            line = jnp.where(sum_lane == g * 3 + tap, high, line)
            line = jnp.where(sum_lane == 16 + g * 3 + tap, total - high, line)
    line = jnp.broadcast_to(line, (blocks, rows))
    for m in members:
        put(m, 6, line)
        put(m, 7, jnp.zeros((blocks, rows), jnp.float32))
    out_ref[...] = send_ref[...].reshape(out_ref.shape).astype(jnp.bfloat16)


def finish_kernel(
    in_ref,
    seq_ref,
    in_weight_ref,
    out_weight_ref,
    grad_ref,
    outputs_ref,
    grad_inputs_ref,
    short_ref,
    one_ref,
    two_ref,
    part_ref,
    rows_ref,
):
    width, slots, rows = in_ref.shape
    contract_last = (((1,), (1,)), ((), ()))
    rows_ref[...] = in_ref[...].astype(jnp.float32).reshape(width * slots, rows)

    def column(index):
        return rows_ref[pl.ds(index, width, stride=slots), :]

    pre_out = column(0)
    outputs_ref[0] = bf16_dot(pre_out.T.astype(jnp.bfloat16), out_weight_ref[...]).astype(
        jnp.bfloat16
    )
    parts = []
    seq_turned = seq_ref[0].astype(jnp.float32).T.astype(jnp.bfloat16)
    total = None
    for group in range(3):
        grad = column(1 + group).T.astype(jnp.bfloat16)
        term = lax.dot_general(
            grad,
            in_weight_ref[:, group * width : (group + 1) * width],
            contract_last,
            preferred_element_type=jnp.float32,
        )
        total = term if total is None else total + term
        parts.append(bf16_dot(seq_turned, grad))
    grad_inputs_ref[0] = total.astype(jnp.bfloat16)
    parts.append(bf16_dot(pre_out.astype(jnp.bfloat16), grad_ref[0]))
    for index, part in enumerate(parts):
        for half in range(2):
            place = (index * 2 + half) * width
            part_ref[place : place + width, :] = part[
                :, half * rows : (half + 1) * rows
            ].astype(jnp.bfloat16)
    one_ref[...] = column(4).T
    two_ref[...] = column(5).T
    sums = column(6).T
    for group in range(3):
        short_ref[:, group * width : (group + 1) * width] = (
            sums[group * 3 : group * 3 + 3, :] + sums[16 + group * 3 : 19 + group * 3, :]
        )


def add_kernel(in_ref, out_ref):
    scale = 1.0 / math.sqrt(in_ref.shape[0] * 128)
    total = jnp.sum(in_ref[...].astype(jnp.float32), axis=0) * scale
    out_ref[...] = jnp.broadcast_to(total[None], out_ref.shape).astype(jnp.bfloat16)


def place_kernel(in_ref, in_weight_ref, out_weight_ref):
    width, lanes = out_weight_ref.shape[0], in_ref.shape[1]
    for index in range(8):
        block = in_ref[index * width : (index + 1) * width, :].astype(jnp.float32)
        if index < 6:
            in_weight_ref[:, index * lanes : (index + 1) * lanes] = block
        else:
            out_weight_ref[:, (index - 6) * lanes : (index - 5) * lanes] = block


def call(kernel, out_shape, scratch=()):
    return pl.pallas_call(
        kernel,
        out_shape=out_shape,
        scratch_shapes=list(scratch),
        compiler_params=pltpu.CompilerParams(vmem_limit_bytes=vmem_limit),
    )


def exchange(x):
    return lax.all_to_all(x, everyone, split_axis=0, concat_axis=0, tiled=True)


def per_device(inputs, in_weight, short_kernel, filter_one, filter_two, out_weight, out_grad):
    width = out_weight.shape[0]
    rows = inputs.shape[1]
    devices = lax.axis_size(everyone)
    shape = jax.ShapeDtypeStruct
    f32, bf16 = jnp.float32, jnp.bfloat16
    scratch = pltpu.VMEM((devices * 8, rows), f32)
    packed = call(pack_kernel, shape((width, 8, rows), bf16), [scratch])(
        inputs, in_weight, filter_one, filter_two, out_weight, out_grad
    )
    received = exchange(packed)
    tables = [jnp.asarray(t) for t in transform_tables(devices // 2, rows)]
    back = call(convolve_kernel, shape((devices, 8, rows), bf16), [scratch, scratch])(
        received, short_kernel, *tables
    )
    home = exchange(back)
    outputs, grad_inputs, grad_short, grad_one, grad_two, part = call(
        finish_kernel,
        (
            shape((1, rows, width), bf16),
            shape((1, rows, width), bf16),
            shape((3, 3 * width), f32),
            shape((rows, width), f32),
            shape((rows, width), f32),
            shape((8 * width, rows), bf16),
        ),
        [scratch],
    )(home, inputs, in_weight, out_weight, out_grad)
    part = exchange(part.reshape(devices, 8 * width // devices, rows))
    whole = exchange(call(add_kernel, shape(part.shape, bf16))(part))
    grad_in_weight, grad_out_weight = call(
        place_kernel, (shape((width, 3 * width), f32), shape((width, width), f32))
    )(whole.reshape(8 * width, rows))
    return (
        outputs,
        grad_inputs,
        grad_in_weight,
        grad_short,
        grad_one,
        grad_two,
        grad_out_weight,
    )


def solution(mesh):
    split_rows = P("batch", ("narrow", "wide"), None)
    split_filter = P(("narrow", "wide"), None)
    return jax.shard_map(
        per_device,
        mesh=mesh,
        in_specs=(split_rows, P(), P(), split_filter, split_filter, P(), split_rows),
        out_specs=(split_rows, split_rows, P(), P(), split_filter, split_filter, P()),
        check_vma=False,
    )
```

```python
import functools
import math

import jax
import jax.numpy as jnp
import numpy as np
from jax import lax
from jax.experimental import pallas as pl
from jax.experimental.pallas import tpu as pltpu
from jax.sharding import Mesh
from jax.sharding import PartitionSpec as P

everyone = ("zh", "x", "core", "zl", "y")
vmem_limit = 56 * 1024 * 1024


def two_terms(table):
    high = table.astype(np.float32).astype(jnp.bfloat16)
    low = (table - high.astype(np.float64)).astype(np.float32).astype(jnp.bfloat16)
    return high, low


def transform_tables(blocks, rows):
    length = 2 * blocks * rows
    outer = np.arange(blocks) + 0.5
    step = 2.0 * math.pi * np.outer(outer, np.arange(blocks)) / (2 * blocks)
    turn = 2.0 * math.pi * np.outer(outer, np.arange(rows)) / length
    inner = 2.0 * math.pi * np.outer(np.arange(rows), np.arange(rows)) / rows
    first = np.concatenate([np.cos(step), -np.sin(step)], 0)
    c, s = np.cos(inner), np.sin(inner)
    second = np.block([[c, -s], [s, c]])
    second_back = np.block([[c, s], [-s, c]])
    first_back = np.concatenate([np.cos(step).T, -np.sin(step).T], 1) * (2.0 / length)
    tables = []
    for table in (first, second, second_back, first_back):
        tables.extend(two_terms(table))
    tables.append(np.cos(turn).astype(np.float32))
    tables.append(np.sin(turn).astype(np.float32))
    return tables


def bf16_dot(a, b):
    return jnp.dot(a, b, preferred_element_type=jnp.float32)


def split(x):
    high = x.astype(jnp.bfloat16)
    low = (x - high.astype(jnp.float32)).astype(jnp.bfloat16)
    return high, low


def table_left(high, low, x):
    x_high, x_low = split(x)
    return bf16_dot(high, x_high) + bf16_dot(low, x_high) + bf16_dot(high, x_low)


def table_right(x, high, low):
    x_high, x_low = split(x)
    return bf16_dot(x_high, high) + bf16_dot(x_high, low) + bf16_dot(x_low, high)


def pack_kernel(seq_ref, in_weight_ref, one_ref, two_ref, out_weight_ref, grad_ref, out_ref, both_ref, rows_ref):
    width = out_weight_ref.shape[0]
    slots = rows_ref.shape[0] // width
    contract_first = (((0,), (1,)), ((), ()))
    contract_last = (((1,), (1,)), ((), ()))
    seq = seq_ref[0]

    def put(index, x):
        rows_ref[pl.ds(index, width, stride=slots), :] = x

    def put_two(index, x):
        high = x.astype(jnp.bfloat16).astype(jnp.float32)
        put(index, high)
        put(index + 1, x - high)

    projected = [
        lax.dot_general(
            in_weight_ref[:, group * width : (group + 1) * width],
            seq,
            contract_first,
            preferred_element_type=jnp.float32,
        )
        for group in range(3)
    ]
    put(0, projected[0])
    put_two(1, projected[1])
    put_two(3, projected[2])
    put(
        5,
        lax.dot_general(
            out_weight_ref[...], grad_ref[0], contract_last, preferred_element_type=jnp.float32
        ),
    )
    chosen = jnp.where(lax.axis_index("zh") == 0, one_ref[...], two_ref[...])
    put_two(6, chosen.T)
    both_ref[:, :width] = seq
    both_ref[:, width:] = grad_ref[0]
    out_ref[...] = rows_ref[...].reshape(out_ref.shape).astype(jnp.bfloat16)


def convolve_kernel(
    in_ref,
    short_ref,
    first_high,
    first_low,
    second_high,
    second_low,
    second_back_high,
    second_back_low,
    first_back_high,
    first_back_low,
    turn_cos_ref,
    turn_sin_ref,
    out_ref,
    sums_ref,
    rows_ref,
):
    sources, slots, rows = in_ref.shape
    blocks = sources // 2
    width = short_ref.shape[1] // 3
    scale = 1.0 / math.sqrt(sources * rows)
    turn_cos = turn_cos_ref[...]
    turn_sin = turn_sin_ref[...]
    lane = lax.broadcasted_iota(jnp.int32, (blocks, rows), 1)
    block = lax.broadcasted_iota(jnp.int32, (blocks, rows), 0)

    rows_ref[...] = in_ref[...].astype(jnp.float32).reshape(sources * slots, rows)

    def row(member, index):
        return rows_ref[pl.ds(member * blocks * slots + index, blocks, stride=slots), :]

    def later(x, distance):
        moved = pltpu.roll(x, distance, 1)
        carried = jnp.where(block == 0, 0.0, pltpu.roll(moved, 1, 0))
        return jnp.where(lane < distance, carried, moved)

    def earlier(x, distance):
        moved = pltpu.roll(x, rows - distance, 1)
        carried = jnp.where(block == blocks - 1, 0.0, pltpu.roll(moved, blocks - 1, 0))
        return jnp.where(lane >= rows - distance, carried, moved)

    def forward(signals):
        outer = table_left(first_high[...], first_low[...], jnp.concatenate(signals, 1))
        turned = []
        for i in range(len(signals)):
            re = outer[:blocks, i * rows : (i + 1) * rows]
            im = outer[blocks:, i * rows : (i + 1) * rows]
            turned.append(
                jnp.concatenate(
                    [re * turn_cos + im * turn_sin, im * turn_cos - re * turn_sin], 1
                )
            )
        inner = table_right(jnp.concatenate(turned, 0), second_high[...], second_low[...])
        return [
            (inner[i * blocks : (i + 1) * blocks, :rows], inner[i * blocks : (i + 1) * blocks, rows:])
            for i in range(len(signals))
        ]

    def backward(spectra):
        stacked = jnp.concatenate([jnp.concatenate(pair, 1) for pair in spectra], 0)
        inner = table_right(stacked, second_back_high[...], second_back_low[...])
        turned = []
        for i in range(len(spectra)):
            re = inner[i * blocks : (i + 1) * blocks, :rows]
            im = inner[i * blocks : (i + 1) * blocks, rows:]
            turned.append(
                jnp.concatenate(
                    [re * turn_cos - im * turn_sin, im * turn_cos + re * turn_sin], 0
                )
            )
        outer = table_left(first_back_high[...], first_back_low[...], jnp.concatenate(turned, 1))
        return [outer[:, i * rows : (i + 1) * rows] for i in range(len(spectra))]

    def times(a, b):
        return a[0] * b[0] - a[1] * b[1], a[0] * b[1] + a[1] * b[0]

    def conj_times(a, b):
        return a[0] * b[0] + a[1] * b[1], a[0] * b[1] - a[1] * b[0]

    def added(a, b):
        return a[0] + b[0], a[1] + b[1]

    mesh_place = lax.axis_index(everyone)
    short = short_ref[...]
    short_lane = lax.broadcasted_iota(jnp.int32, short.shape, 1)
    taps = []
    for group in range(3):
        column = jnp.sum(
            jnp.where(short_lane == mesh_place + group * width, short, 0.0), axis=1, keepdims=True
        )
        taps.append([column[tap : tap + 1, :] for tap in range(3)])

    projected, lagged_one, lagged_two, mixed, pre = [], [], [], [], []
    for member in range(2):
        now = [
            row(member, 0),
            row(member, 1) + row(member, 2),
            row(member, 3) + row(member, 4),
        ]
        one = [later(x, 1) for x in now]
        two = [later(x, 2) for x in now]
        projected.append(now)
        lagged_one.append(one)
        lagged_two.append(two)
        mixed.append(
            [
                taps[g][0] * now[g] + taps[g][1] * one[g] + taps[g][2] * two[g]
                for g in range(3)
            ]
        )
        pre.append(row(member, 5))
    members = range(2)
    grad_conv_two = [pre[m] * mixed[m][2] for m in members]
    spectra = forward(
        [row(m, 6) + row(m, 7) for m in members] + [mixed[m][0] for m in members] + grad_conv_two
    )
    one_spec, two_spec = spectra[0], spectra[1]
    value_spec, conv_two_spec = spectra[2:4], spectra[4:6]
    found = backward(
        [times(one_spec, value_spec[m]) for m in members]
        + [conj_times(two_spec, conv_two_spec[m]) for m in members]
    )
    conv_one, grad_gated = found[:2], found[2:]
    spectra = forward(
        [mixed[m][1] * conv_one[m] for m in members]
        + [mixed[m][1] * grad_gated[m] for m in members]
    )
    gated_spec, conv_one_spec = spectra[:2], spectra[2:]
    found = backward(
        [times(two_spec, gated_spec[m]) for m in members]
        + [conj_times(one_spec, conv_one_spec[m]) for m in members]
        + [
            added(*[conj_times(value_spec[m], conv_one_spec[m]) for m in members]),
            added(*[conj_times(gated_spec[m], conv_two_spec[m]) for m in members]),
        ]
    )
    conv_two, grad_value = found[:2], found[2:4]
    grad_filters = [found[4] * scale, found[5] * scale]

    new = lax.broadcasted_iota(jnp.int32, (blocks, blocks), 0)
    old = lax.broadcasted_iota(jnp.int32, (blocks, blocks), 1)
    wanted = (new & 99) | (((new >> 2) & 1) << 4) | (((new >> 3) & 3) << 2)
    reorder = jnp.where(old == wanted, 1.0, 0.0).astype(jnp.bfloat16)
    sums = [[0.0] * 3 for _ in range(3)]
    for m in members:
        sent = [mixed[m][2] * conv_two[m]]
        grads = [grad_value[m], grad_gated[m] * conv_one[m], pre[m] * conv_two[m]]
        for g in range(3):
            sent.append(
                taps[g][0] * grads[g]
                + taps[g][1] * earlier(grads[g], 1)
                + taps[g][2] * earlier(grads[g], 2)
            )
            for tap, lagged in enumerate((projected, lagged_one, lagged_two)):
                sums[g][tap] = sums[g][tap] + jnp.sum(
                    jnp.sum(grads[g] * lagged[m][g], axis=0, keepdims=True), axis=1, keepdims=True
                )
        sent.extend(grad_filters)
        turned = bf16_dot(reorder, jnp.concatenate(sent, 1).astype(jnp.bfloat16))
        half = out_ref.shape[0] // 2
        for index in range(len(sent)):
            out_ref[m * half : (m + 1) * half, index] = (
                turned[:, index * rows : (index + 1) * rows]
                .reshape(half, blocks // half, rows)
                .astype(jnp.bfloat16)
            )
    shape = sums_ref.shape
    sum_lane = lax.broadcasted_iota(jnp.int32, shape, 1)
    line = jnp.zeros(shape, jnp.float32)
    for g in range(3):
        for tap in range(3):
            total = sums[g][tap] * scale
            high = total.astype(jnp.bfloat16).astype(jnp.float32)
            line = jnp.where(sum_lane == g * 3 + tap, high, line)
            line = jnp.where(sum_lane == 16 + g * 3 + tap, total - high, line)
    own_row = lax.broadcasted_iota(jnp.int32, shape, 0) == lax.axis_index(("zh", "zl"))
    sums_ref[...] = jnp.where(own_row, line, 0.0)


def channel_order(place_of):
    channel = lax.broadcasted_iota(jnp.int32, (256, 256), 0)
    row = lax.broadcasted_iota(jnp.int32, (256, 256), 1)
    zh, x, core = channel >> 7, (channel >> 5) & 3, (channel >> 4) & 1
    zl, y = (channel >> 2) & 3, channel & 3
    return jnp.where(row == place_of(zh, x, core, zl, y), 1.0, 0.0).astype(jnp.bfloat16)


def part_kernel(in_ref, *refs):
    both_refs, part_ref, send_refs, rows_ref = refs[:8], refs[8], refs[9:13], refs[13]
    sources, kinds, blocks, rows = in_ref.shape
    width = both_refs[0].shape[1] // 2
    core, y = lax.axis_index("core"), lax.axis_index("y")
    rows_ref[...] = in_ref[...].astype(jnp.float32).reshape(sources * kinds * blocks, rows)
    out_part = jnp.zeros((sources, width), jnp.float32)
    in_part = jnp.zeros((3 * sources, width), jnp.float32)
    for other in range(2):
        for ahead in range(4):
            block = (core ^ other) * 4 + ((y + ahead) & 3)
            kept = jnp.concatenate(
                [
                    rows_ref[pl.ds(kind * blocks + block, sources, stride=kinds * blocks), :]
                    for kind in range(kinds)
                ],
                0,
            ).astype(jnp.bfloat16)
            send_refs[ahead][other] = kept
            both_ref = both_refs[other * 4 + (4 - ahead) % 4]
            out_part += bf16_dot(kept[:sources], both_ref[:, width:])
            in_part += bf16_dot(kept[sources : 4 * sources], both_ref[:, :width])
    part_ref[0] = out_part
    for group in range(3):
        part_ref[1 + group] = in_part[group * sources : (group + 1) * sources]


def finish_kernel(*refs):
    held = refs[:8]
    in_weight_ref, out_weight_ref, outputs_ref, grad_inputs_ref, one_ref, two_ref = refs[8:]
    width = out_weight_ref.shape[0]
    count = width // 8
    core, y = lax.axis_index("core"), lax.axis_index("y")
    order = channel_order(
        lambda zh, x, c, zl, v: (
            (((c ^ core) * 4 + ((y - v) & 3)) * 32) + (zh * 16 + x * 4 + zl)
        )
    )
    contract_first = (((0,), (1,)), ((), ()))
    contract_last = (((1,), (1,)), ((), ()))

    def natural(kind):
        stacked = jnp.concatenate(
            [held[i][i // 4, kind * count : (kind + 1) * count, :] for i in range(8)], 0
        )
        return lax.dot_general(
            stacked, order, contract_first, preferred_element_type=jnp.float32
        )

    outputs_ref[0] = bf16_dot(natural(0).astype(jnp.bfloat16), out_weight_ref[...]).astype(
        jnp.bfloat16
    )
    total = None
    for group in range(3):
        term = lax.dot_general(
            natural(1 + group).astype(jnp.bfloat16),
            in_weight_ref[:, group * width : (group + 1) * width],
            contract_last,
            preferred_element_type=jnp.float32,
        )
        total = term if total is None else total + term
    grad_inputs_ref[0] = total.astype(jnp.bfloat16)
    one_ref[...] = natural(4)
    two_ref[...] = natural(5)


def add_x_kernel(in_ref, sums_ref, out_ref):
    total = jnp.sum(in_ref[...], axis=0)
    count, lanes = total.shape[0], out_ref.shape[2]
    rows = jnp.concatenate([total[:, :lanes], total[:, lanes:], sums_ref[...]], 0)
    out_ref[...] = jnp.broadcast_to(rows.astype(jnp.bfloat16)[None], out_ref.shape)


def add_z_kernel(scale, in_ref, out_ref):
    total = jnp.sum(in_ref[...].astype(jnp.float32), axis=0)
    row = lax.broadcasted_iota(jnp.int32, total.shape, 0)
    total = total * jnp.where(row < 64, scale, 1.0)
    out_ref[...] = jnp.broadcast_to(total.astype(jnp.bfloat16)[None], out_ref.shape)


def place_kernel(own_ref, other_ref, in_weight_ref, out_weight_ref, short_ref):
    width, lanes = out_weight_ref.shape[0], own_ref.shape[2]
    core = lax.axis_index("core")
    order = channel_order(
        lambda zh, x, c, zl, y: ((c ^ core) * 4 + y) * 32 + (zh * 16 + x * 4 + zl)
    )
    contract_first = (((0,), (1,)), ((), ()))
    for kind in range(4):
        for half in range(2):
            stacked = jnp.concatenate(
                [
                    ref[kind * 4 + y, half * 32 : (half + 1) * 32, :]
                    for ref in (own_ref, other_ref)
                    for y in range(4)
                ],
                0,
            )
            if kind == 0:
                out_weight_ref[:, half * lanes : (half + 1) * lanes] = bf16_dot(order, stacked)
            else:
                in_weight_ref[
                    half * lanes : (half + 1) * lanes, (kind - 1) * width : kind * width
                ] = lax.dot_general(
                    stacked, order, contract_first, preferred_element_type=jnp.float32
                )
    sums = jnp.concatenate(
        [
            ref[i, 64:80, :].astype(jnp.float32)[:8]
            for ref in (own_ref, other_ref)
            for i in range(16)
        ],
        0,
    ).astype(jnp.bfloat16)
    order = channel_order(
        lambda zh, x, c, zl, y: ((c ^ core) * 16 + x * 4 + y) * 8 + zh * 4 + zl
    )
    sums = lax.dot_general(sums, order, contract_first, preferred_element_type=jnp.float32)
    for group in range(3):
        short_ref[:, group * width : (group + 1) * width] = (
            sums[group * 3 : group * 3 + 3, :] + sums[16 + group * 3 : 19 + group * 3, :]
        )


def call(kernel, out_shape, scratch=()):
    return pl.pallas_call(
        kernel,
        out_shape=out_shape,
        scratch_shapes=list(scratch),
        compiler_params=pltpu.CompilerParams(vmem_limit_bytes=vmem_limit),
    )


def exchange(x, axes):
    return lax.all_to_all(x, axes, split_axis=0, concat_axis=0, tiled=True)


def swap_core(x):
    return lax.ppermute(x, "core", [(0, 1), (1, 0)])


def ring(x, distance):
    return lax.ppermute(x, "y", [(i, (i + distance) % 4) for i in range(4)])


def per_device(inputs, in_weight, short_kernel, filter_one, filter_two, out_weight, out_grad):
    width = out_weight.shape[0]
    rows = inputs.shape[1]
    devices = lax.axis_size(everyone)
    scale = 1.0 / math.sqrt(devices * rows)
    shape = jax.ShapeDtypeStruct
    f32, bf16 = jnp.float32, jnp.bfloat16
    packed, both = call(
        pack_kernel,
        (shape((width, 8, rows), bf16), shape((rows, 2 * width), bf16)),
        [pltpu.VMEM((width * 8, rows), f32)],
    )(inputs, in_weight, filter_one, filter_two, out_weight, out_grad)
    received = exchange(packed, everyone)
    gathered = [both] + [ring(both, distance) for distance in (1, 2, 3)]
    gathered += [swap_core(x) for x in gathered]
    tables = [jnp.asarray(t) for t in transform_tables(devices // 2, rows)]
    back, sums = call(
        convolve_kernel,
        (shape((32, 6, 8, rows), bf16), shape((16, rows), f32)),
        [pltpu.VMEM((devices * 8, rows), f32)],
    )(received, short_kernel, *tables)
    halfway = exchange(back, ("zh", "x", "zl"))
    part, *leaving = call(
        part_kernel,
        (shape((4, 32, width), f32),) + (shape((2, 6 * 32, rows), bf16),) * 4,
        [pltpu.VMEM((32 * 6 * 8, rows), f32)],
    )(halfway, *gathered)
    arrived = [leaving[0]] + [ring(leaving[distance], distance) for distance in (1, 2, 3)]
    arrived += [swap_core(x) for x in arrived]
    part = exchange(part, "x")
    part = call(add_x_kernel, shape((8, 80, rows), bf16))(part, sums)
    part = exchange(part, ("zh", "zl"))
    part = call(functools.partial(add_z_kernel, scale), shape((16, 80, rows), bf16))(part)
    part = exchange(part, ("x", "y"))
    grad_in_weight, grad_out_weight, grad_short = call(
        place_kernel,
        (shape((width, 3 * width), f32), shape((width, width), f32), shape((3, 3 * width), f32)),
    )(part, swap_core(part))
    outputs, grad_inputs, grad_one, grad_two = call(
        finish_kernel,
        (
            shape((1, rows, width), bf16),
            shape((1, rows, width), bf16),
            shape((rows, width), f32),
            shape((rows, width), f32),
        ),
    )(*arrived, in_weight, out_weight)
    return (
        outputs,
        grad_inputs,
        grad_in_weight,
        grad_short,
        grad_one,
        grad_two,
        grad_out_weight,
    )


def solution(mesh):
    mesh = Mesh(mesh.devices.reshape(2, 4, 2, 4, 4), everyone)
    positions = ("x", "core", "zl", "y")
    split_rows, split_filter = P("zh", positions, None), P(positions, None)
    return jax.shard_map(
        per_device,
        mesh=mesh,
        in_specs=(split_rows, P(), P(), split_filter, split_filter, P(), split_rows),
        out_specs=(split_rows, split_rows, P(), P(), split_filter, split_filter, P()),
        check_vma=False,
    )
```

```python
import functools
import math

import jax
import jax.numpy as jnp
import numpy as np
from jax import lax
from jax.experimental import pallas as pl
from jax.experimental.pallas import tpu as pltpu
from jax.sharding import Mesh
from jax.sharding import PartitionSpec as P

everyone = ("zh", "x", "core", "zl", "y")
vmem_limit = 16 * 1024 * 1024


def two_terms(table):
    high = table.astype(np.float32).astype(jnp.bfloat16)
    low = (table - high.astype(np.float64)).astype(np.float32).astype(jnp.bfloat16)
    return high, low


def transform_tables(blocks, rows):
    length = 2 * blocks * rows
    outer = np.arange(blocks) + 0.5
    step = 2.0 * math.pi * np.outer(outer, np.arange(blocks)) / (2 * blocks)
    turn = 2.0 * math.pi * np.outer(outer, np.arange(rows)) / length
    inner = 2.0 * math.pi * np.outer(np.arange(rows), np.arange(rows)) / rows
    first = np.concatenate([np.cos(step), -np.sin(step)], 0)
    c, s = np.cos(inner), np.sin(inner)
    second = np.block([[c, -s], [s, c]])
    second_back = np.block([[c, s], [-s, c]])
    first_back = np.concatenate([np.cos(step).T, -np.sin(step).T], 1) * (2.0 / length)
    tables = []
    for table in (first, second, second_back, first_back):
        tables.extend(two_terms(table))
    tables.append(np.cos(turn).astype(np.float32))
    tables.append(np.sin(turn).astype(np.float32))
    return tables


def bf16_dot(a, b):
    return jnp.dot(a, b, preferred_element_type=jnp.float32)


def split(x):
    high = x.astype(jnp.bfloat16)
    low = (x - high.astype(jnp.float32)).astype(jnp.bfloat16)
    return high, low


def table_left(high, low, x):
    x_high, x_low = split(x)
    return bf16_dot(high, x_high) + bf16_dot(low, x_high) + bf16_dot(high, x_low)


def table_right(x, high, low):
    x_high, x_low = split(x)
    return bf16_dot(x_high, high) + bf16_dot(x_high, low) + bf16_dot(x_low, high)


def pack_kernel(seq_ref, in_weight_ref, one_ref, two_ref, out_weight_ref, grad_ref, out_ref, both_ref, rows_ref):
    width = out_weight_ref.shape[0]
    slots = rows_ref.shape[0] // width
    contract_first = (((0,), (1,)), ((), ()))
    contract_last = (((1,), (1,)), ((), ()))
    seq = seq_ref[0]

    def put(index, x):
        rows_ref[pl.ds(index, width, stride=slots), :] = x

    def put_two(index, x):
        high = x.astype(jnp.bfloat16).astype(jnp.float32)
        put(index, high)
        put(index + 1, x - high)

    projected = [
        lax.dot_general(
            in_weight_ref[:, group * width : (group + 1) * width],
            seq,
            contract_first,
            preferred_element_type=jnp.float32,
        )
        for group in range(3)
    ]
    put(0, projected[0])
    put_two(1, projected[1])
    put_two(3, projected[2])
    put(
        5,
        lax.dot_general(
            out_weight_ref[...], grad_ref[0], contract_last, preferred_element_type=jnp.float32
        ),
    )
    chosen = jnp.where(lax.axis_index("zh") == 0, one_ref[...], two_ref[...])
    put_two(6, chosen.T)
    both_ref[:, :width] = seq
    both_ref[:, width:] = grad_ref[0]
    out_ref[...] = rows_ref[...].reshape(out_ref.shape).astype(jnp.bfloat16)


def convolve_kernel(
    in_ref,
    short_ref,
    first_high,
    first_low,
    second_high,
    second_low,
    second_back_high,
    second_back_low,
    first_back_high,
    first_back_low,
    turn_cos_ref,
    turn_sin_ref,
    out_ref,
    rows_ref,
):
    sources, slots, rows = in_ref.shape
    blocks = sources // 2
    width = short_ref.shape[1] // 3
    scale = 1.0 / math.sqrt(sources * rows)
    turn_cos = turn_cos_ref[...]
    turn_sin = turn_sin_ref[...]
    lane = lax.broadcasted_iota(jnp.int32, (blocks, rows), 1)
    block = lax.broadcasted_iota(jnp.int32, (blocks, rows), 0)

    rows_ref[...] = in_ref[...].astype(jnp.float32).reshape(sources * slots, rows)

    def row(member, index):
        return rows_ref[pl.ds(member * blocks * slots + index, blocks, stride=slots), :]

    def later(x, distance):
        moved = pltpu.roll(x, distance, 1)
        carried = jnp.where(block == 0, 0.0, pltpu.roll(moved, 1, 0))
        return jnp.where(lane < distance, carried, moved)

    def earlier(x, distance):
        moved = pltpu.roll(x, rows - distance, 1)
        carried = jnp.where(block == blocks - 1, 0.0, pltpu.roll(moved, blocks - 1, 0))
        return jnp.where(lane >= rows - distance, carried, moved)

    def forward(signals):
        outer = table_left(first_high[...], first_low[...], jnp.concatenate(signals, 1))
        turned = []
        for i in range(len(signals)):
            re = outer[:blocks, i * rows : (i + 1) * rows]
            im = outer[blocks:, i * rows : (i + 1) * rows]
            turned.append(
                jnp.concatenate(
                    [re * turn_cos + im * turn_sin, im * turn_cos - re * turn_sin], 1
                )
            )
        inner = table_right(jnp.concatenate(turned, 0), second_high[...], second_low[...])
        return [
            (inner[i * blocks : (i + 1) * blocks, :rows], inner[i * blocks : (i + 1) * blocks, rows:])
            for i in range(len(signals))
        ]

    def backward(spectra):
        stacked = jnp.concatenate([jnp.concatenate(pair, 1) for pair in spectra], 0)
        inner = table_right(stacked, second_back_high[...], second_back_low[...])
        turned = []
        for i in range(len(spectra)):
            re = inner[i * blocks : (i + 1) * blocks, :rows]
            im = inner[i * blocks : (i + 1) * blocks, rows:]
            turned.append(
                jnp.concatenate(
                    [re * turn_cos - im * turn_sin, im * turn_cos + re * turn_sin], 0
                )
            )
        outer = table_left(first_back_high[...], first_back_low[...], jnp.concatenate(turned, 1))
        return [outer[:, i * rows : (i + 1) * rows] for i in range(len(spectra))]

    def times(a, b):
        return a[0] * b[0] - a[1] * b[1], a[0] * b[1] + a[1] * b[0]

    def conj_times(a, b):
        return a[0] * b[0] + a[1] * b[1], a[0] * b[1] - a[1] * b[0]

    def added(a, b):
        return a[0] + b[0], a[1] + b[1]

    mesh_place = lax.axis_index(everyone)
    short = short_ref[...]
    short_lane = lax.broadcasted_iota(jnp.int32, short.shape, 1)
    taps = []
    for group in range(3):
        column = jnp.sum(
            jnp.where(short_lane == mesh_place + group * width, short, 0.0), axis=1, keepdims=True
        )
        taps.append([column[tap : tap + 1, :] for tap in range(3)])

    projected, lagged_one, lagged_two, mixed, pre = [], [], [], [], []
    for member in range(2):
        now = [
            row(member, 0),
            row(member, 1) + row(member, 2),
            row(member, 3) + row(member, 4),
        ]
        one = [later(x, 1) for x in now]
        two = [later(x, 2) for x in now]
        projected.append(now)
        lagged_one.append(one)
        lagged_two.append(two)
        mixed.append(
            [
                taps[g][0] * now[g] + taps[g][1] * one[g] + taps[g][2] * two[g]
                for g in range(3)
            ]
        )
        pre.append(row(member, 5))
    members = range(2)
    grad_conv_two = [pre[m] * mixed[m][2] for m in members]
    spectra = forward(
        [row(m, 6) + row(m, 7) for m in members] + [mixed[m][0] for m in members] + grad_conv_two
    )
    one_spec, two_spec = spectra[0], spectra[1]
    value_spec, conv_two_spec = spectra[2:4], spectra[4:6]
    found = backward(
        [times(one_spec, value_spec[m]) for m in members]
        + [conj_times(two_spec, conv_two_spec[m]) for m in members]
    )
    conv_one, grad_gated = found[:2], found[2:]
    spectra = forward(
        [mixed[m][1] * conv_one[m] for m in members]
        + [mixed[m][1] * grad_gated[m] for m in members]
    )
    gated_spec, conv_one_spec = spectra[:2], spectra[2:]
    found = backward(
        [times(two_spec, gated_spec[m]) for m in members]
        + [conj_times(one_spec, conv_one_spec[m]) for m in members]
        + [
            added(*[conj_times(value_spec[m], conv_one_spec[m]) for m in members]),
            added(*[conj_times(gated_spec[m], conv_two_spec[m]) for m in members]),
        ]
    )
    conv_two, grad_value = found[:2], found[2:4]
    grad_filters = [found[4] * scale, found[5] * scale]

    new = lax.broadcasted_iota(jnp.int32, (blocks, blocks), 0)
    old = lax.broadcasted_iota(jnp.int32, (blocks, blocks), 1)
    wanted = (new & 99) | (((new >> 2) & 1) << 4) | (((new >> 3) & 3) << 2)
    reorder = jnp.where(old == wanted, 1.0, 0.0).astype(jnp.bfloat16)
    sums = [[0.0] * 3 for _ in range(3)]
    for m in members:
        sent = [mixed[m][2] * conv_two[m]]
        grads = [grad_value[m], grad_gated[m] * conv_one[m], pre[m] * conv_two[m]]
        for g in range(3):
            sent.append(
                taps[g][0] * grads[g]
                + taps[g][1] * earlier(grads[g], 1)
                + taps[g][2] * earlier(grads[g], 2)
            )
            for tap, lagged in enumerate((projected, lagged_one, lagged_two)):
                sums[g][tap] = sums[g][tap] + jnp.sum(
                    jnp.sum(grads[g] * lagged[m][g], axis=0, keepdims=True), axis=1, keepdims=True
                )
        sent.extend(grad_filters)
        turned = bf16_dot(reorder, jnp.concatenate(sent, 1).astype(jnp.bfloat16))
        half = out_ref.shape[0] // 2
        for index in range(len(sent)):
            out_ref[m * half : (m + 1) * half, index] = (
                turned[:, index * rows : (index + 1) * rows]
                .reshape(half, blocks // half, rows)
                .astype(jnp.bfloat16)
            )
    shape = (blocks // half, rows)
    sum_lane = lax.broadcasted_iota(jnp.int32, shape, 1)
    line = jnp.zeros(shape, jnp.float32)
    for g in range(3):
        for tap in range(3):
            total = sums[g][tap] * scale
            high = total.astype(jnp.bfloat16).astype(jnp.float32)
            line = jnp.where(sum_lane == g * 3 + tap, high, line)
            line = jnp.where(sum_lane == 16 + g * 3 + tap, total - high, line)
    out_ref[:, 6] = jnp.broadcast_to(line[None], (2 * half,) + shape).astype(jnp.bfloat16)


def channel_order(place_of):
    channel = lax.broadcasted_iota(jnp.int32, (256, 256), 0)
    row = lax.broadcasted_iota(jnp.int32, (256, 256), 1)
    zh, x, core = channel >> 7, (channel >> 5) & 3, (channel >> 4) & 1
    zl, y = (channel >> 2) & 3, channel & 3
    return jnp.where(row == place_of(zh, x, core, zl, y), 1.0, 0.0).astype(jnp.bfloat16)


def part_kernel(in_ref, *refs):
    both_refs, part_ref, send_refs, rows_ref = refs[:8], refs[8], refs[9:13], refs[13]
    sources, kinds, blocks, rows = in_ref.shape
    width = both_refs[0].shape[1] // 2
    core, y = lax.axis_index("core"), lax.axis_index("y")
    rows_ref[...] = in_ref[...].astype(jnp.float32).reshape(sources * kinds * blocks, rows)
    out_part = jnp.zeros((sources, width), jnp.float32)
    in_part = jnp.zeros((3 * sources, width), jnp.float32)
    for other in range(2):
        for ahead in range(4):
            block = (core ^ other) * 4 + ((y + ahead) & 3)
            kept = jnp.concatenate(
                [
                    rows_ref[pl.ds(kind * blocks + block, sources, stride=kinds * blocks), :]
                    for kind in range(kinds)
                ],
                0,
            ).astype(jnp.bfloat16)
            send_refs[ahead][other] = kept
            both_ref = both_refs[other * 4 + (4 - ahead) % 4]
            out_part += bf16_dot(kept[:sources], both_ref[:, width:])
            in_part += bf16_dot(kept[sources : 4 * sources], both_ref[:, :width])
    part_ref[0] = out_part
    for group in range(3):
        part_ref[1 + group] = in_part[group * sources : (group + 1) * sources]


def finish_kernel(*refs):
    held = refs[:8]
    in_weight_ref, out_weight_ref, outputs_ref, grad_inputs_ref, short_ref = refs[8:13]
    one_ref, two_ref = refs[13:]
    width = out_weight_ref.shape[0]
    count = width // 8
    core, y = lax.axis_index("core"), lax.axis_index("y")
    order = channel_order(
        lambda zh, x, c, zl, v: (
            (((c ^ core) * 4 + ((y - v) & 3)) * 32) + (zh * 16 + x * 4 + zl)
        )
    )
    contract_first = (((0,), (1,)), ((), ()))
    contract_last = (((1,), (1,)), ((), ()))

    def stacked_rows(kind):
        return jnp.concatenate(
            [held[i][i // 4, kind * count : (kind + 1) * count, :] for i in range(8)], 0
        )

    def natural(kind):
        stacked = stacked_rows(kind)
        return lax.dot_general(
            stacked, order, contract_first, preferred_element_type=jnp.float32
        )

    outputs_ref[0] = bf16_dot(natural(0).astype(jnp.bfloat16), out_weight_ref[...]).astype(
        jnp.bfloat16
    )
    total = None
    for group in range(3):
        term = lax.dot_general(
            natural(1 + group).astype(jnp.bfloat16),
            in_weight_ref[:, group * width : (group + 1) * width],
            contract_last,
            preferred_element_type=jnp.float32,
        )
        total = term if total is None else total + term
    grad_inputs_ref[0] = total.astype(jnp.bfloat16)
    one_ref[...] = natural(4)
    two_ref[...] = natural(5)
    sums = lax.dot_general(
        stacked_rows(6), order, contract_first, preferred_element_type=jnp.float32
    )
    for group in range(3):
        short_ref[:, group * width : (group + 1) * width] = (
            sums[group * 3 : group * 3 + 3, :] + sums[16 + group * 3 : 19 + group * 3, :]
        )


def add_x_kernel(in_ref, *refs):
    out_ref = refs[-1]
    total = jnp.sum(in_ref[...], axis=0)
    lanes = out_ref.shape[2]
    rows = jnp.concatenate([total[:, :lanes], total[:, lanes:]], 0)
    out_ref[...] = jnp.broadcast_to(rows.astype(jnp.bfloat16)[None], out_ref.shape)


def add_z_kernel(scale, in_ref, *refs):
    out_ref = refs[-1]
    total = jnp.sum(in_ref[...].astype(jnp.float32), axis=0) * scale
    out_ref[...] = jnp.broadcast_to(total.astype(jnp.bfloat16)[None], out_ref.shape)


def place_kernel(own_ref, other_ref, in_weight_ref, out_weight_ref):
    width, lanes = out_weight_ref.shape[0], own_ref.shape[2]
    core = lax.axis_index("core")
    order = channel_order(
        lambda zh, x, c, zl, y: ((c ^ core) * 4 + y) * 32 + (zh * 16 + x * 4 + zl)
    )
    contract_first = (((0,), (1,)), ((), ()))
    for kind in range(4):
        for half in range(2):
            stacked = jnp.concatenate(
                [
                    ref[kind * 4 + y, half * 32 : (half + 1) * 32, :]
                    for ref in (own_ref, other_ref)
                    for y in range(4)
                ],
                0,
            )
            if kind == 0:
                out_weight_ref[:, half * lanes : (half + 1) * lanes] = bf16_dot(order, stacked)
            else:
                in_weight_ref[
                    half * lanes : (half + 1) * lanes, (kind - 1) * width : kind * width
                ] = lax.dot_general(
                    stacked, order, contract_first, preferred_element_type=jnp.float32
                )


def call(kernel, out_shape, scratch=(), whole=0, waited=0):
    specs = {}
    if waited:
        specs["in_specs"] = [pl.BlockSpec(memory_space=pltpu.VMEM)] * whole + [
            pl.BlockSpec(memory_space=pl.ANY)
        ] * waited
    return pl.pallas_call(
        kernel,
        out_shape=out_shape,
        scratch_shapes=list(scratch),
        compiler_params=pltpu.CompilerParams(vmem_limit_bytes=vmem_limit),
        **specs,
    )


def exchange(x, axes):
    return lax.all_to_all(x, axes, split_axis=0, concat_axis=0, tiled=True)


def swap_core(x):
    return lax.ppermute(x, "core", [(0, 1), (1, 0)])


def ring(x, distance):
    return lax.ppermute(x, "y", [(i, (i + distance) % 4) for i in range(4)])


def per_device(inputs, in_weight, short_kernel, filter_one, filter_two, out_weight, out_grad):
    width = out_weight.shape[0]
    rows = inputs.shape[1]
    devices = lax.axis_size(everyone)
    scale = 1.0 / math.sqrt(devices * rows)
    shape = jax.ShapeDtypeStruct
    f32, bf16 = jnp.float32, jnp.bfloat16
    packed, both = call(
        pack_kernel,
        (shape((width, 8, rows), bf16), shape((rows, 2 * width), bf16)),
        [pltpu.VMEM((width * 8, rows), f32)],
    )(inputs, in_weight, filter_one, filter_two, out_weight, out_grad)
    received = exchange(packed, everyone)
    gathered = [both] + [ring(both, distance) for distance in (1, 2, 3)]
    gathered += [swap_core(x) for x in gathered]
    tables = [jnp.asarray(t) for t in transform_tables(devices // 2, rows)]
    back = call(
        convolve_kernel,
        shape((32, 7, 8, rows), bf16),
        [pltpu.VMEM((devices * 8, rows), f32)],
    )(received, short_kernel, *tables)
    halfway = exchange(back, ("zh", "x", "zl"))
    part, *leaving = call(
        part_kernel,
        (shape((4, 32, width), f32),) + (shape((2, 7 * 32, rows), bf16),) * 4,
        [pltpu.VMEM((32 * 7 * 8, rows), f32)],
    )(halfway, *gathered)
    arrived = [leaving[0]] + [ring(leaving[distance], distance) for distance in (1, 2, 3)]
    part = exchange(part, "x")
    part = call(add_x_kernel, shape((8, 64, rows), bf16), whole=1, waited=3)(part, *arrived[1:])
    arrived += [swap_core(x) for x in arrived]
    part = exchange(part, ("zh", "zl"))
    outputs, grad_inputs, grad_short, grad_one, grad_two = call(
        finish_kernel,
        (
            shape((1, rows, width), bf16),
            shape((1, rows, width), bf16),
            shape((3, 3 * width), f32),
            shape((rows, width), f32),
            shape((rows, width), f32),
        ),
    )(*arrived, in_weight, out_weight)
    part = call(
        functools.partial(add_z_kernel, scale), shape((16, 64, rows), bf16), whole=1, waited=1
    )(part, grad_short)
    part = exchange(part, ("x", "y"))
    grad_in_weight, grad_out_weight = call(
        place_kernel, (shape((width, 3 * width), f32), shape((width, width), f32))
    )(part, swap_core(part))
    return (
        outputs,
        grad_inputs,
        grad_in_weight,
        grad_short,
        grad_one,
        grad_two,
        grad_out_weight,
    )


def solution(mesh):
    mesh = Mesh(mesh.devices.reshape(2, 4, 2, 4, 4), everyone)
    positions = ("x", "core", "zl", "y")
    split_rows, split_filter = P("zh", positions, None), P(positions, None)
    return jax.shard_map(
        per_device,
        mesh=mesh,
        in_specs=(split_rows, P(), P(), split_filter, split_filter, P(), split_rows),
        out_specs=(split_rows, split_rows, P(), P(), split_filter, split_filter, P()),
        check_vma=False,
    )
```

```python
import functools
import math

import jax
import jax.numpy as jnp
import numpy as np
from jax import lax
from jax.experimental import pallas as pl
from jax.experimental.pallas import tpu as pltpu
from jax.sharding import Mesh
from jax.sharding import PartitionSpec as P

everyone = ("zh", "x", "core", "zl", "y")
vmem_limit = 16 * 1024 * 1024


def two_terms(table):
    high = table.astype(np.float32).astype(jnp.bfloat16)
    low = (table - high.astype(np.float64)).astype(np.float32).astype(jnp.bfloat16)
    return high, low


def transform_tables(blocks, rows):
    length = 2 * blocks * rows
    outer = np.arange(blocks) + 0.5
    step = 2.0 * math.pi * np.outer(outer, np.arange(blocks)) / (2 * blocks)
    turn = 2.0 * math.pi * np.outer(outer, np.arange(rows)) / length
    inner = 2.0 * math.pi * np.outer(np.arange(rows), np.arange(rows)) / rows
    first = np.concatenate([np.cos(step), -np.sin(step)], 0)
    c, s = np.cos(inner), np.sin(inner)
    second = np.block([[c, -s], [s, c]])
    second_back = np.block([[c, s], [-s, c]])
    first_back = np.concatenate([np.cos(step).T, -np.sin(step).T], 1) * (2.0 / length)
    tables = []
    for table in (first, second, second_back, first_back):
        tables.extend(two_terms(table))
    tables.append(np.cos(turn).astype(np.float32))
    tables.append(np.sin(turn).astype(np.float32))
    return tables


def bf16_dot(a, b):
    return jnp.dot(a, b, preferred_element_type=jnp.float32)


def split(x):
    high = x.astype(jnp.bfloat16)
    low = (x - high.astype(jnp.float32)).astype(jnp.bfloat16)
    return high, low


def table_left(high, low, x):
    x_high, x_low = split(x)
    return bf16_dot(high, x_high) + bf16_dot(low, x_high) + bf16_dot(high, x_low)


def table_right(x, high, low):
    x_high, x_low = split(x)
    return bf16_dot(x_high, high) + bf16_dot(x_high, low) + bf16_dot(x_low, high)


def pack_kernel(seq_ref, in_weight_ref, one_ref, two_ref, out_weight_ref, grad_ref, out_ref, both_ref, rows_ref):
    width = out_weight_ref.shape[0]
    slots = rows_ref.shape[0] // width
    contract_first = (((0,), (1,)), ((), ()))
    contract_last = (((1,), (1,)), ((), ()))
    seq = seq_ref[0]

    def put(index, x):
        rows_ref[pl.ds(index, width, stride=slots), :] = x

    def put_two(index, x):
        high = x.astype(jnp.bfloat16).astype(jnp.float32)
        put(index, high)
        put(index + 1, x - high)

    projected = [
        lax.dot_general(
            in_weight_ref[:, group * width : (group + 1) * width],
            seq,
            contract_first,
            preferred_element_type=jnp.float32,
        )
        for group in range(3)
    ]
    put(0, projected[0])
    put_two(1, projected[1])
    put_two(3, projected[2])
    put(
        5,
        lax.dot_general(
            out_weight_ref[...], grad_ref[0], contract_last, preferred_element_type=jnp.float32
        ),
    )
    chosen = jnp.where(lax.axis_index("zh") == 0, one_ref[...], two_ref[...])
    put_two(6, chosen.T)
    both_ref[:, :width] = seq
    both_ref[:, width:] = grad_ref[0]
    out_ref[...] = rows_ref[...].reshape(out_ref.shape).astype(jnp.bfloat16)


def convolve_kernel(
    in_ref,
    short_ref,
    first_high,
    first_low,
    second_high,
    second_low,
    second_back_high,
    second_back_low,
    first_back_high,
    first_back_low,
    turn_cos_ref,
    turn_sin_ref,
    out_ref,
    rows_ref,
):
    sources, slots, rows = in_ref.shape
    blocks = sources // 2
    width = short_ref.shape[1] // 3
    scale = 1.0 / math.sqrt(sources * rows)
    turn_cos = turn_cos_ref[...]
    turn_sin = turn_sin_ref[...]
    lane = lax.broadcasted_iota(jnp.int32, (blocks, rows), 1)
    block = lax.broadcasted_iota(jnp.int32, (blocks, rows), 0)

    rows_ref[...] = in_ref[...].astype(jnp.float32).reshape(sources * slots, rows)

    def row(member, index):
        return rows_ref[pl.ds(member * blocks * slots + index, blocks, stride=slots), :]

    def later(x, distance):
        moved = pltpu.roll(x, distance, 1)
        carried = jnp.where(block == 0, 0.0, pltpu.roll(moved, 1, 0))
        return jnp.where(lane < distance, carried, moved)

    def earlier(x, distance):
        moved = pltpu.roll(x, rows - distance, 1)
        carried = jnp.where(block == blocks - 1, 0.0, pltpu.roll(moved, blocks - 1, 0))
        return jnp.where(lane >= rows - distance, carried, moved)

    def forward(signals):
        outer = table_left(first_high[...], first_low[...], jnp.concatenate(signals, 1))
        turned = []
        for i in range(len(signals)):
            re = outer[:blocks, i * rows : (i + 1) * rows]
            im = outer[blocks:, i * rows : (i + 1) * rows]
            turned.append(
                jnp.concatenate(
                    [re * turn_cos + im * turn_sin, im * turn_cos - re * turn_sin], 1
                )
            )
        inner = table_right(jnp.concatenate(turned, 0), second_high[...], second_low[...])
        return [
            (inner[i * blocks : (i + 1) * blocks, :rows], inner[i * blocks : (i + 1) * blocks, rows:])
            for i in range(len(signals))
        ]

    def backward(spectra):
        stacked = jnp.concatenate([jnp.concatenate(pair, 1) for pair in spectra], 0)
        inner = table_right(stacked, second_back_high[...], second_back_low[...])
        turned = []
        for i in range(len(spectra)):
            re = inner[i * blocks : (i + 1) * blocks, :rows]
            im = inner[i * blocks : (i + 1) * blocks, rows:]
            turned.append(
                jnp.concatenate(
                    [re * turn_cos - im * turn_sin, im * turn_cos + re * turn_sin], 0
                )
            )
        outer = table_left(first_back_high[...], first_back_low[...], jnp.concatenate(turned, 1))
        return [outer[:, i * rows : (i + 1) * rows] for i in range(len(spectra))]

    def times(a, b):
        return a[0] * b[0] - a[1] * b[1], a[0] * b[1] + a[1] * b[0]

    def conj_times(a, b):
        return a[0] * b[0] + a[1] * b[1], a[0] * b[1] - a[1] * b[0]

    def added(a, b):
        return a[0] + b[0], a[1] + b[1]

    mesh_place = lax.axis_index(everyone)
    short = short_ref[...]
    short_lane = lax.broadcasted_iota(jnp.int32, short.shape, 1)
    taps = []
    for group in range(3):
        column = jnp.sum(
            jnp.where(short_lane == mesh_place + group * width, short, 0.0), axis=1, keepdims=True
        )
        taps.append([column[tap : tap + 1, :] for tap in range(3)])

    projected, lagged_one, lagged_two, mixed, pre = [], [], [], [], []
    for member in range(2):
        now = [
            row(member, 0),
            row(member, 1) + row(member, 2),
            row(member, 3) + row(member, 4),
        ]
        one = [later(x, 1) for x in now]
        two = [later(x, 2) for x in now]
        projected.append(now)
        lagged_one.append(one)
        lagged_two.append(two)
        mixed.append(
            [
                taps[g][0] * now[g] + taps[g][1] * one[g] + taps[g][2] * two[g]
                for g in range(3)
            ]
        )
        pre.append(row(member, 5))
    members = range(2)
    grad_conv_two = [pre[m] * mixed[m][2] for m in members]
    spectra = forward(
        [row(m, 6) + row(m, 7) for m in members] + [mixed[m][0] for m in members] + grad_conv_two
    )
    one_spec, two_spec = spectra[0], spectra[1]
    value_spec, conv_two_spec = spectra[2:4], spectra[4:6]
    found = backward(
        [times(one_spec, value_spec[m]) for m in members]
        + [conj_times(two_spec, conv_two_spec[m]) for m in members]
    )
    conv_one, grad_gated = found[:2], found[2:]
    spectra = forward(
        [mixed[m][1] * conv_one[m] for m in members]
        + [mixed[m][1] * grad_gated[m] for m in members]
    )
    gated_spec, conv_one_spec = spectra[:2], spectra[2:]
    found = backward(
        [times(two_spec, gated_spec[m]) for m in members]
        + [conj_times(one_spec, conv_one_spec[m]) for m in members]
        + [
            added(*[conj_times(value_spec[m], conv_one_spec[m]) for m in members]),
            added(*[conj_times(gated_spec[m], conv_two_spec[m]) for m in members]),
        ]
    )
    conv_two, grad_value = found[:2], found[2:4]
    grad_filters = [found[4] * scale, found[5] * scale]

    new = lax.broadcasted_iota(jnp.int32, (blocks, blocks), 0)
    old = lax.broadcasted_iota(jnp.int32, (blocks, blocks), 1)
    wanted = (new & 99) | (((new >> 2) & 1) << 4) | (((new >> 3) & 3) << 2)
    reorder = jnp.where(old == wanted, 1.0, 0.0).astype(jnp.bfloat16)
    sums = [[0.0] * 3 for _ in range(3)]
    for m in members:
        sent = [mixed[m][2] * conv_two[m]]
        grads = [grad_value[m], grad_gated[m] * conv_one[m], pre[m] * conv_two[m]]
        for g in range(3):
            sent.append(
                taps[g][0] * grads[g]
                + taps[g][1] * earlier(grads[g], 1)
                + taps[g][2] * earlier(grads[g], 2)
            )
            for tap, lagged in enumerate((projected, lagged_one, lagged_two)):
                sums[g][tap] = sums[g][tap] + jnp.sum(
                    jnp.sum(grads[g] * lagged[m][g], axis=0, keepdims=True), axis=1, keepdims=True
                )
        sent.extend(grad_filters)
        turned = bf16_dot(reorder, jnp.concatenate(sent, 1).astype(jnp.bfloat16))
        half = out_ref.shape[0] // 2
        for index in range(len(sent)):
            out_ref[m * half : (m + 1) * half, index] = (
                turned[:, index * rows : (index + 1) * rows]
                .reshape(half, blocks // half, rows)
                .astype(jnp.bfloat16)
            )
    shape = (blocks // half, rows)
    sum_lane = lax.broadcasted_iota(jnp.int32, shape, 1)
    line = jnp.zeros(shape, jnp.float32)
    for g in range(3):
        for tap in range(3):
            total = sums[g][tap] * scale
            high = total.astype(jnp.bfloat16).astype(jnp.float32)
            line = jnp.where(sum_lane == g * 3 + tap, high, line)
            line = jnp.where(sum_lane == 16 + g * 3 + tap, total - high, line)
    out_ref[:, 6] = jnp.broadcast_to(line[None], (2 * half,) + shape).astype(jnp.bfloat16)


def channel_order(place_of):
    channel = lax.broadcasted_iota(jnp.int32, (256, 256), 0)
    row = lax.broadcasted_iota(jnp.int32, (256, 256), 1)
    zh, x, core = channel >> 7, (channel >> 5) & 3, (channel >> 4) & 1
    zl, y = (channel >> 2) & 3, channel & 3
    return jnp.where(row == place_of(zh, x, core, zl, y), 1.0, 0.0).astype(jnp.bfloat16)


def part_kernel(in_ref, *refs):
    both_refs, part_refs, send_refs = refs[:8], refs[8:12], refs[12:16]
    rows_ref, sums_ref = refs[16:]
    sources, kinds, blocks, rows = in_ref.shape
    width = both_refs[0].shape[1] // 2
    x, core, y = lax.axis_index("x"), lax.axis_index("core"), lax.axis_index("y")
    rows_ref[...] = in_ref[...].astype(jnp.float32).reshape(sources * kinds * blocks, rows)
    out_part = jnp.zeros((sources, width), jnp.float32)
    in_part = jnp.zeros((3 * sources, width), jnp.float32)
    for other in range(2):
        for ahead in range(4):
            block = (core ^ other) * 4 + ((y + ahead) & 3)
            kept = jnp.concatenate(
                [
                    rows_ref[pl.ds(kind * blocks + block, sources, stride=kinds * blocks), :]
                    for kind in range(kinds)
                ],
                0,
            ).astype(jnp.bfloat16)
            send_refs[ahead][other] = kept
            both_ref = both_refs[other * 4 + (4 - ahead) % 4]
            out_part += bf16_dot(kept[:sources], both_ref[:, width:])
            in_part += bf16_dot(kept[sources : 4 * sources], both_ref[:, :width])
    sums_ref[0] = out_part
    for group in range(3):
        sums_ref[1 + group] = in_part[group * sources : (group + 1) * sources]
    for ahead in range(4):
        part_refs[ahead][...] = sums_ref[(x + ahead) & 3]


def finish_kernel(*refs):
    held = refs[:8]
    in_weight_ref, out_weight_ref, outputs_ref, grad_inputs_ref, short_ref = refs[8:13]
    one_ref, two_ref = refs[13:]
    width = out_weight_ref.shape[0]
    count = width // 8
    core, y = lax.axis_index("core"), lax.axis_index("y")
    order = channel_order(
        lambda zh, x, c, zl, v: (
            (((c ^ core) * 4 + ((y - v) & 3)) * 32) + (zh * 16 + x * 4 + zl)
        )
    )
    contract_first = (((0,), (1,)), ((), ()))
    contract_last = (((1,), (1,)), ((), ()))

    def stacked_rows(kind):
        return jnp.concatenate(
            [held[i][i // 4, kind * count : (kind + 1) * count, :] for i in range(8)], 0
        )

    def natural(kind):
        stacked = stacked_rows(kind)
        return lax.dot_general(
            stacked, order, contract_first, preferred_element_type=jnp.float32
        )

    outputs_ref[0] = bf16_dot(natural(0).astype(jnp.bfloat16), out_weight_ref[...]).astype(
        jnp.bfloat16
    )
    total = None
    for group in range(3):
        term = lax.dot_general(
            natural(1 + group).astype(jnp.bfloat16),
            in_weight_ref[:, group * width : (group + 1) * width],
            contract_last,
            preferred_element_type=jnp.float32,
        )
        total = term if total is None else total + term
    grad_inputs_ref[0] = total.astype(jnp.bfloat16)
    one_ref[...] = natural(4)
    two_ref[...] = natural(5)
    sums = lax.dot_general(
        stacked_rows(6), order, contract_first, preferred_element_type=jnp.float32
    )
    for group in range(3):
        short_ref[:, group * width : (group + 1) * width] = (
            sums[group * 3 : group * 3 + 3, :] + sums[16 + group * 3 : 19 + group * 3, :]
        )


def add_x_kernel(*refs):
    out_ref = refs[-1]
    total = refs[0][...] + refs[1][...] + refs[2][...] + refs[3][...]
    lanes = out_ref.shape[2]
    rows = jnp.concatenate([total[:, :lanes], total[:, lanes:]], 0)
    out_ref[...] = jnp.broadcast_to(rows.astype(jnp.bfloat16)[None], out_ref.shape)


def add_z_kernel(scale, in_ref, *refs):
    out_ref = refs[-1]
    total = jnp.sum(in_ref[...].astype(jnp.float32), axis=0) * scale
    out_ref[...] = jnp.broadcast_to(total.astype(jnp.bfloat16)[None], out_ref.shape)


def place_kernel(own_ref, other_ref, in_weight_ref, out_weight_ref):
    width, lanes = out_weight_ref.shape[0], own_ref.shape[2]
    core = lax.axis_index("core")
    order = channel_order(
        lambda zh, x, c, zl, y: ((c ^ core) * 4 + y) * 32 + (zh * 16 + x * 4 + zl)
    )
    contract_first = (((0,), (1,)), ((), ()))
    for kind in range(4):
        for half in range(2):
            stacked = jnp.concatenate(
                [
                    ref[kind * 4 + y, half * 32 : (half + 1) * 32, :]
                    for ref in (own_ref, other_ref)
                    for y in range(4)
                ],
                0,
            )
            if kind == 0:
                out_weight_ref[:, half * lanes : (half + 1) * lanes] = bf16_dot(order, stacked)
            else:
                in_weight_ref[
                    half * lanes : (half + 1) * lanes, (kind - 1) * width : kind * width
                ] = lax.dot_general(
                    stacked, order, contract_first, preferred_element_type=jnp.float32
                )


def call(kernel, out_shape, scratch=(), whole=0, waited=0, limit=vmem_limit):
    specs = {}
    if waited:
        specs["in_specs"] = [pl.BlockSpec(memory_space=pltpu.VMEM)] * whole + [
            pl.BlockSpec(memory_space=pl.ANY)
        ] * waited
    return pl.pallas_call(
        kernel,
        out_shape=out_shape,
        scratch_shapes=list(scratch),
        compiler_params=pltpu.CompilerParams(vmem_limit_bytes=limit),
        **specs,
    )


def exchange(x, axes):
    return lax.all_to_all(x, axes, split_axis=0, concat_axis=0, tiled=True)


def swap_core(x):
    return lax.ppermute(x, "core", [(0, 1), (1, 0)])


def ring(x, axis, distance):
    return lax.ppermute(x, axis, [(i, (i + distance) % 4) for i in range(4)])


def per_device(inputs, in_weight, short_kernel, filter_one, filter_two, out_weight, out_grad):
    width = out_weight.shape[0]
    rows = inputs.shape[1]
    devices = lax.axis_size(everyone)
    scale = 1.0 / math.sqrt(devices * rows)
    shape = jax.ShapeDtypeStruct
    f32, bf16 = jnp.float32, jnp.bfloat16
    packed, both = call(
        pack_kernel,
        (shape((width, 8, rows), bf16), shape((rows, 2 * width), bf16)),
        [pltpu.VMEM((width * 8, rows), f32)],
        limit=56 * 1024 * 1024,
    )(inputs, in_weight, filter_one, filter_two, out_weight, out_grad)
    received = exchange(packed, everyone)
    gathered = [both] + [ring(both, "y", distance) for distance in (1, 2, 3)]
    gathered += [swap_core(x) for x in gathered]
    tables = [jnp.asarray(t) for t in transform_tables(devices // 2, rows)]
    back = call(
        convolve_kernel,
        shape((32, 7, 8, rows), bf16),
        [pltpu.VMEM((devices * 8, rows), f32)],
    )(received, short_kernel, *tables)
    halfway = exchange(back, ("zh", "x", "zl"))
    found = call(
        part_kernel,
        (shape((32, width), f32),) * 4 + (shape((2, 7 * 32, rows), bf16),) * 4,
        [pltpu.VMEM((32 * 7 * 8, rows), f32), pltpu.VMEM((4, 32, width), f32)],
    )(halfway, *gathered)
    part = [found[0]] + [ring(found[distance], "x", distance) for distance in (1, 2, 3)]
    arrived = [found[4]] + [ring(found[4 + distance], "y", distance) for distance in (1, 2, 3)]
    arrived += [swap_core(x) for x in arrived]
    part = call(add_x_kernel, shape((8, 64, rows), bf16))(*part)
    part = exchange(part, ("zh", "zl"))
    part = call(
        functools.partial(add_z_kernel, scale), shape((16, 64, rows), bf16), whole=1, waited=4
    )(part, *arrived[4:])
    part = exchange(part, ("x", "y"))
    outputs, grad_inputs, grad_short, grad_one, grad_two = call(
        finish_kernel,
        (
            shape((1, rows, width), bf16),
            shape((1, rows, width), bf16),
            shape((3, 3 * width), f32),
            shape((rows, width), f32),
            shape((rows, width), f32),
        ),
    )(*arrived, in_weight, out_weight)
    part, grad_short = lax.optimization_barrier((part, grad_short))
    grad_in_weight, grad_out_weight = call(
        place_kernel, (shape((width, 3 * width), f32), shape((width, width), f32))
    )(part, swap_core(part))
    return (
        outputs,
        grad_inputs,
        grad_in_weight,
        grad_short,
        grad_one,
        grad_two,
        grad_out_weight,
    )


def solution(mesh):
    mesh = Mesh(mesh.devices.reshape(2, 4, 2, 4, 4), everyone)
    positions = ("x", "core", "zl", "y")
    split_rows, split_filter = P("zh", positions, None), P(positions, None)
    return jax.shard_map(
        per_device,
        mesh=mesh,
        in_specs=(split_rows, P(), P(), split_filter, split_filter, P(), split_rows),
        out_specs=(split_rows, split_rows, P(), P(), split_filter, split_filter, P()),
        check_vma=False,
    )
```

```python
import functools
import math

import jax
import jax.numpy as jnp
import numpy as np
from jax import lax
from jax.experimental import pallas as pl
from jax.experimental.pallas import tpu as pltpu
from jax.sharding import Mesh
from jax.sharding import PartitionSpec as P

everyone = ("zh", "x", "core", "zl", "y")
vmem_limit = 16 * 1024 * 1024


def two_terms(table):
    high = table.astype(np.float32).astype(jnp.bfloat16)
    low = (table - high.astype(np.float64)).astype(np.float32).astype(jnp.bfloat16)
    return high, low


def transform_tables(blocks, rows):
    length = 2 * blocks * rows
    outer = np.arange(blocks) + 0.5
    step = 2.0 * math.pi * np.outer(outer, np.arange(blocks)) / (2 * blocks)
    turn = 2.0 * math.pi * np.outer(outer, np.arange(rows)) / length
    inner = 2.0 * math.pi * np.outer(np.arange(rows), np.arange(rows)) / rows
    first = np.concatenate([np.cos(step), -np.sin(step)], 0)
    c, s = np.cos(inner), np.sin(inner)
    second = np.block([[c, -s], [s, c]])
    second_back = np.block([[c, s], [-s, c]])
    first_back = np.concatenate([np.cos(step).T, -np.sin(step).T], 1) * (2.0 / length)
    tables = []
    for table in (first, second, second_back, first_back):
        tables.extend(two_terms(table))
    tables.append(np.cos(turn).astype(np.float32))
    tables.append(np.sin(turn).astype(np.float32))
    return tables


def bf16_dot(a, b):
    return jnp.dot(a, b, preferred_element_type=jnp.float32)


def split(x):
    high = x.astype(jnp.bfloat16)
    low = (x - high.astype(jnp.float32)).astype(jnp.bfloat16)
    return high, low


def table_left(high, low, x):
    x_high, x_low = split(x)
    return bf16_dot(high, x_high) + bf16_dot(low, x_high) + bf16_dot(high, x_low)


def table_right(x, high, low):
    x_high, x_low = split(x)
    return bf16_dot(x_high, high) + bf16_dot(x_high, low) + bf16_dot(x_low, high)


def pack_kernel(seq_ref, in_weight_ref, one_ref, two_ref, out_weight_ref, grad_ref, out_ref, both_ref, rows_ref):
    width = out_weight_ref.shape[0]
    slots = rows_ref.shape[0] // width
    contract_first = (((0,), (1,)), ((), ()))
    contract_last = (((1,), (1,)), ((), ()))
    seq = seq_ref[0]

    def put(index, x):
        rows_ref[pl.ds(index, width, stride=slots), :] = x

    def put_two(index, x):
        high = x.astype(jnp.bfloat16).astype(jnp.float32)
        put(index, high)
        put(index + 1, x - high)

    projected = [
        lax.dot_general(
            in_weight_ref[:, group * width : (group + 1) * width],
            seq,
            contract_first,
            preferred_element_type=jnp.float32,
        )
        for group in range(3)
    ]
    put(0, projected[0])
    put_two(1, projected[1])
    put_two(3, projected[2])
    put(
        5,
        lax.dot_general(
            out_weight_ref[...], grad_ref[0], contract_last, preferred_element_type=jnp.float32
        ),
    )
    chosen = jnp.where(lax.axis_index("zh") == 0, one_ref[...], two_ref[...])
    put_two(6, chosen.T)
    both_ref[:, :width] = seq
    both_ref[:, width:] = grad_ref[0]
    out_ref[...] = rows_ref[...].reshape(out_ref.shape).astype(jnp.bfloat16)


def convolve_kernel(
    in_ref,
    short_ref,
    first_high,
    first_low,
    second_high,
    second_low,
    second_back_high,
    second_back_low,
    first_back_high,
    first_back_low,
    turn_cos_ref,
    turn_sin_ref,
    *rest,
):
    out_ref, rows_ref = rest[-2:]
    sources, slots, rows = in_ref.shape
    blocks = sources // 2
    width = short_ref.shape[1] // 3
    scale = 1.0 / math.sqrt(sources * rows)
    turn_cos = turn_cos_ref[...]
    turn_sin = turn_sin_ref[...]
    lane = lax.broadcasted_iota(jnp.int32, (blocks, rows), 1)
    block = lax.broadcasted_iota(jnp.int32, (blocks, rows), 0)

    rows_ref[...] = in_ref[...].astype(jnp.float32).reshape(sources * slots, rows)

    def row(member, index):
        return rows_ref[pl.ds(member * blocks * slots + index, blocks, stride=slots), :]

    def later(x, distance):
        moved = pltpu.roll(x, distance, 1)
        carried = jnp.where(block == 0, 0.0, pltpu.roll(moved, 1, 0))
        return jnp.where(lane < distance, carried, moved)

    def earlier(x, distance):
        moved = pltpu.roll(x, rows - distance, 1)
        carried = jnp.where(block == blocks - 1, 0.0, pltpu.roll(moved, blocks - 1, 0))
        return jnp.where(lane >= rows - distance, carried, moved)

    def forward(signals):
        outer = table_left(first_high[...], first_low[...], jnp.concatenate(signals, 1))
        turned = []
        for i in range(len(signals)):
            re = outer[:blocks, i * rows : (i + 1) * rows]
            im = outer[blocks:, i * rows : (i + 1) * rows]
            turned.append(
                jnp.concatenate(
                    [re * turn_cos + im * turn_sin, im * turn_cos - re * turn_sin], 1
                )
            )
        inner = table_right(jnp.concatenate(turned, 0), second_high[...], second_low[...])
        return [
            (inner[i * blocks : (i + 1) * blocks, :rows], inner[i * blocks : (i + 1) * blocks, rows:])
            for i in range(len(signals))
        ]

    def backward(spectra):
        stacked = jnp.concatenate([jnp.concatenate(pair, 1) for pair in spectra], 0)
        inner = table_right(stacked, second_back_high[...], second_back_low[...])
        turned = []
        for i in range(len(spectra)):
            re = inner[i * blocks : (i + 1) * blocks, :rows]
            im = inner[i * blocks : (i + 1) * blocks, rows:]
            turned.append(
                jnp.concatenate(
                    [re * turn_cos - im * turn_sin, im * turn_cos + re * turn_sin], 0
                )
            )
        outer = table_left(first_back_high[...], first_back_low[...], jnp.concatenate(turned, 1))
        return [outer[:, i * rows : (i + 1) * rows] for i in range(len(spectra))]

    def times(a, b):
        return a[0] * b[0] - a[1] * b[1], a[0] * b[1] + a[1] * b[0]

    def conj_times(a, b):
        return a[0] * b[0] + a[1] * b[1], a[0] * b[1] - a[1] * b[0]

    def added(a, b):
        return a[0] + b[0], a[1] + b[1]

    mesh_place = lax.axis_index(everyone)
    short = short_ref[...]
    short_lane = lax.broadcasted_iota(jnp.int32, short.shape, 1)
    taps = []
    for group in range(3):
        column = jnp.sum(
            jnp.where(short_lane == mesh_place + group * width, short, 0.0), axis=1, keepdims=True
        )
        taps.append([column[tap : tap + 1, :] for tap in range(3)])

    projected, lagged_one, lagged_two, mixed, pre = [], [], [], [], []
    for member in range(2):
        now = [
            row(member, 0),
            row(member, 1) + row(member, 2),
            row(member, 3) + row(member, 4),
        ]
        one = [later(x, 1) for x in now]
        two = [later(x, 2) for x in now]
        projected.append(now)
        lagged_one.append(one)
        lagged_two.append(two)
        mixed.append(
            [
                taps[g][0] * now[g] + taps[g][1] * one[g] + taps[g][2] * two[g]
                for g in range(3)
            ]
        )
        pre.append(row(member, 5))
    members = range(2)
    grad_conv_two = [pre[m] * mixed[m][2] for m in members]
    spectra = forward(
        [row(m, 6) + row(m, 7) for m in members] + [mixed[m][0] for m in members] + grad_conv_two
    )
    one_spec, two_spec = spectra[0], spectra[1]
    value_spec, conv_two_spec = spectra[2:4], spectra[4:6]
    found = backward(
        [times(one_spec, value_spec[m]) for m in members]
        + [conj_times(two_spec, conv_two_spec[m]) for m in members]
    )
    conv_one, grad_gated = found[:2], found[2:]
    spectra = forward(
        [mixed[m][1] * conv_one[m] for m in members]
        + [mixed[m][1] * grad_gated[m] for m in members]
    )
    gated_spec, conv_one_spec = spectra[:2], spectra[2:]
    found = backward(
        [times(two_spec, gated_spec[m]) for m in members]
        + [conj_times(one_spec, conv_one_spec[m]) for m in members]
        + [
            added(*[conj_times(value_spec[m], conv_one_spec[m]) for m in members]),
            added(*[conj_times(gated_spec[m], conv_two_spec[m]) for m in members]),
        ]
    )
    conv_two, grad_value = found[:2], found[2:4]
    grad_filters = [found[4] * scale, found[5] * scale]

    new = lax.broadcasted_iota(jnp.int32, (blocks, blocks), 0)
    old = lax.broadcasted_iota(jnp.int32, (blocks, blocks), 1)
    wanted = (new & 99) | (((new >> 2) & 1) << 4) | (((new >> 3) & 3) << 2)
    reorder = jnp.where(old == wanted, 1.0, 0.0).astype(jnp.bfloat16)
    sums = [[0.0] * 3 for _ in range(3)]
    for m in members:
        sent = [mixed[m][2] * conv_two[m]]
        grads = [grad_value[m], grad_gated[m] * conv_one[m], pre[m] * conv_two[m]]
        for g in range(3):
            sent.append(
                taps[g][0] * grads[g]
                + taps[g][1] * earlier(grads[g], 1)
                + taps[g][2] * earlier(grads[g], 2)
            )
            for tap, lagged in enumerate((projected, lagged_one, lagged_two)):
                sums[g][tap] = sums[g][tap] + jnp.sum(
                    jnp.sum(grads[g] * lagged[m][g], axis=0, keepdims=True), axis=1, keepdims=True
                )
        sent.extend(grad_filters)
        turned = bf16_dot(reorder, jnp.concatenate(sent, 1).astype(jnp.bfloat16))
        half = out_ref.shape[0] // 2
        for index in range(len(sent)):
            out_ref[m * half : (m + 1) * half, index] = (
                turned[:, index * rows : (index + 1) * rows]
                .reshape(half, blocks // half, rows)
                .astype(jnp.bfloat16)
            )
    shape = (blocks // half, rows)
    sum_lane = lax.broadcasted_iota(jnp.int32, shape, 1)
    line = jnp.zeros(shape, jnp.float32)
    for g in range(3):
        for tap in range(3):
            total = sums[g][tap] * scale
            high = total.astype(jnp.bfloat16).astype(jnp.float32)
            line = jnp.where(sum_lane == g * 3 + tap, high, line)
            line = jnp.where(sum_lane == 16 + g * 3 + tap, total - high, line)
    out_ref[:, 6] = jnp.broadcast_to(line[None], (2 * half,) + shape).astype(jnp.bfloat16)


def channel_order(place_of):
    channel = lax.broadcasted_iota(jnp.int32, (256, 256), 0)
    row = lax.broadcasted_iota(jnp.int32, (256, 256), 1)
    zh, x, core = channel >> 7, (channel >> 5) & 3, (channel >> 4) & 1
    zl, y = (channel >> 2) & 3, channel & 3
    return jnp.where(row == place_of(zh, x, core, zl, y), 1.0, 0.0).astype(jnp.bfloat16)


def part_kernel(in_ref, *refs):
    both_refs, part_refs, send_refs = refs[:8], refs[8:12], refs[12:16]
    rows_ref, sums_ref = refs[16:]
    sources, kinds, blocks, rows = in_ref.shape
    width = both_refs[0].shape[1] // 2
    x, core, y = lax.axis_index("x"), lax.axis_index("core"), lax.axis_index("y")
    rows_ref[...] = in_ref[...].astype(jnp.float32).reshape(sources * kinds * blocks, rows)
    out_part = jnp.zeros((sources, width), jnp.float32)
    in_part = jnp.zeros((3 * sources, width), jnp.float32)
    for other in range(2):
        for ahead in range(4):
            block = (core ^ other) * 4 + ((y + ahead) & 3)
            kept = jnp.concatenate(
                [
                    rows_ref[pl.ds(kind * blocks + block, sources, stride=kinds * blocks), :]
                    for kind in range(kinds)
                ],
                0,
            ).astype(jnp.bfloat16)
            send_refs[ahead][other] = kept
            both_ref = both_refs[other * 4 + (4 - ahead) % 4]
            out_part += bf16_dot(kept[:sources], both_ref[:, width:])
            in_part += bf16_dot(kept[sources : 4 * sources], both_ref[:, :width])
    sums_ref[0] = out_part
    for group in range(3):
        sums_ref[1 + group] = in_part[group * sources : (group + 1) * sources]
    for ahead in range(4):
        part_refs[ahead][...] = sums_ref[(x + ahead) & 3]


def finish_kernel(*refs):
    held = refs[:8]
    in_weight_ref, out_weight_ref, outputs_ref, grad_inputs_ref, short_ref = refs[8:13]
    one_ref, two_ref = refs[13:]
    width = out_weight_ref.shape[0]
    count = width // 8
    core, y = lax.axis_index("core"), lax.axis_index("y")
    order = channel_order(
        lambda zh, x, c, zl, v: (
            (((c ^ core) * 4 + ((y - v) & 3)) * 32) + (zh * 16 + x * 4 + zl)
        )
    )
    contract_first = (((0,), (1,)), ((), ()))
    contract_last = (((1,), (1,)), ((), ()))

    def stacked_rows(kind):
        return jnp.concatenate(
            [held[i][i // 4, kind * count : (kind + 1) * count, :] for i in range(8)], 0
        )

    def natural(kind):
        stacked = stacked_rows(kind)
        return lax.dot_general(
            stacked, order, contract_first, preferred_element_type=jnp.float32
        )

    outputs_ref[0] = bf16_dot(natural(0).astype(jnp.bfloat16), out_weight_ref[...]).astype(
        jnp.bfloat16
    )
    total = None
    for group in range(3):
        term = lax.dot_general(
            natural(1 + group).astype(jnp.bfloat16),
            in_weight_ref[:, group * width : (group + 1) * width],
            contract_last,
            preferred_element_type=jnp.float32,
        )
        total = term if total is None else total + term
    grad_inputs_ref[0] = total.astype(jnp.bfloat16)
    one_ref[...] = natural(4)
    two_ref[...] = natural(5)
    sums = lax.dot_general(
        stacked_rows(6), order, contract_first, preferred_element_type=jnp.float32
    )
    for group in range(3):
        short_ref[:, group * width : (group + 1) * width] = (
            sums[group * 3 : group * 3 + 3, :] + sums[16 + group * 3 : 19 + group * 3, :]
        )


def add_x_kernel(*refs):
    out_ref = refs[7]
    total = refs[0][...] + refs[1][...] + refs[2][...] + refs[3][...]
    lanes = out_ref.shape[2]
    rows = jnp.concatenate([total[:, :lanes], total[:, lanes:]], 0)
    out_ref[...] = jnp.broadcast_to(rows.astype(jnp.bfloat16)[None], out_ref.shape)


def add_z_kernel(scale, in_ref, *refs):
    out_ref = refs[-1]
    total = jnp.sum(in_ref[...].astype(jnp.float32), axis=0) * scale
    out_ref[...] = jnp.broadcast_to(total.astype(jnp.bfloat16)[None], out_ref.shape)


def place_kernel(own_ref, other_ref, in_weight_ref, out_weight_ref):
    width, lanes = out_weight_ref.shape[0], own_ref.shape[2]
    core = lax.axis_index("core")
    order = channel_order(
        lambda zh, x, c, zl, y: ((c ^ core) * 4 + y) * 32 + (zh * 16 + x * 4 + zl)
    )
    contract_first = (((0,), (1,)), ((), ()))
    for kind in range(4):
        for half in range(2):
            stacked = jnp.concatenate(
                [
                    ref[kind * 4 + y, half * 32 : (half + 1) * 32, :]
                    for ref in (own_ref, other_ref)
                    for y in range(4)
                ],
                0,
            )
            if kind == 0:
                out_weight_ref[:, half * lanes : (half + 1) * lanes] = bf16_dot(order, stacked)
            else:
                in_weight_ref[
                    half * lanes : (half + 1) * lanes, (kind - 1) * width : kind * width
                ] = lax.dot_general(
                    stacked, order, contract_first, preferred_element_type=jnp.float32
                )


def call(kernel, out_shape, scratch=(), limit=vmem_limit, **options):
    return pl.pallas_call(
        kernel,
        out_shape=out_shape,
        scratch_shapes=list(scratch),
        compiler_params=pltpu.CompilerParams(vmem_limit_bytes=limit),
        **options,
    )


def specs(*spaces):
    return [pl.BlockSpec(memory_space=space) for space in spaces]


def exchange(x, axes):
    return lax.all_to_all(x, axes, split_axis=0, concat_axis=0, tiled=True)


def swap_core(x):
    return lax.ppermute(x, "core", [(0, 1), (1, 0)])


def ring(x, axis, distance):
    return lax.ppermute(x, axis, [(i, (i + distance) % 4) for i in range(4)])


def per_device(inputs, in_weight, short_kernel, filter_one, filter_two, out_weight, out_grad):
    width = out_weight.shape[0]
    rows = inputs.shape[1]
    devices = lax.axis_size(everyone)
    scale = 1.0 / math.sqrt(devices * rows)
    shape = jax.ShapeDtypeStruct
    f32, bf16 = jnp.float32, jnp.bfloat16
    packed, both = call(
        pack_kernel,
        (shape((width, 8, rows), bf16), shape((rows, 2 * width), bf16)),
        [pltpu.VMEM((width * 8, rows), f32)],
        limit=56 * 1024 * 1024,
    )(inputs, in_weight, filter_one, filter_two, out_weight, out_grad)
    received = exchange(packed, everyone)
    gathered = [both] + [ring(both, "y", distance) for distance in (1, 2, 3)]
    gathered += [swap_core(x) for x in gathered]
    tables = [jnp.asarray(t) for t in transform_tables(devices // 2, rows)]
    back = call(
        convolve_kernel,
        shape((32, 7, 8, rows), bf16),
        [pltpu.VMEM((devices * 8, rows), f32)],
        in_specs=specs(*[pltpu.VMEM] * (2 + len(tables)), *[pl.ANY] * 3),
    )(received, short_kernel, *tables, *gathered[1:4])
    halfway = exchange(back, ("zh", "x", "zl"))
    found = call(
        part_kernel,
        (shape((32, width), f32),) * 4 + (shape((2, 7 * 32, rows), bf16),) * 4,
        [pltpu.VMEM((32 * 7 * 8, rows), f32), pltpu.VMEM((4, 32, width), f32)],
    )(halfway, *gathered)
    part = [found[0]] + [ring(found[distance], "x", distance) for distance in (1, 2, 3)]
    leaving = found[5:]
    part, *leaving = call(
        add_x_kernel,
        (shape((8, 64, rows), bf16),) + (shape(leaving[0].shape, bf16),) * 3,
        in_specs=specs(*[pltpu.VMEM] * 4, *[pl.ANY] * 3),
        out_specs=specs(pltpu.VMEM, *[pl.ANY] * 3),
        input_output_aliases={4: 1, 5: 2, 6: 3},
    )(*part, *leaving)
    arrived = [found[4]] + [ring(x, "y", 1 + i) for i, x in enumerate(leaving)]
    part = exchange(part, ("zh", "zl"))
    part = call(
        functools.partial(add_z_kernel, scale),
        shape((16, 64, rows), bf16),
        in_specs=specs(pltpu.VMEM, *[pl.ANY] * 3),
    )(part, *arrived[1:])
    arrived += [swap_core(x) for x in arrived]
    part = exchange(part, ("x", "y"))
    outputs, grad_inputs, grad_short, grad_one, grad_two = call(
        finish_kernel,
        (
            shape((1, rows, width), bf16),
            shape((1, rows, width), bf16),
            shape((3, 3 * width), f32),
            shape((rows, width), f32),
            shape((rows, width), f32),
        ),
    )(*arrived, in_weight, out_weight)
    part, grad_short = lax.optimization_barrier((part, grad_short))
    grad_in_weight, grad_out_weight = call(
        place_kernel, (shape((width, 3 * width), f32), shape((width, width), f32))
    )(part, swap_core(part))
    return (
        outputs,
        grad_inputs,
        grad_in_weight,
        grad_short,
        grad_one,
        grad_two,
        grad_out_weight,
    )


def solution(mesh):
    mesh = Mesh(mesh.devices.reshape(2, 4, 2, 4, 4), everyone)
    positions = ("x", "core", "zl", "y")
    split_rows, split_filter = P("zh", positions, None), P(positions, None)
    return jax.shard_map(
        per_device,
        mesh=mesh,
        in_specs=(split_rows, P(), P(), split_filter, split_filter, P(), split_rows),
        out_specs=(split_rows, split_rows, P(), P(), split_filter, split_filter, P()),
        check_vma=False,
    )
```

```python
import functools
import math

import jax
import jax.numpy as jnp
import numpy as np
from jax import lax
from jax.experimental import pallas as pl
from jax.experimental.pallas import tpu as pltpu
from jax.sharding import Mesh
from jax.sharding import PartitionSpec as P

everyone = ("zh", "x", "core", "zl", "y")
vmem_limit = 16 * 1024 * 1024


def two_terms(table):
    high = table.astype(np.float32).astype(jnp.bfloat16)
    low = (table - high.astype(np.float64)).astype(np.float32).astype(jnp.bfloat16)
    return high, low


def left_table(table):
    high, low = two_terms(table)
    return np.concatenate([high, low, high], 1)


def right_table(table):
    high, low = two_terms(table)
    return np.concatenate([high, low, high], 0)


def transform_tables(blocks, rows):
    length = 2 * blocks * rows
    outer = np.arange(blocks) + 0.5
    step = 2.0 * math.pi * np.outer(outer, np.arange(blocks)) / (2 * blocks)
    turn = 2.0 * math.pi * np.outer(outer, np.arange(rows)) / length
    inner = 2.0 * math.pi * np.outer(np.arange(rows), np.arange(rows)) / rows
    first = np.concatenate([np.cos(step), -np.sin(step)], 0)
    c, s = np.cos(inner), np.sin(inner)
    second = np.block([[c, -s], [s, c]])
    second_back = np.block([[c, s], [-s, c]])
    first_back = np.concatenate([np.cos(step).T, -np.sin(step).T], 1) * (2.0 / length)
    return [
        left_table(first),
        right_table(second),
        right_table(second_back),
        left_table(first_back),
        np.cos(turn).astype(np.float32),
        np.sin(turn).astype(np.float32),
    ]


def bf16_dot(a, b):
    return jnp.dot(a, b, preferred_element_type=jnp.float32)


def split(x):
    high = x.astype(jnp.bfloat16)
    low = (x - high.astype(jnp.float32)).astype(jnp.bfloat16)
    return high, low


def table_left(table, x):
    x_high, x_low = split(x)
    return bf16_dot(table, jnp.concatenate([x_high, x_high, x_low], 0))


def table_right(x, table):
    x_high, x_low = split(x)
    return bf16_dot(jnp.concatenate([x_high, x_high, x_low], 1), table)


def pack_kernel(seq_ref, in_weight_ref, one_ref, two_ref, out_weight_ref, grad_ref, out_ref, both_ref, rows_ref):
    width = out_weight_ref.shape[0]
    slots = rows_ref.shape[0] // width
    contract_first = (((0,), (1,)), ((), ()))
    contract_last = (((1,), (1,)), ((), ()))
    seq = seq_ref[0]

    def put(index, x):
        rows_ref[pl.ds(index, width, stride=slots), :] = x

    def put_two(index, x):
        high = x.astype(jnp.bfloat16).astype(jnp.float32)
        put(index, high)
        put(index + 1, x - high)

    projected = [
        lax.dot_general(
            in_weight_ref[:, group * width : (group + 1) * width],
            seq,
            contract_first,
            preferred_element_type=jnp.float32,
        )
        for group in range(3)
    ]
    put(0, projected[0])
    put_two(1, projected[1])
    put_two(3, projected[2])
    put(
        5,
        lax.dot_general(
            out_weight_ref[...], grad_ref[0], contract_last, preferred_element_type=jnp.float32
        ),
    )
    chosen = jnp.where(lax.axis_index("zh") == 0, one_ref[...], two_ref[...])
    put_two(6, chosen.T)
    both_ref[:, :width] = seq
    both_ref[:, width:] = grad_ref[0]
    out_ref[...] = rows_ref[...].reshape(out_ref.shape).astype(jnp.bfloat16)


def convolve_kernel(
    in_ref,
    short_ref,
    first_ref,
    second_ref,
    second_back_ref,
    first_back_ref,
    turn_cos_ref,
    turn_sin_ref,
    *rest,
):
    out_ref, rows_ref = rest[-2:]
    sources, slots, rows = in_ref.shape
    blocks = sources // 2
    width = short_ref.shape[1] // 3
    scale = 1.0 / math.sqrt(sources * rows)
    turn_cos = turn_cos_ref[...]
    turn_sin = turn_sin_ref[...]
    lane = lax.broadcasted_iota(jnp.int32, (blocks, rows), 1)
    block = lax.broadcasted_iota(jnp.int32, (blocks, rows), 0)

    rows_ref[...] = in_ref[...].astype(jnp.float32).reshape(sources * slots, rows)

    def row(member, index):
        return rows_ref[pl.ds(member * blocks * slots + index, blocks, stride=slots), :]

    def later(x, distance):
        moved = pltpu.roll(x, distance, 1)
        carried = jnp.where(block == 0, 0.0, pltpu.roll(moved, 1, 0))
        return jnp.where(lane < distance, carried, moved)

    def earlier(x, distance):
        moved = pltpu.roll(x, rows - distance, 1)
        carried = jnp.where(block == blocks - 1, 0.0, pltpu.roll(moved, blocks - 1, 0))
        return jnp.where(lane >= rows - distance, carried, moved)

    def forward(signals):
        outer = table_left(first_ref[...], jnp.concatenate(signals, 1))
        turned = []
        for i in range(len(signals)):
            re = outer[:blocks, i * rows : (i + 1) * rows]
            im = outer[blocks:, i * rows : (i + 1) * rows]
            turned.append(
                jnp.concatenate(
                    [re * turn_cos + im * turn_sin, im * turn_cos - re * turn_sin], 1
                )
            )
        inner = table_right(jnp.concatenate(turned, 0), second_ref[...])
        return [
            (inner[i * blocks : (i + 1) * blocks, :rows], inner[i * blocks : (i + 1) * blocks, rows:])
            for i in range(len(signals))
        ]

    def backward(spectra):
        stacked = jnp.concatenate([jnp.concatenate(pair, 1) for pair in spectra], 0)
        inner = table_right(stacked, second_back_ref[...])
        turned = []
        for i in range(len(spectra)):
            re = inner[i * blocks : (i + 1) * blocks, :rows]
            im = inner[i * blocks : (i + 1) * blocks, rows:]
            turned.append(
                jnp.concatenate(
                    [re * turn_cos - im * turn_sin, im * turn_cos + re * turn_sin], 0
                )
            )
        outer = table_left(first_back_ref[...], jnp.concatenate(turned, 1))
        return [outer[:, i * rows : (i + 1) * rows] for i in range(len(spectra))]

    def times(a, b):
        return a[0] * b[0] - a[1] * b[1], a[0] * b[1] + a[1] * b[0]

    def conj_times(a, b):
        return a[0] * b[0] + a[1] * b[1], a[0] * b[1] - a[1] * b[0]

    def added(a, b):
        return a[0] + b[0], a[1] + b[1]

    mesh_place = lax.axis_index(everyone)
    short = short_ref[...]
    short_lane = lax.broadcasted_iota(jnp.int32, short.shape, 1)
    taps = []
    for group in range(3):
        column = jnp.sum(
            jnp.where(short_lane == mesh_place + group * width, short, 0.0), axis=1, keepdims=True
        )
        taps.append([column[tap : tap + 1, :] for tap in range(3)])

    projected, lagged_one, lagged_two, mixed, pre = [], [], [], [], []
    for member in range(2):
        now = [
            row(member, 0),
            row(member, 1) + row(member, 2),
            row(member, 3) + row(member, 4),
        ]
        one = [later(x, 1) for x in now]
        two = [later(x, 2) for x in now]
        projected.append(now)
        lagged_one.append(one)
        lagged_two.append(two)
        mixed.append(
            [
                taps[g][0] * now[g] + taps[g][1] * one[g] + taps[g][2] * two[g]
                for g in range(3)
            ]
        )
        pre.append(row(member, 5))
    members = range(2)
    grad_conv_two = [pre[m] * mixed[m][2] for m in members]
    spectra = forward(
        [row(m, 6) + row(m, 7) for m in members] + [mixed[m][0] for m in members] + grad_conv_two
    )
    one_spec, two_spec = spectra[0], spectra[1]
    value_spec, conv_two_spec = spectra[2:4], spectra[4:6]
    found = backward(
        [times(one_spec, value_spec[m]) for m in members]
        + [conj_times(two_spec, conv_two_spec[m]) for m in members]
    )
    conv_one, grad_gated = found[:2], found[2:]
    spectra = forward(
        [mixed[m][1] * conv_one[m] for m in members]
        + [mixed[m][1] * grad_gated[m] for m in members]
    )
    gated_spec, conv_one_spec = spectra[:2], spectra[2:]
    found = backward(
        [times(two_spec, gated_spec[m]) for m in members]
        + [conj_times(one_spec, conv_one_spec[m]) for m in members]
        + [
            added(*[conj_times(value_spec[m], conv_one_spec[m]) for m in members]),
            added(*[conj_times(gated_spec[m], conv_two_spec[m]) for m in members]),
        ]
    )
    conv_two, grad_value = found[:2], found[2:4]
    grad_filters = [found[4] * scale, found[5] * scale]

    new = lax.broadcasted_iota(jnp.int32, (blocks, blocks), 0)
    old = lax.broadcasted_iota(jnp.int32, (blocks, blocks), 1)
    wanted = (new & 99) | (((new >> 2) & 1) << 4) | (((new >> 3) & 3) << 2)
    reorder = jnp.where(old == wanted, 1.0, 0.0).astype(jnp.bfloat16)
    sums = [[0.0] * 3 for _ in range(3)]
    for m in members:
        sent = [mixed[m][2] * conv_two[m]]
        grads = [grad_value[m], grad_gated[m] * conv_one[m], pre[m] * conv_two[m]]
        for g in range(3):
            sent.append(
                taps[g][0] * grads[g]
                + taps[g][1] * earlier(grads[g], 1)
                + taps[g][2] * earlier(grads[g], 2)
            )
            for tap, lagged in enumerate((projected, lagged_one, lagged_two)):
                sums[g][tap] = sums[g][tap] + jnp.sum(
                    jnp.sum(grads[g] * lagged[m][g], axis=0, keepdims=True), axis=1, keepdims=True
                )
        sent.extend(grad_filters)
        turned = bf16_dot(reorder, jnp.concatenate(sent, 1).astype(jnp.bfloat16))
        half = out_ref.shape[0] // 2
        for index in range(len(sent)):
            out_ref[m * half : (m + 1) * half, index] = (
                turned[:, index * rows : (index + 1) * rows]
                .reshape(half, blocks // half, rows)
                .astype(jnp.bfloat16)
            )
    shape = (blocks // half, rows)
    sum_lane = lax.broadcasted_iota(jnp.int32, shape, 1)
    line = jnp.zeros(shape, jnp.float32)
    for g in range(3):
        for tap in range(3):
            total = sums[g][tap] * scale
            high = total.astype(jnp.bfloat16).astype(jnp.float32)
            line = jnp.where(sum_lane == g * 3 + tap, high, line)
            line = jnp.where(sum_lane == 16 + g * 3 + tap, total - high, line)
    out_ref[:, 6] = jnp.broadcast_to(line[None], (2 * half,) + shape).astype(jnp.bfloat16)


def channel_order(place_of):
    channel = lax.broadcasted_iota(jnp.int32, (256, 256), 0)
    row = lax.broadcasted_iota(jnp.int32, (256, 256), 1)
    zh, x, core = channel >> 7, (channel >> 5) & 3, (channel >> 4) & 1
    zl, y = (channel >> 2) & 3, channel & 3
    return jnp.where(row == place_of(zh, x, core, zl, y), 1.0, 0.0).astype(jnp.bfloat16)


def part_kernel(in_ref, *refs):
    both_refs, part_refs, send_refs = refs[:8], refs[8:12], refs[12:16]
    rows_ref, sums_ref = refs[16:]
    sources, kinds, blocks, rows = in_ref.shape
    width = both_refs[0].shape[1] // 2
    x, core, y = lax.axis_index("x"), lax.axis_index("core"), lax.axis_index("y")
    rows_ref[...] = in_ref[...].astype(jnp.float32).reshape(sources * kinds * blocks, rows)
    out_part = jnp.zeros((sources, width), jnp.float32)
    in_part = jnp.zeros((3 * sources, width), jnp.float32)
    for other in range(2):
        for ahead in range(4):
            block = (core ^ other) * 4 + ((y + ahead) & 3)
            kept = jnp.concatenate(
                [
                    rows_ref[pl.ds(kind * blocks + block, sources, stride=kinds * blocks), :]
                    for kind in range(kinds)
                ],
                0,
            ).astype(jnp.bfloat16)
            send_refs[ahead][other] = kept
            both_ref = both_refs[other * 4 + (4 - ahead) % 4]
            out_part += bf16_dot(kept[:sources], both_ref[:, width:])
            in_part += bf16_dot(kept[sources : 4 * sources], both_ref[:, :width])
    sums_ref[0] = out_part
    for group in range(3):
        sums_ref[1 + group] = in_part[group * sources : (group + 1) * sources]
    for ahead in range(4):
        part_refs[ahead][...] = sums_ref[(x + ahead) & 3]


def finish_kernel(*refs):
    held = refs[:8]
    in_weight_ref, out_weight_ref, outputs_ref, grad_inputs_ref, short_ref = refs[8:13]
    one_ref, two_ref = refs[13:]
    width = out_weight_ref.shape[0]
    count = width // 8
    core, y = lax.axis_index("core"), lax.axis_index("y")
    order = channel_order(
        lambda zh, x, c, zl, v: (
            (((c ^ core) * 4 + ((y - v) & 3)) * 32) + (zh * 16 + x * 4 + zl)
        )
    )
    contract_first = (((0,), (1,)), ((), ()))
    contract_last = (((1,), (1,)), ((), ()))

    def stacked_rows(kind):
        return jnp.concatenate(
            [held[i][i // 4, kind * count : (kind + 1) * count, :] for i in range(8)], 0
        )

    def natural(kind):
        stacked = stacked_rows(kind)
        return lax.dot_general(
            stacked, order, contract_first, preferred_element_type=jnp.float32
        )

    outputs_ref[0] = bf16_dot(natural(0).astype(jnp.bfloat16), out_weight_ref[...]).astype(
        jnp.bfloat16
    )
    total = None
    for group in range(3):
        term = lax.dot_general(
            natural(1 + group).astype(jnp.bfloat16),
            in_weight_ref[:, group * width : (group + 1) * width],
            contract_last,
            preferred_element_type=jnp.float32,
        )
        total = term if total is None else total + term
    grad_inputs_ref[0] = total.astype(jnp.bfloat16)
    one_ref[...] = natural(4)
    two_ref[...] = natural(5)
    sums = lax.dot_general(
        stacked_rows(6), order, contract_first, preferred_element_type=jnp.float32
    )
    for group in range(3):
        short_ref[:, group * width : (group + 1) * width] = (
            sums[group * 3 : group * 3 + 3, :] + sums[16 + group * 3 : 19 + group * 3, :]
        )


def add_x_kernel(*refs):
    out_ref = refs[7]
    total = refs[0][...] + refs[1][...] + refs[2][...] + refs[3][...]
    lanes = out_ref.shape[2]
    rows = jnp.concatenate([total[:, :lanes], total[:, lanes:]], 0)
    out_ref[...] = jnp.broadcast_to(rows.astype(jnp.bfloat16)[None], out_ref.shape)


def add_z_kernel(scale, in_ref, *refs):
    out_ref = refs[3]
    total = jnp.sum(in_ref[...].astype(jnp.float32), axis=0) * scale
    out_ref[...] = jnp.broadcast_to(total.astype(jnp.bfloat16)[None], out_ref.shape)


def place_kernel(own_ref, other_ref, in_weight_ref, out_weight_ref):
    width, lanes = out_weight_ref.shape[0], own_ref.shape[2]
    core = lax.axis_index("core")
    order = channel_order(
        lambda zh, x, c, zl, y: ((c ^ core) * 4 + y) * 32 + (zh * 16 + x * 4 + zl)
    )
    contract_first = (((0,), (1,)), ((), ()))
    for kind in range(4):
        for half in range(2):
            stacked = jnp.concatenate(
                [
                    ref[kind * 4 + y, half * 32 : (half + 1) * 32, :]
                    for ref in (own_ref, other_ref)
                    for y in range(4)
                ],
                0,
            )
            if kind == 0:
                out_weight_ref[:, half * lanes : (half + 1) * lanes] = bf16_dot(order, stacked)
            else:
                in_weight_ref[
                    half * lanes : (half + 1) * lanes, (kind - 1) * width : kind * width
                ] = lax.dot_general(
                    stacked, order, contract_first, preferred_element_type=jnp.float32
                )


def call(kernel, out_shape, scratch=(), limit=vmem_limit, **options):
    return pl.pallas_call(
        kernel,
        out_shape=out_shape,
        scratch_shapes=list(scratch),
        compiler_params=pltpu.CompilerParams(vmem_limit_bytes=limit),
        **options,
    )


def specs(*spaces):
    return [pl.BlockSpec(memory_space=space) for space in spaces]


def exchange(x, axes):
    return lax.all_to_all(x, axes, split_axis=0, concat_axis=0, tiled=True)


def swap_core(x):
    return lax.ppermute(x, "core", [(0, 1), (1, 0)])


def ring(x, axis, distance):
    return lax.ppermute(x, axis, [(i, (i + distance) % 4) for i in range(4)])


def per_device(inputs, in_weight, short_kernel, filter_one, filter_two, out_weight, out_grad):
    width = out_weight.shape[0]
    rows = inputs.shape[1]
    devices = lax.axis_size(everyone)
    scale = 1.0 / math.sqrt(devices * rows)
    shape = jax.ShapeDtypeStruct
    f32, bf16 = jnp.float32, jnp.bfloat16
    packed, both = call(
        pack_kernel,
        (shape((width, 8, rows), bf16), shape((rows, 2 * width), bf16)),
        [pltpu.VMEM((width * 8, rows), f32)],
        limit=56 * 1024 * 1024,
    )(inputs, in_weight, filter_one, filter_two, out_weight, out_grad)
    received = exchange(packed, everyone)
    gathered = [both] + [ring(both, "y", distance) for distance in (1, 2, 3)]
    gathered += [swap_core(x) for x in gathered]
    tables = [jnp.asarray(t) for t in transform_tables(devices // 2, rows)]
    back = call(
        convolve_kernel,
        shape((32, 7, 8, rows), bf16),
        [pltpu.VMEM((devices * 8, rows), f32)],
        in_specs=specs(*[pltpu.VMEM] * (2 + len(tables)), *[pl.ANY] * 3),
    )(received, short_kernel, *tables, *gathered[1:4])
    halfway = exchange(back, ("zh", "x", "zl"))
    found = call(
        part_kernel,
        (shape((32, width), f32),) * 4 + (shape((2, 7 * 32, rows), bf16),) * 4,
        [pltpu.VMEM((32 * 7 * 8, rows), f32), pltpu.VMEM((4, 32, width), f32)],
    )(halfway, *gathered)
    part = [found[0]] + [ring(found[distance], "x", distance) for distance in (1, 2, 3)]
    leaving = found[5:]
    part, *leaving = call(
        add_x_kernel,
        (shape((8, 64, rows), bf16),) + (shape(leaving[0].shape, bf16),) * 3,
        in_specs=specs(*[pltpu.VMEM] * 4, *[pl.ANY] * 3),
        out_specs=specs(pltpu.VMEM, *[pl.ANY] * 3),
        input_output_aliases={4: 1, 5: 2, 6: 3},
    )(*part, *leaving)
    near = [ring(leaving[0], "y", 1), ring(leaving[2], "y", 3)]
    part = exchange(part, ("zh", "zl"))
    part, far = call(
        functools.partial(add_z_kernel, scale),
        (shape((16, 64, rows), bf16), shape(leaving[1].shape, bf16)),
        in_specs=specs(pltpu.VMEM, *[pl.ANY] * 3),
        out_specs=specs(pltpu.VMEM, pl.ANY),
        input_output_aliases={3: 1},
    )(part, *near, leaving[1])
    arrived = [found[4], near[0], ring(far, "y", 2), near[1]]
    arrived += [swap_core(x) for x in arrived]
    part = exchange(part, ("x", "y"))
    outputs, grad_inputs, grad_short, grad_one, grad_two = call(
        finish_kernel,
        (
            shape((1, rows, width), bf16),
            shape((1, rows, width), bf16),
            shape((3, 3 * width), f32),
            shape((rows, width), f32),
            shape((rows, width), f32),
        ),
    )(*arrived, in_weight, out_weight)
    part, grad_short = lax.optimization_barrier((part, grad_short))
    grad_in_weight, grad_out_weight = call(
        place_kernel, (shape((width, 3 * width), f32), shape((width, width), f32))
    )(part, swap_core(part))
    return (
        outputs,
        grad_inputs,
        grad_in_weight,
        grad_short,
        grad_one,
        grad_two,
        grad_out_weight,
    )


def solution(mesh):
    mesh = Mesh(mesh.devices.reshape(2, 4, 2, 4, 4), everyone)
    positions = ("x", "core", "zl", "y")
    split_rows, split_filter = P("zh", positions, None), P(positions, None)
    return jax.shard_map(
        per_device,
        mesh=mesh,
        in_specs=(split_rows, P(), P(), split_filter, split_filter, P(), split_rows),
        out_specs=(split_rows, split_rows, P(), P(), split_filter, split_filter, P()),
        check_vma=False,
    )
```

```python
import functools
import math

import jax
import jax.numpy as jnp
import numpy as np
from jax import lax
from jax.experimental import pallas as pl
from jax.experimental.pallas import tpu as pltpu
from jax.sharding import Mesh
from jax.sharding import PartitionSpec as P

everyone = ("zh", "x", "core", "zl", "y")
vmem_limit = 16 * 1024 * 1024


def two_terms(table):
    high = table.astype(np.float32).astype(jnp.bfloat16)
    low = (table - high.astype(np.float64)).astype(np.float32).astype(jnp.bfloat16)
    return high, low


def left_table(table):
    high, low = two_terms(table)
    return np.concatenate([high, low, high], 1)


def right_table(table):
    high, low = two_terms(table)
    return np.concatenate([high, low, high], 0)


def transform_tables(blocks, rows):
    length = 2 * blocks * rows
    outer = np.arange(blocks) + 0.5
    step = 2.0 * math.pi * np.outer(outer, np.arange(blocks)) / (2 * blocks)
    turn = 2.0 * math.pi * np.outer(outer, np.arange(rows)) / length
    inner = 2.0 * math.pi * np.outer(np.arange(rows), np.arange(rows)) / rows
    first = np.concatenate([np.cos(step), -np.sin(step)], 0)
    c, s = np.cos(inner), np.sin(inner)
    second = np.block([[c, -s], [s, c]])
    second_back = np.block([[c, s], [-s, c]])
    first_back = np.concatenate([np.cos(step).T, -np.sin(step).T], 1) * (2.0 / length)
    return [
        left_table(first),
        right_table(second),
        right_table(second_back),
        left_table(first_back),
        np.cos(turn).astype(np.float32),
        np.sin(turn).astype(np.float32),
    ]


def bf16_dot(a, b):
    return jnp.dot(a, b, preferred_element_type=jnp.float32)


def split(x):
    high = x.astype(jnp.bfloat16)
    low = (x - high.astype(jnp.float32)).astype(jnp.bfloat16)
    return high, low


def table_left(table, x):
    x_high, x_low = split(x)
    return bf16_dot(table, jnp.concatenate([x_high, x_high, x_low], 0))


def table_right(x, table):
    x_high, x_low = split(x)
    return bf16_dot(jnp.concatenate([x_high, x_high, x_low], 1), table)


def pack_kernel(seq_ref, in_weight_ref, one_ref, two_ref, out_weight_ref, grad_ref, out_ref, both_ref, rows_ref):
    width = out_weight_ref.shape[0]
    lanes = rows_ref.shape[2]
    contract_first = (((0,), (1,)), ((), ()))
    contract_last = (((1,), (1,)), ((), ()))
    seq = seq_ref[0]

    def put(index, x):
        rows_ref[index // 2, pl.ds(index % 2, width, stride=2), :] = x

    for group in range(3):
        weight = in_weight_ref[:, group * width : (group + 1) * width]
        put(
            group,
            lax.dot_general(weight, seq, contract_first, preferred_element_type=jnp.float32),
        )
    put(
        3,
        lax.dot_general(
            out_weight_ref[...], grad_ref[0], contract_last, preferred_element_type=jnp.float32
        ),
    )
    chosen = jnp.where(lax.axis_index("zh") == 0, one_ref[...], two_ref[...]).T
    high = chosen.astype(jnp.bfloat16).astype(jnp.float32)
    put(4, high)
    put(5, chosen - high)
    both_ref[:, :width] = seq
    both_ref[:, width:] = grad_ref[0]
    for pair in range(3):
        out_ref[:, :, pair * lanes : (pair + 1) * lanes] = (
            rows_ref[pair].reshape(width, 2, lanes).astype(jnp.bfloat16)
        )


def convolve_kernel(
    in_ref,
    short_ref,
    first_ref,
    second_ref,
    second_back_ref,
    first_back_ref,
    turn_cos_ref,
    turn_sin_ref,
    *rest,
):
    out_ref, rows_ref = rest[-2:]
    sources, rows = in_ref.shape[0], in_ref.shape[2] // 3
    blocks = sources // 2
    width = short_ref.shape[1] // 3
    scale = 1.0 / math.sqrt(sources * rows)
    turn_cos = turn_cos_ref[...]
    turn_sin = turn_sin_ref[...]
    lane = lax.broadcasted_iota(jnp.int32, (blocks, rows), 1)
    block = lax.broadcasted_iota(jnp.int32, (blocks, rows), 0)

    for pair in range(3):
        rows_ref[pair] = (
            in_ref[:, :, pair * rows : (pair + 1) * rows]
            .astype(jnp.float32)
            .reshape(sources * 2, rows)
        )

    def row(member, index):
        return rows_ref[index // 2, pl.ds(member * sources + index % 2, blocks, stride=2), :]

    def later(x, distance):
        moved = pltpu.roll(x, distance, 1)
        carried = jnp.where(block == 0, 0.0, pltpu.roll(moved, 1, 0))
        return jnp.where(lane < distance, carried, moved)

    def earlier(x, distance):
        moved = pltpu.roll(x, rows - distance, 1)
        carried = jnp.where(block == blocks - 1, 0.0, pltpu.roll(moved, blocks - 1, 0))
        return jnp.where(lane >= rows - distance, carried, moved)

    def forward(signals):
        outer = table_left(first_ref[...], jnp.concatenate(signals, 1))
        turned = []
        for i in range(len(signals)):
            re = outer[:blocks, i * rows : (i + 1) * rows]
            im = outer[blocks:, i * rows : (i + 1) * rows]
            turned.append(
                jnp.concatenate(
                    [re * turn_cos + im * turn_sin, im * turn_cos - re * turn_sin], 1
                )
            )
        inner = table_right(jnp.concatenate(turned, 0), second_ref[...])
        return [
            (inner[i * blocks : (i + 1) * blocks, :rows], inner[i * blocks : (i + 1) * blocks, rows:])
            for i in range(len(signals))
        ]

    def backward(spectra):
        stacked = jnp.concatenate([jnp.concatenate(pair, 1) for pair in spectra], 0)
        inner = table_right(stacked, second_back_ref[...])
        turned = []
        for i in range(len(spectra)):
            re = inner[i * blocks : (i + 1) * blocks, :rows]
            im = inner[i * blocks : (i + 1) * blocks, rows:]
            turned.append(
                jnp.concatenate(
                    [re * turn_cos - im * turn_sin, im * turn_cos + re * turn_sin], 0
                )
            )
        outer = table_left(first_back_ref[...], jnp.concatenate(turned, 1))
        return [outer[:, i * rows : (i + 1) * rows] for i in range(len(spectra))]

    def times(a, b):
        return a[0] * b[0] - a[1] * b[1], a[0] * b[1] + a[1] * b[0]

    def conj_times(a, b):
        return a[0] * b[0] + a[1] * b[1], a[0] * b[1] - a[1] * b[0]

    def added(a, b):
        return a[0] + b[0], a[1] + b[1]

    mesh_place = lax.axis_index(everyone)
    short = short_ref[...]
    short_lane = lax.broadcasted_iota(jnp.int32, short.shape, 1)
    taps = []
    for group in range(3):
        column = jnp.sum(
            jnp.where(short_lane == mesh_place + group * width, short, 0.0), axis=1, keepdims=True
        )
        taps.append([column[tap : tap + 1, :] for tap in range(3)])

    projected, lagged_one, lagged_two, mixed, pre = [], [], [], [], []
    for member in range(2):
        now = [row(member, group) for group in range(3)]
        one = [later(x, 1) for x in now]
        two = [later(x, 2) for x in now]
        projected.append(now)
        lagged_one.append(one)
        lagged_two.append(two)
        mixed.append(
            [
                taps[g][0] * now[g] + taps[g][1] * one[g] + taps[g][2] * two[g]
                for g in range(3)
            ]
        )
        pre.append(row(member, 3))
    members = range(2)
    grad_conv_two = [pre[m] * mixed[m][2] for m in members]
    spectra = forward(
        [row(m, 4) + row(m, 5) for m in members] + [mixed[m][0] for m in members] + grad_conv_two
    )
    one_spec, two_spec = spectra[0], spectra[1]
    value_spec, conv_two_spec = spectra[2:4], spectra[4:6]
    found = backward(
        [times(one_spec, value_spec[m]) for m in members]
        + [conj_times(two_spec, conv_two_spec[m]) for m in members]
    )
    conv_one, grad_gated = found[:2], found[2:]
    spectra = forward(
        [mixed[m][1] * conv_one[m] for m in members]
        + [mixed[m][1] * grad_gated[m] for m in members]
    )
    gated_spec, conv_one_spec = spectra[:2], spectra[2:]
    found = backward(
        [times(two_spec, gated_spec[m]) for m in members]
        + [conj_times(one_spec, conv_one_spec[m]) for m in members]
        + [
            added(*[conj_times(value_spec[m], conv_one_spec[m]) for m in members]),
            added(*[conj_times(gated_spec[m], conv_two_spec[m]) for m in members]),
        ]
    )
    conv_two, grad_value = found[:2], found[2:4]
    grad_filters = [found[4] * scale, found[5] * scale]

    new = lax.broadcasted_iota(jnp.int32, (blocks, blocks), 0)
    old = lax.broadcasted_iota(jnp.int32, (blocks, blocks), 1)
    wanted = (new & 99) | (((new >> 2) & 1) << 4) | (((new >> 3) & 3) << 2)
    reorder = jnp.where(old == wanted, 1.0, 0.0).astype(jnp.bfloat16)
    sums = [[0.0] * 3 for _ in range(3)]
    for m in members:
        sent = [mixed[m][2] * conv_two[m]]
        grads = [grad_value[m], grad_gated[m] * conv_one[m], pre[m] * conv_two[m]]
        for g in range(3):
            sent.append(
                taps[g][0] * grads[g]
                + taps[g][1] * earlier(grads[g], 1)
                + taps[g][2] * earlier(grads[g], 2)
            )
            for tap, lagged in enumerate((projected, lagged_one, lagged_two)):
                sums[g][tap] = sums[g][tap] + jnp.sum(
                    jnp.sum(grads[g] * lagged[m][g], axis=0, keepdims=True), axis=1, keepdims=True
                )
        sent.extend(grad_filters)
        turned = bf16_dot(reorder, jnp.concatenate(sent, 1).astype(jnp.bfloat16))
        half = out_ref.shape[0] // 2
        for index in range(len(sent)):
            out_ref[m * half : (m + 1) * half, index] = (
                turned[:, index * rows : (index + 1) * rows]
                .reshape(half, blocks // half, rows)
                .astype(jnp.bfloat16)
            )
    shape = (blocks // half, rows)
    sum_lane = lax.broadcasted_iota(jnp.int32, shape, 1)
    line = jnp.zeros(shape, jnp.float32)
    for g in range(3):
        for tap in range(3):
            total = sums[g][tap] * scale
            high = total.astype(jnp.bfloat16).astype(jnp.float32)
            line = jnp.where(sum_lane == g * 3 + tap, high, line)
            line = jnp.where(sum_lane == 16 + g * 3 + tap, total - high, line)
    out_ref[:, 6] = jnp.broadcast_to(line[None], (2 * half,) + shape).astype(jnp.bfloat16)


def channel_order(place_of):
    channel = lax.broadcasted_iota(jnp.int32, (256, 256), 0)
    row = lax.broadcasted_iota(jnp.int32, (256, 256), 1)
    zh, x, core = channel >> 7, (channel >> 5) & 3, (channel >> 4) & 1
    zl, y = (channel >> 2) & 3, channel & 3
    return jnp.where(row == place_of(zh, x, core, zl, y), 1.0, 0.0).astype(jnp.bfloat16)


def part_kernel(in_ref, *refs):
    both_refs, part_refs, send_refs = refs[:8], refs[8:12], refs[12:16]
    rows_ref, sums_ref = refs[16:]
    sources, kinds, blocks, rows = in_ref.shape
    width = both_refs[0].shape[1] // 2
    x, core, y = lax.axis_index("x"), lax.axis_index("core"), lax.axis_index("y")
    rows_ref[...] = in_ref[...].astype(jnp.float32).reshape(sources * kinds * blocks, rows)
    out_part = jnp.zeros((sources, width), jnp.float32)
    in_part = jnp.zeros((3 * sources, width), jnp.float32)
    for other in range(2):
        for ahead in range(4):
            block = (core ^ other) * 4 + ((y + ahead) & 3)
            kept = jnp.concatenate(
                [
                    rows_ref[pl.ds(kind * blocks + block, sources, stride=kinds * blocks), :]
                    for kind in range(kinds)
                ],
                0,
            ).astype(jnp.bfloat16)
            send_refs[ahead][other] = kept
            both_ref = both_refs[other * 4 + (4 - ahead) % 4]
            out_part += bf16_dot(kept[:sources], both_ref[:, width:])
            in_part += bf16_dot(kept[sources : 4 * sources], both_ref[:, :width])
    sums_ref[0] = out_part
    for group in range(3):
        sums_ref[1 + group] = in_part[group * sources : (group + 1) * sources]
    for ahead in range(4):
        part_refs[ahead][...] = sums_ref[(x + ahead) & 3]


def finish_kernel(*refs):
    held = refs[:8]
    in_weight_ref, out_weight_ref, outputs_ref, grad_inputs_ref, short_ref = refs[8:13]
    one_ref, two_ref = refs[13:]
    width = out_weight_ref.shape[0]
    count = width // 8
    core, y = lax.axis_index("core"), lax.axis_index("y")
    order = channel_order(
        lambda zh, x, c, zl, v: (
            (((c ^ core) * 4 + ((y - v) & 3)) * 32) + (zh * 16 + x * 4 + zl)
        )
    )
    contract_first = (((0,), (1,)), ((), ()))
    contract_last = (((1,), (1,)), ((), ()))

    def stacked_rows(kind):
        return jnp.concatenate(
            [held[i][i // 4, kind * count : (kind + 1) * count, :] for i in range(8)], 0
        )

    def natural(kind):
        stacked = stacked_rows(kind)
        return lax.dot_general(
            stacked, order, contract_first, preferred_element_type=jnp.float32
        )

    outputs_ref[0] = bf16_dot(natural(0).astype(jnp.bfloat16), out_weight_ref[...]).astype(
        jnp.bfloat16
    )
    total = None
    for group in range(3):
        term = lax.dot_general(
            natural(1 + group).astype(jnp.bfloat16),
            in_weight_ref[:, group * width : (group + 1) * width],
            contract_last,
            preferred_element_type=jnp.float32,
        )
        total = term if total is None else total + term
    grad_inputs_ref[0] = total.astype(jnp.bfloat16)
    one_ref[...] = natural(4)
    two_ref[...] = natural(5)
    sums = lax.dot_general(
        stacked_rows(6), order, contract_first, preferred_element_type=jnp.float32
    )
    for group in range(3):
        short_ref[:, group * width : (group + 1) * width] = (
            sums[group * 3 : group * 3 + 3, :] + sums[16 + group * 3 : 19 + group * 3, :]
        )


def add_x_kernel(*refs):
    out_ref = refs[7]
    total = refs[0][...] + refs[1][...] + refs[2][...] + refs[3][...]
    lanes = out_ref.shape[2]
    rows = jnp.concatenate([total[:, :lanes], total[:, lanes:]], 0)
    out_ref[...] = jnp.broadcast_to(rows.astype(jnp.bfloat16)[None], out_ref.shape)


def add_z_kernel(scale, in_ref, *refs):
    out_ref = refs[-1]
    total = jnp.sum(in_ref[...].astype(jnp.float32), axis=0) * scale
    out_ref[...] = jnp.broadcast_to(total.astype(jnp.bfloat16)[None], out_ref.shape)


def place_kernel(own_ref, other_ref, in_weight_ref, out_weight_ref):
    width, lanes = out_weight_ref.shape[0], own_ref.shape[2]
    core = lax.axis_index("core")
    order = channel_order(
        lambda zh, x, c, zl, y: ((c ^ core) * 4 + y) * 32 + (zh * 16 + x * 4 + zl)
    )
    contract_first = (((0,), (1,)), ((), ()))
    for kind in range(4):
        for half in range(2):
            stacked = jnp.concatenate(
                [
                    ref[kind * 4 + y, half * 32 : (half + 1) * 32, :]
                    for ref in (own_ref, other_ref)
                    for y in range(4)
                ],
                0,
            )
            if kind == 0:
                out_weight_ref[:, half * lanes : (half + 1) * lanes] = bf16_dot(order, stacked)
            else:
                in_weight_ref[
                    half * lanes : (half + 1) * lanes, (kind - 1) * width : kind * width
                ] = lax.dot_general(
                    stacked, order, contract_first, preferred_element_type=jnp.float32
                )


def call(kernel, out_shape, scratch=(), limit=vmem_limit, **options):
    return pl.pallas_call(
        kernel,
        out_shape=out_shape,
        scratch_shapes=list(scratch),
        compiler_params=pltpu.CompilerParams(vmem_limit_bytes=limit),
        **options,
    )


def specs(*spaces):
    return [pl.BlockSpec(memory_space=space) for space in spaces]


def exchange(x, axes):
    return lax.all_to_all(x, axes, split_axis=0, concat_axis=0, tiled=True)


def swap_core(x):
    return lax.ppermute(x, "core", [(0, 1), (1, 0)])


def ring(x, axis, distance):
    return lax.ppermute(x, axis, [(i, (i + distance) % 4) for i in range(4)])


def per_device(inputs, in_weight, short_kernel, filter_one, filter_two, out_weight, out_grad):
    width = out_weight.shape[0]
    rows = inputs.shape[1]
    devices = lax.axis_size(everyone)
    scale = 1.0 / math.sqrt(devices * rows)
    shape = jax.ShapeDtypeStruct
    f32, bf16 = jnp.float32, jnp.bfloat16
    packed, both = call(
        pack_kernel,
        (shape((width, 2, 3 * rows), bf16), shape((rows, 2 * width), bf16)),
        [pltpu.VMEM((3, 2 * width, rows), f32)],
        limit=56 * 1024 * 1024,
    )(inputs, in_weight, filter_one, filter_two, out_weight, out_grad)
    received = exchange(packed, everyone)
    gathered = [both] + [ring(both, "y", distance) for distance in (1, 2, 3)]
    gathered += [swap_core(x) for x in gathered]
    tables = [jnp.asarray(t) for t in transform_tables(devices // 2, rows)]
    back = call(
        convolve_kernel,
        shape((32, 7, 8, rows), bf16),
        [pltpu.VMEM((3, 2 * devices, rows), f32)],
        in_specs=specs(*[pltpu.VMEM] * (2 + len(tables)), *[pl.ANY] * 3),
    )(received, short_kernel, *tables, *gathered[1:4])
    halfway = exchange(back, ("zh", "x", "zl"))
    found = call(
        part_kernel,
        (shape((32, width), f32),) * 4 + (shape((2, 7 * 32, rows), bf16),) * 4,
        [pltpu.VMEM((32 * 7 * 8, rows), f32), pltpu.VMEM((4, 32, width), f32)],
    )(halfway, *gathered)
    part = [found[0]] + [ring(found[distance], "x", distance) for distance in (1, 2, 3)]
    leaving = found[5:]
    part, *leaving = call(
        add_x_kernel,
        (shape((8, 64, rows), bf16),) + (shape(leaving[0].shape, bf16),) * 3,
        in_specs=specs(*[pltpu.VMEM] * 4, *[pl.ANY] * 3),
        out_specs=specs(pltpu.VMEM, *[pl.ANY] * 3),
        input_output_aliases={4: 1, 5: 2, 6: 3},
    )(*part, *leaving)
    arrived = [found[4]] + [ring(x, "y", 1 + i) for i, x in enumerate(leaving)]
    part = exchange(part, ("zh", "zl"))
    part = call(
        functools.partial(add_z_kernel, scale),
        shape((16, 64, rows), bf16),
        in_specs=specs(pltpu.VMEM, *[pl.ANY] * 3),
    )(part, *arrived[1:])
    arrived += [swap_core(x) for x in arrived]
    part = exchange(part, ("x", "y"))
    outputs, grad_inputs, grad_short, grad_one, grad_two = call(
        finish_kernel,
        (
            shape((1, rows, width), bf16),
            shape((1, rows, width), bf16),
            shape((3, 3 * width), f32),
            shape((rows, width), f32),
            shape((rows, width), f32),
        ),
    )(*arrived, in_weight, out_weight)
    part, grad_short = lax.optimization_barrier((part, grad_short))
    grad_in_weight, grad_out_weight = call(
        place_kernel, (shape((width, 3 * width), f32), shape((width, width), f32))
    )(part, swap_core(part))
    return (
        outputs,
        grad_inputs,
        grad_in_weight,
        grad_short,
        grad_one,
        grad_two,
        grad_out_weight,
    )


def solution(mesh):
    mesh = Mesh(mesh.devices.reshape(2, 4, 2, 4, 4), everyone)
    positions = ("x", "core", "zl", "y")
    split_rows, split_filter = P("zh", positions, None), P(positions, None)
    return jax.shard_map(
        per_device,
        mesh=mesh,
        in_specs=(split_rows, P(), P(), split_filter, split_filter, P(), split_rows),
        out_specs=(split_rows, split_rows, P(), P(), split_filter, split_filter, P()),
        check_vma=False,
    )
```

```python
import functools
import math

import jax
import jax.numpy as jnp
import numpy as np
from jax import lax
from jax.experimental import pallas as pl
from jax.experimental.pallas import tpu as pltpu
from jax.sharding import Mesh
from jax.sharding import PartitionSpec as P

everyone = ("zh", "x", "core", "zl", "y")
vmem_limit = 16 * 1024 * 1024


def two_terms(table):
    high = table.astype(np.float32).astype(jnp.bfloat16)
    low = (table - high.astype(np.float64)).astype(np.float32).astype(jnp.bfloat16)
    return high, low


def left_table(table):
    high, low = two_terms(table)
    return np.concatenate([high, low, high], 1)


def right_table(table):
    high, low = two_terms(table)
    return np.concatenate([high, low, high], 0)


def transform_tables(blocks, rows):
    length = 2 * blocks * rows
    outer = np.arange(blocks) + 0.5
    step = 2.0 * math.pi * np.outer(outer, np.arange(blocks)) / (2 * blocks)
    turn = 2.0 * math.pi * np.outer(outer, np.arange(rows)) / length
    inner = 2.0 * math.pi * np.outer(np.arange(rows), np.arange(rows)) / rows
    first = np.concatenate([np.cos(step), -np.sin(step)], 0)
    c, s = np.cos(inner), np.sin(inner)
    second = np.block([[c, -s], [s, c]])
    second_back = np.block([[c, s], [-s, c]])
    first_back = np.concatenate([np.cos(step).T, -np.sin(step).T], 1) * (2.0 / length)
    return [
        left_table(first),
        right_table(second),
        right_table(second_back),
        left_table(first_back),
        np.cos(turn).astype(np.float32),
        np.sin(turn).astype(np.float32),
    ]


def bf16_dot(a, b):
    return jnp.dot(a, b, preferred_element_type=jnp.float32)


def split(x):
    high = x.astype(jnp.bfloat16)
    low = (x - high.astype(jnp.float32)).astype(jnp.bfloat16)
    return high, low


def table_left(table, x):
    x_high, x_low = split(x)
    return bf16_dot(table, jnp.concatenate([x_high, x_high, x_low], 0))


def table_right(x, table):
    x_high, x_low = split(x)
    return bf16_dot(jnp.concatenate([x_high, x_high, x_low], 1), table)


def pack_kernel(seq_ref, in_weight_ref, one_ref, two_ref, out_weight_ref, grad_ref, out_ref, both_ref, rows_ref):
    width = out_weight_ref.shape[0]
    lanes = rows_ref.shape[2]
    contract_first = (((0,), (1,)), ((), ()))
    contract_last = (((1,), (1,)), ((), ()))
    seq = seq_ref[0]

    def put(index, x):
        rows_ref[index // 2, pl.ds(index % 2, width, stride=2), :] = x

    for group in range(3):
        weight = in_weight_ref[:, group * width : (group + 1) * width]
        put(
            group,
            lax.dot_general(weight, seq, contract_first, preferred_element_type=jnp.float32),
        )
    put(
        3,
        lax.dot_general(
            out_weight_ref[...], grad_ref[0], contract_last, preferred_element_type=jnp.float32
        ),
    )
    chosen = jnp.where(lax.axis_index("zh") == 0, one_ref[...], two_ref[...]).T
    high = chosen.astype(jnp.bfloat16).astype(jnp.float32)
    put(4, high)
    put(5, chosen - high)
    both_ref[:, :width] = seq
    both_ref[:, width:] = grad_ref[0]
    for pair in range(3):
        out_ref[:, :, pair * lanes : (pair + 1) * lanes] = (
            rows_ref[pair].reshape(width, 2, lanes).astype(jnp.bfloat16)
        )


def convolve_kernel(
    in_ref,
    short_ref,
    first_ref,
    second_ref,
    second_back_ref,
    first_back_ref,
    turn_cos_ref,
    turn_sin_ref,
    *rest,
):
    out_ref, rows_ref = rest[-2:]
    sources, rows = in_ref.shape[0], in_ref.shape[2] // 3
    blocks = sources // 2
    width = short_ref.shape[1] // 3
    scale = 1.0 / math.sqrt(sources * rows)
    turn_cos = turn_cos_ref[...]
    turn_sin = turn_sin_ref[...]
    lane = lax.broadcasted_iota(jnp.int32, (blocks, rows), 1)
    block = lax.broadcasted_iota(jnp.int32, (blocks, rows), 0)

    for pair in range(3):
        rows_ref[pair] = (
            in_ref[:, :, pair * rows : (pair + 1) * rows]
            .astype(jnp.float32)
            .reshape(sources * 2, rows)
        )

    def row(member, index):
        return rows_ref[index // 2, pl.ds(member * sources + index % 2, blocks, stride=2), :]

    def later(x, distance):
        moved = pltpu.roll(x, distance, 1)
        carried = jnp.where(block == 0, 0.0, pltpu.roll(moved, 1, 0))
        return jnp.where(lane < distance, carried, moved)

    def earlier(x, distance):
        moved = pltpu.roll(x, rows - distance, 1)
        carried = jnp.where(block == blocks - 1, 0.0, pltpu.roll(moved, blocks - 1, 0))
        return jnp.where(lane >= rows - distance, carried, moved)

    def forward(signals):
        outer = table_left(first_ref[...], jnp.concatenate(signals, 1))
        turned = []
        for i in range(len(signals)):
            re = outer[:blocks, i * rows : (i + 1) * rows]
            im = outer[blocks:, i * rows : (i + 1) * rows]
            turned.append(
                jnp.concatenate(
                    [re * turn_cos + im * turn_sin, im * turn_cos - re * turn_sin], 1
                )
            )
        inner = table_right(jnp.concatenate(turned, 0), second_ref[...])
        return [
            (inner[i * blocks : (i + 1) * blocks, :rows], inner[i * blocks : (i + 1) * blocks, rows:])
            for i in range(len(signals))
        ]

    def backward(spectra):
        stacked = jnp.concatenate([jnp.concatenate(pair, 1) for pair in spectra], 0)
        inner = table_right(stacked, second_back_ref[...])
        turned = []
        for i in range(len(spectra)):
            re = inner[i * blocks : (i + 1) * blocks, :rows]
            im = inner[i * blocks : (i + 1) * blocks, rows:]
            turned.append(
                jnp.concatenate(
                    [re * turn_cos - im * turn_sin, im * turn_cos + re * turn_sin], 0
                )
            )
        outer = table_left(first_back_ref[...], jnp.concatenate(turned, 1))
        return [outer[:, i * rows : (i + 1) * rows] for i in range(len(spectra))]

    def times(a, b):
        return a[0] * b[0] - a[1] * b[1], a[0] * b[1] + a[1] * b[0]

    def conj_times(a, b):
        return a[0] * b[0] + a[1] * b[1], a[0] * b[1] - a[1] * b[0]

    def added(a, b):
        return a[0] + b[0], a[1] + b[1]

    mesh_place = lax.axis_index(everyone)
    short = short_ref[...]
    short_lane = lax.broadcasted_iota(jnp.int32, short.shape, 1)
    taps = []
    for group in range(3):
        column = jnp.sum(
            jnp.where(short_lane == mesh_place + group * width, short, 0.0), axis=1, keepdims=True
        )
        taps.append([column[tap : tap + 1, :] for tap in range(3)])

    projected, lagged_one, lagged_two, mixed, pre = [], [], [], [], []
    for member in range(2):
        now = [row(member, group) for group in range(3)]
        one = [later(x, 1) for x in now]
        two = [later(x, 2) for x in now]
        projected.append(now)
        lagged_one.append(one)
        lagged_two.append(two)
        mixed.append(
            [
                taps[g][0] * now[g] + taps[g][1] * one[g] + taps[g][2] * two[g]
                for g in range(3)
            ]
        )
        pre.append(row(member, 3))
    members = range(2)
    grad_conv_two = [pre[m] * mixed[m][2] for m in members]
    spectra = forward(
        [row(m, 4) + row(m, 5) for m in members] + [mixed[m][0] for m in members] + grad_conv_two
    )
    one_spec, two_spec = spectra[0], spectra[1]
    value_spec, conv_two_spec = spectra[2:4], spectra[4:6]
    found = backward(
        [times(one_spec, value_spec[m]) for m in members]
        + [conj_times(two_spec, conv_two_spec[m]) for m in members]
    )
    conv_one, grad_gated = found[:2], found[2:]
    spectra = forward(
        [mixed[m][1] * conv_one[m] for m in members]
        + [mixed[m][1] * grad_gated[m] for m in members]
    )
    gated_spec, conv_one_spec = spectra[:2], spectra[2:]
    found = backward(
        [times(two_spec, gated_spec[m]) for m in members]
        + [conj_times(one_spec, conv_one_spec[m]) for m in members]
        + [
            added(*[conj_times(value_spec[m], conv_one_spec[m]) for m in members]),
            added(*[conj_times(gated_spec[m], conv_two_spec[m]) for m in members]),
        ]
    )
    conv_two, grad_value = found[:2], found[2:4]
    grad_filters = [found[4] * scale, found[5] * scale]

    new = lax.broadcasted_iota(jnp.int32, (blocks, blocks), 0)
    old = lax.broadcasted_iota(jnp.int32, (blocks, blocks), 1)
    wanted = (new & 99) | (((new >> 2) & 1) << 4) | (((new >> 3) & 3) << 2)
    reorder = jnp.where(old == wanted, 1.0, 0.0).astype(jnp.bfloat16)
    sums = [[0.0] * 3 for _ in range(3)]
    for m in members:
        sent = [mixed[m][2] * conv_two[m]]
        grads = [grad_value[m], grad_gated[m] * conv_one[m], pre[m] * conv_two[m]]
        for g in range(3):
            sent.append(
                taps[g][0] * grads[g]
                + taps[g][1] * earlier(grads[g], 1)
                + taps[g][2] * earlier(grads[g], 2)
            )
            for tap, lagged in enumerate((projected, lagged_one, lagged_two)):
                sums[g][tap] = sums[g][tap] + jnp.sum(
                    jnp.sum(grads[g] * lagged[m][g], axis=0, keepdims=True), axis=1, keepdims=True
                )
        sent.extend(grad_filters)
        turned = bf16_dot(reorder, jnp.concatenate(sent, 1).astype(jnp.bfloat16))
        half = out_ref.shape[0] // 2
        for index in range(len(sent)):
            out_ref[m * half : (m + 1) * half, index] = (
                turned[:, index * rows : (index + 1) * rows]
                .reshape(half, blocks // half, rows)
                .astype(jnp.bfloat16)
            )
    shape = (blocks // half, rows)
    sum_lane = lax.broadcasted_iota(jnp.int32, shape, 1)
    line = jnp.zeros(shape, jnp.float32)
    for g in range(3):
        for tap in range(3):
            total = sums[g][tap] * scale
            high = total.astype(jnp.bfloat16).astype(jnp.float32)
            line = jnp.where(sum_lane == g * 3 + tap, high, line)
            line = jnp.where(sum_lane == 16 + g * 3 + tap, total - high, line)
    out_ref[:, 6] = jnp.broadcast_to(line[None], (2 * half,) + shape).astype(jnp.bfloat16)


def channel_order(place_of):
    channel = lax.broadcasted_iota(jnp.int32, (256, 256), 0)
    row = lax.broadcasted_iota(jnp.int32, (256, 256), 1)
    zh, x, core = channel >> 7, (channel >> 5) & 3, (channel >> 4) & 1
    zl, y = (channel >> 2) & 3, channel & 3
    return jnp.where(row == place_of(zh, x, core, zl, y), 1.0, 0.0).astype(jnp.bfloat16)


def part_kernel(in_ref, *refs):
    both_refs, part_refs, send_refs = refs[:8], refs[8:12], refs[12:16]
    rows_ref, sums_ref = refs[16:]
    sources, kinds, blocks, rows = in_ref.shape
    width = both_refs[0].shape[1] // 2
    x, core, y = lax.axis_index("x"), lax.axis_index("core"), lax.axis_index("y")
    turn = 1 - 2 * core
    rows_ref[...] = in_ref[...].astype(jnp.float32).reshape(sources * kinds * blocks, rows)
    out_part = jnp.zeros((sources, width), jnp.float32)
    in_part = jnp.zeros((3 * sources, width), jnp.float32)
    for other in range(2):
        for ahead in range(4):
            block = (core ^ other) * 4 + ((y + turn * ahead) & 3)
            kept = jnp.concatenate(
                [
                    rows_ref[pl.ds(kind * blocks + block, sources, stride=kinds * blocks), :]
                    for kind in range(kinds)
                ],
                0,
            ).astype(jnp.bfloat16)
            send_refs[ahead][other] = kept
            both_ref = both_refs[4 + ahead if other else (4 - ahead) % 4]
            out_part += bf16_dot(kept[:sources], both_ref[:, width:])
            in_part += bf16_dot(kept[sources : 4 * sources], both_ref[:, :width])
    sums_ref[0] = out_part
    for group in range(3):
        sums_ref[1 + group] = in_part[group * sources : (group + 1) * sources]
    for ahead in range(4):
        part_refs[ahead][...] = sums_ref[(x + turn * ahead) & 3]


def finish_kernel(*refs):
    held = refs[:8]
    in_weight_ref, out_weight_ref, outputs_ref, grad_inputs_ref, short_ref = refs[8:13]
    one_ref, two_ref = refs[13:]
    width = out_weight_ref.shape[0]
    count = width // 8
    core, y = lax.axis_index("core"), lax.axis_index("y")
    turn = 1 - 2 * core

    def row_of(zh, x, c, zl, v):
        other = c ^ core
        step = (turn * (1 - 2 * other) * (y - v)) & 3
        return (other * 4 + step) * 32 + (zh * 16 + x * 4 + zl)

    order = channel_order(row_of)
    contract_first = (((0,), (1,)), ((), ()))
    contract_last = (((1,), (1,)), ((), ()))

    def stacked_rows(kind):
        return jnp.concatenate(
            [held[i][i // 4, kind * count : (kind + 1) * count, :] for i in range(8)], 0
        )

    def natural(kind):
        stacked = stacked_rows(kind)
        return lax.dot_general(
            stacked, order, contract_first, preferred_element_type=jnp.float32
        )

    outputs_ref[0] = bf16_dot(natural(0).astype(jnp.bfloat16), out_weight_ref[...]).astype(
        jnp.bfloat16
    )
    total = None
    for group in range(3):
        term = lax.dot_general(
            natural(1 + group).astype(jnp.bfloat16),
            in_weight_ref[:, group * width : (group + 1) * width],
            contract_last,
            preferred_element_type=jnp.float32,
        )
        total = term if total is None else total + term
    grad_inputs_ref[0] = total.astype(jnp.bfloat16)
    one_ref[...] = natural(4)
    two_ref[...] = natural(5)
    sums = lax.dot_general(
        stacked_rows(6), order, contract_first, preferred_element_type=jnp.float32
    )
    for group in range(3):
        short_ref[:, group * width : (group + 1) * width] = (
            sums[group * 3 : group * 3 + 3, :] + sums[16 + group * 3 : 19 + group * 3, :]
        )


def add_x_kernel(*refs):
    out_ref = refs[7]
    total = refs[0][...] + refs[1][...] + refs[2][...] + refs[3][...]
    lanes = out_ref.shape[2]
    rows = jnp.concatenate([total[:, :lanes], total[:, lanes:]], 0)
    out_ref[...] = jnp.broadcast_to(rows.astype(jnp.bfloat16)[None], out_ref.shape)


def add_z_kernel(scale, in_ref, *refs):
    out_ref = refs[-1]
    total = jnp.sum(in_ref[...].astype(jnp.float32), axis=0) * scale
    out_ref[...] = jnp.broadcast_to(total.astype(jnp.bfloat16)[None], out_ref.shape)


def place_kernel(own_ref, other_ref, in_weight_ref, out_weight_ref):
    width, lanes = out_weight_ref.shape[0], own_ref.shape[2]
    core = lax.axis_index("core")
    order = channel_order(
        lambda zh, x, c, zl, y: ((c ^ core) * 4 + y) * 32 + (zh * 16 + x * 4 + zl)
    )
    contract_first = (((0,), (1,)), ((), ()))
    for kind in range(4):
        for half in range(2):
            stacked = jnp.concatenate(
                [
                    ref[kind * 4 + y, half * 32 : (half + 1) * 32, :]
                    for ref in (own_ref, other_ref)
                    for y in range(4)
                ],
                0,
            )
            if kind == 0:
                out_weight_ref[:, half * lanes : (half + 1) * lanes] = bf16_dot(order, stacked)
            else:
                in_weight_ref[
                    half * lanes : (half + 1) * lanes, (kind - 1) * width : kind * width
                ] = lax.dot_general(
                    stacked, order, contract_first, preferred_element_type=jnp.float32
                )


def call(kernel, out_shape, scratch=(), limit=vmem_limit, **options):
    return pl.pallas_call(
        kernel,
        out_shape=out_shape,
        scratch_shapes=list(scratch),
        compiler_params=pltpu.CompilerParams(vmem_limit_bytes=limit),
        **options,
    )


def specs(*spaces):
    return [pl.BlockSpec(memory_space=space) for space in spaces]


def exchange(x, axes):
    return lax.all_to_all(x, axes, split_axis=0, concat_axis=0, tiled=True)


def swap_core(x):
    return lax.ppermute(x, "core", [(0, 1), (1, 0)])


def ring(x, axis, distance):
    axes = ("x", "core") if axis == "x" else ("core", "y")
    route = []
    for core, turn in ((0, distance), (1, -distance)):
        for i in range(4):
            j = (i + turn) % 4
            pair = (i * 2 + core, j * 2 + core) if axis == "x" else (core * 4 + i, core * 4 + j)
            route.append(pair)
    return lax.ppermute(x, axes, route)


def per_device(inputs, in_weight, short_kernel, filter_one, filter_two, out_weight, out_grad):
    width = out_weight.shape[0]
    rows = inputs.shape[1]
    devices = lax.axis_size(everyone)
    scale = 1.0 / math.sqrt(devices * rows)
    shape = jax.ShapeDtypeStruct
    f32, bf16 = jnp.float32, jnp.bfloat16
    packed, both = call(
        pack_kernel,
        (shape((width, 2, 3 * rows), bf16), shape((rows, 2 * width), bf16)),
        [pltpu.VMEM((3, 2 * width, rows), f32)],
        limit=56 * 1024 * 1024,
    )(inputs, in_weight, filter_one, filter_two, out_weight, out_grad)
    received = exchange(packed, everyone)
    gathered = [both] + [ring(both, "y", distance) for distance in (1, 2, 3)]
    gathered += [swap_core(x) for x in gathered]
    tables = [jnp.asarray(t) for t in transform_tables(devices // 2, rows)]
    back = call(
        convolve_kernel,
        shape((32, 7, 8, rows), bf16),
        [pltpu.VMEM((3, 2 * devices, rows), f32)],
        in_specs=specs(*[pltpu.VMEM] * (2 + len(tables)), *[pl.ANY] * 2),
    )(received, short_kernel, *tables, gathered[1], gathered[3])
    halfway = exchange(back, ("zh", "x", "zl"))
    found = call(
        part_kernel,
        (shape((32, width), f32),) * 4 + (shape((2, 7 * 32, rows), bf16),) * 4,
        [pltpu.VMEM((32 * 7 * 8, rows), f32), pltpu.VMEM((4, 32, width), f32)],
    )(halfway, *gathered)
    part = [found[0]] + [ring(found[distance], "x", distance) for distance in (1, 2, 3)]
    leaving = found[5:]
    part, *leaving = call(
        add_x_kernel,
        (shape((8, 64, rows), bf16),) + (shape(leaving[0].shape, bf16),) * 3,
        in_specs=specs(*[pltpu.VMEM] * 4, *[pl.ANY] * 3),
        out_specs=specs(pltpu.VMEM, *[pl.ANY] * 3),
        input_output_aliases={4: 1, 5: 2, 6: 3},
    )(*part, *leaving)
    arrived = [found[4]] + [ring(x, "y", 1 + i) for i, x in enumerate(leaving)]
    part = exchange(part, ("zh", "zl"))
    part = call(
        functools.partial(add_z_kernel, scale),
        shape((16, 64, rows), bf16),
        in_specs=specs(pltpu.VMEM, *[pl.ANY] * 3),
    )(part, *arrived[1:])
    arrived += [swap_core(x) for x in arrived]
    part = exchange(part, ("x", "y"))
    outputs, grad_inputs, grad_short, grad_one, grad_two = call(
        finish_kernel,
        (
            shape((1, rows, width), bf16),
            shape((1, rows, width), bf16),
            shape((3, 3 * width), f32),
            shape((rows, width), f32),
            shape((rows, width), f32),
        ),
    )(*arrived, in_weight, out_weight)
    part, grad_short = lax.optimization_barrier((part, grad_short))
    grad_in_weight, grad_out_weight = call(
        place_kernel, (shape((width, 3 * width), f32), shape((width, width), f32))
    )(part, swap_core(part))
    return (
        outputs,
        grad_inputs,
        grad_in_weight,
        grad_short,
        grad_one,
        grad_two,
        grad_out_weight,
    )


def solution(mesh):
    mesh = Mesh(mesh.devices.reshape(2, 4, 2, 4, 4), everyone)
    positions = ("x", "core", "zl", "y")
    split_rows, split_filter = P("zh", positions, None), P(positions, None)
    return jax.shard_map(
        per_device,
        mesh=mesh,
        in_specs=(split_rows, P(), P(), split_filter, split_filter, P(), split_rows),
        out_specs=(split_rows, split_rows, P(), P(), split_filter, split_filter, P()),
        check_vma=False,
    )
```

```python
import functools
import math

import jax
import jax.numpy as jnp
import numpy as np
from jax import lax
from jax.experimental import pallas as pl
from jax.experimental.pallas import tpu as pltpu
from jax.sharding import Mesh
from jax.sharding import PartitionSpec as P

everyone = ("zh", "x", "core", "zl", "y")
vmem_limit = 16 * 1024 * 1024


def two_terms(table):
    high = table.astype(np.float32).astype(jnp.bfloat16)
    low = (table - high.astype(np.float64)).astype(np.float32).astype(jnp.bfloat16)
    return high, low


def left_table(table):
    high, low = two_terms(table)
    return np.concatenate([high, low, high], 1)


def right_table(table):
    high, low = two_terms(table)
    return np.concatenate([high, low, high], 0)


def transform_tables(blocks, rows):
    length = 2 * blocks * rows
    outer = np.arange(blocks) + 0.5
    step = 2.0 * math.pi * np.outer(outer, np.arange(blocks)) / (2 * blocks)
    turn = 2.0 * math.pi * np.outer(outer, np.arange(rows)) / length
    inner = 2.0 * math.pi * np.outer(np.arange(rows), np.arange(rows)) / rows
    first = np.concatenate([np.cos(step), -np.sin(step)], 0)
    c, s = np.cos(inner), np.sin(inner)
    second = np.block([[c, -s], [s, c]])
    second_back = np.block([[c, s], [-s, c]])
    first_back = np.concatenate([np.cos(step).T, -np.sin(step).T], 1) * (2.0 / length)
    return [
        left_table(first),
        right_table(second),
        right_table(second_back),
        left_table(first_back),
        np.cos(turn).astype(np.float32),
        np.sin(turn).astype(np.float32),
    ]


def bf16_dot(a, b):
    return jnp.dot(a, b, preferred_element_type=jnp.float32)


def split(x):
    high = x.astype(jnp.bfloat16)
    low = (x - high.astype(jnp.float32)).astype(jnp.bfloat16)
    return high, low


def table_left(table, x):
    x_high, x_low = split(x)
    return bf16_dot(table, jnp.concatenate([x_high, x_high, x_low], 0))


def table_right(x, table):
    x_high, x_low = split(x)
    return bf16_dot(jnp.concatenate([x_high, x_high, x_low], 1), table)


def pack_kernel(seq_ref, in_weight_ref, one_ref, two_ref, out_weight_ref, grad_ref, out_ref, both_ref, rows_ref):
    width = out_weight_ref.shape[0]
    lanes = rows_ref.shape[2]
    contract_first = (((0,), (1,)), ((), ()))
    contract_last = (((1,), (1,)), ((), ()))
    seq = seq_ref[0]

    def put(index, x):
        rows_ref[index // 2, pl.ds(index % 2, width, stride=2), :] = x

    for group in range(3):
        weight = in_weight_ref[:, group * width : (group + 1) * width]
        put(
            group,
            lax.dot_general(weight, seq, contract_first, preferred_element_type=jnp.float32),
        )
    put(
        3,
        lax.dot_general(
            out_weight_ref[...], grad_ref[0], contract_last, preferred_element_type=jnp.float32
        ),
    )
    chosen = jnp.where(lax.axis_index("zh") == 0, one_ref[...], two_ref[...]).T
    high = chosen.astype(jnp.bfloat16).astype(jnp.float32)
    put(4, high)
    put(5, chosen - high)
    both_ref[:, :width] = seq
    both_ref[:, width:] = grad_ref[0]
    for pair in range(3):
        out_ref[:, :, pair * lanes : (pair + 1) * lanes] = (
            rows_ref[pair].reshape(width, 2, lanes).astype(jnp.bfloat16)
        )


def convolve_kernel(
    in_ref,
    short_ref,
    first_ref,
    second_ref,
    second_back_ref,
    first_back_ref,
    turn_cos_ref,
    turn_sin_ref,
    *rest,
):
    out_ref, rows_ref = rest[-2:]
    sources, rows = in_ref.shape[0], in_ref.shape[2] // 3
    blocks = sources // 2
    width = short_ref.shape[1] // 3
    scale = 1.0 / math.sqrt(sources * rows)
    turn_cos = turn_cos_ref[...]
    turn_sin = turn_sin_ref[...]
    lane = lax.broadcasted_iota(jnp.int32, (blocks, rows), 1)
    block = lax.broadcasted_iota(jnp.int32, (blocks, rows), 0)

    for pair in range(3):
        rows_ref[pair] = (
            in_ref[:, :, pair * rows : (pair + 1) * rows]
            .astype(jnp.float32)
            .reshape(sources * 2, rows)
        )

    def row(member, index):
        return rows_ref[index // 2, pl.ds(member * sources + index % 2, blocks, stride=2), :]

    def later(x, distance):
        moved = pltpu.roll(x, distance, 1)
        carried = jnp.where(block == 0, 0.0, pltpu.roll(moved, 1, 0))
        return jnp.where(lane < distance, carried, moved)

    def earlier(x, distance):
        moved = pltpu.roll(x, rows - distance, 1)
        carried = jnp.where(block == blocks - 1, 0.0, pltpu.roll(moved, blocks - 1, 0))
        return jnp.where(lane >= rows - distance, carried, moved)

    def forward(signals):
        outer = table_left(first_ref[...], jnp.concatenate(signals, 1))
        turned = []
        for i in range(len(signals)):
            re = outer[:blocks, i * rows : (i + 1) * rows]
            im = outer[blocks:, i * rows : (i + 1) * rows]
            turned.append(
                jnp.concatenate(
                    [re * turn_cos + im * turn_sin, im * turn_cos - re * turn_sin], 1
                )
            )
        inner = table_right(jnp.concatenate(turned, 0), second_ref[...])
        return [
            (inner[i * blocks : (i + 1) * blocks, :rows], inner[i * blocks : (i + 1) * blocks, rows:])
            for i in range(len(signals))
        ]

    def backward(spectra):
        stacked = jnp.concatenate([jnp.concatenate(pair, 1) for pair in spectra], 0)
        inner = table_right(stacked, second_back_ref[...])
        turned = []
        for i in range(len(spectra)):
            re = inner[i * blocks : (i + 1) * blocks, :rows]
            im = inner[i * blocks : (i + 1) * blocks, rows:]
            turned.append(
                jnp.concatenate(
                    [re * turn_cos - im * turn_sin, im * turn_cos + re * turn_sin], 0
                )
            )
        outer = table_left(first_back_ref[...], jnp.concatenate(turned, 1))
        return [outer[:, i * rows : (i + 1) * rows] for i in range(len(spectra))]

    def times(a, b):
        return a[0] * b[0] - a[1] * b[1], a[0] * b[1] + a[1] * b[0]

    def conj_times(a, b):
        return a[0] * b[0] + a[1] * b[1], a[0] * b[1] - a[1] * b[0]

    def added(a, b):
        return a[0] + b[0], a[1] + b[1]

    mesh_place = lax.axis_index(everyone)
    short = short_ref[...]
    short_lane = lax.broadcasted_iota(jnp.int32, short.shape, 1)
    taps = []
    for group in range(3):
        column = jnp.sum(
            jnp.where(short_lane == mesh_place + group * width, short, 0.0), axis=1, keepdims=True
        )
        taps.append([column[tap : tap + 1, :] for tap in range(3)])

    projected, lagged_one, lagged_two, mixed, pre = [], [], [], [], []
    for member in range(2):
        now = [row(member, group) for group in range(3)]
        one = [later(x, 1) for x in now]
        two = [later(x, 2) for x in now]
        projected.append(now)
        lagged_one.append(one)
        lagged_two.append(two)
        mixed.append(
            [
                taps[g][0] * now[g] + taps[g][1] * one[g] + taps[g][2] * two[g]
                for g in range(3)
            ]
        )
        pre.append(row(member, 3))
    members = range(2)
    grad_conv_two = [pre[m] * mixed[m][2] for m in members]
    spectra = forward(
        [row(m, 4) + row(m, 5) for m in members] + [mixed[m][0] for m in members] + grad_conv_two
    )
    one_spec, two_spec = spectra[0], spectra[1]
    value_spec, conv_two_spec = spectra[2:4], spectra[4:6]
    found = backward(
        [times(one_spec, value_spec[m]) for m in members]
        + [conj_times(two_spec, conv_two_spec[m]) for m in members]
    )
    conv_one, grad_gated = found[:2], found[2:]
    spectra = forward(
        [mixed[m][1] * conv_one[m] for m in members]
        + [mixed[m][1] * grad_gated[m] for m in members]
    )
    gated_spec, conv_one_spec = spectra[:2], spectra[2:]
    found = backward(
        [times(two_spec, gated_spec[m]) for m in members]
        + [conj_times(one_spec, conv_one_spec[m]) for m in members]
        + [
            added(*[conj_times(value_spec[m], conv_one_spec[m]) for m in members]),
            added(*[conj_times(gated_spec[m], conv_two_spec[m]) for m in members]),
        ]
    )
    conv_two, grad_value = found[:2], found[2:4]
    grad_filters = [found[4] * scale, found[5] * scale]

    new = lax.broadcasted_iota(jnp.int32, (blocks, blocks), 0)
    old = lax.broadcasted_iota(jnp.int32, (blocks, blocks), 1)
    wanted = (new & 99) | (((new >> 2) & 1) << 4) | (((new >> 3) & 3) << 2)
    reorder = jnp.where(old == wanted, 1.0, 0.0).astype(jnp.bfloat16)
    sums = [[0.0] * 3 for _ in range(3)]
    for m in members:
        sent = [mixed[m][2] * conv_two[m]]
        grads = [grad_value[m], grad_gated[m] * conv_one[m], pre[m] * conv_two[m]]
        for g in range(3):
            sent.append(
                taps[g][0] * grads[g]
                + taps[g][1] * earlier(grads[g], 1)
                + taps[g][2] * earlier(grads[g], 2)
            )
            for tap, lagged in enumerate((projected, lagged_one, lagged_two)):
                sums[g][tap] = sums[g][tap] + jnp.sum(
                    jnp.sum(grads[g] * lagged[m][g], axis=0, keepdims=True), axis=1, keepdims=True
                )
        sent.extend(grad_filters)
        turned = bf16_dot(reorder, jnp.concatenate(sent, 1).astype(jnp.bfloat16))
        half = out_ref.shape[0] // 2
        for index in range(len(sent)):
            out_ref[m * half : (m + 1) * half, index] = (
                turned[:, index * rows : (index + 1) * rows]
                .reshape(half, blocks // half, rows)
                .astype(jnp.bfloat16)
            )
    shape = (blocks // half, rows)
    sum_lane = lax.broadcasted_iota(jnp.int32, shape, 1)
    line = jnp.zeros(shape, jnp.float32)
    for g in range(3):
        for tap in range(3):
            total = sums[g][tap] * scale
            high = total.astype(jnp.bfloat16).astype(jnp.float32)
            line = jnp.where(sum_lane == g * 3 + tap, high, line)
            line = jnp.where(sum_lane == 16 + g * 3 + tap, total - high, line)
    out_ref[:, 6] = jnp.broadcast_to(line[None], (2 * half,) + shape).astype(jnp.bfloat16)


def channel_order(place_of):
    channel = lax.broadcasted_iota(jnp.int32, (256, 256), 0)
    row = lax.broadcasted_iota(jnp.int32, (256, 256), 1)
    zh, x, core = channel >> 7, (channel >> 5) & 3, (channel >> 4) & 1
    zl, y = (channel >> 2) & 3, channel & 3
    return jnp.where(row == place_of(zh, x, core, zl, y), 1.0, 0.0).astype(jnp.bfloat16)


def part_kernel(in_ref, *refs):
    both_refs, part_refs, send_refs = refs[:8], refs[8:12], refs[12:16]
    rows_ref, sums_ref = refs[16:]
    sources, kinds, blocks, rows = in_ref.shape
    width = both_refs[0].shape[1] // 2
    x, core, y = lax.axis_index("x"), lax.axis_index("core"), lax.axis_index("y")
    turn = 1 - 2 * core
    rows_ref[...] = in_ref[...].astype(jnp.float32).reshape(sources * kinds * blocks, rows)
    out_part = jnp.zeros((sources, width), jnp.float32)
    in_part = jnp.zeros((3 * sources, width), jnp.float32)
    for other in range(2):
        for ahead in range(4):
            block = (core ^ other) * 4 + ((y + turn * ahead) & 3)
            kept = jnp.concatenate(
                [
                    rows_ref[pl.ds(kind * blocks + block, sources, stride=kinds * blocks), :]
                    for kind in range(kinds)
                ],
                0,
            ).astype(jnp.bfloat16)
            send_refs[ahead][other] = kept
            both_ref = both_refs[4 + ahead if other else (4 - ahead) % 4]
            out_part += bf16_dot(kept[:sources], both_ref[:, width:])
            in_part += bf16_dot(kept[sources : 4 * sources], both_ref[:, :width])
    sums_ref[0] = out_part
    for group in range(3):
        sums_ref[1 + group] = in_part[group * sources : (group + 1) * sources]
    for ahead in range(4):
        part_refs[ahead][...] = sums_ref[(x + turn * ahead) & 3]


def finish_kernel(*refs):
    held = refs[:8]
    in_weight_ref, out_weight_ref, outputs_ref, grad_inputs_ref, short_ref = refs[8:13]
    one_ref, two_ref = refs[13:]
    width = out_weight_ref.shape[0]
    count = width // 8
    core, y = lax.axis_index("core"), lax.axis_index("y")
    turn = 1 - 2 * core

    def row_of(zh, x, c, zl, v):
        other = c ^ core
        step = (turn * (1 - 2 * other) * (y - v)) & 3
        return (other * 4 + step) * 32 + (zh * 16 + x * 4 + zl)

    order = channel_order(row_of)
    contract_first = (((0,), (1,)), ((), ()))
    contract_last = (((1,), (1,)), ((), ()))

    def stacked_rows(kind):
        return jnp.concatenate(
            [held[i][i // 4, kind * count : (kind + 1) * count, :] for i in range(8)], 0
        )

    def natural(kind):
        stacked = stacked_rows(kind)
        return lax.dot_general(
            stacked, order, contract_first, preferred_element_type=jnp.float32
        )

    outputs_ref[0] = bf16_dot(natural(0).astype(jnp.bfloat16), out_weight_ref[...]).astype(
        jnp.bfloat16
    )
    total = None
    for group in range(3):
        term = lax.dot_general(
            natural(1 + group).astype(jnp.bfloat16),
            in_weight_ref[:, group * width : (group + 1) * width],
            contract_last,
            preferred_element_type=jnp.float32,
        )
        total = term if total is None else total + term
    grad_inputs_ref[0] = total.astype(jnp.bfloat16)
    one_ref[...] = natural(4)
    two_ref[...] = natural(5)
    sums = lax.dot_general(
        stacked_rows(6), order, contract_first, preferred_element_type=jnp.float32
    )
    for group in range(3):
        short_ref[:, group * width : (group + 1) * width] = (
            sums[group * 3 : group * 3 + 3, :] + sums[16 + group * 3 : 19 + group * 3, :]
        )


def add_x_kernel(*refs):
    out_ref = refs[7]
    total = refs[0][...] + refs[1][...] + refs[2][...] + refs[3][...]
    lanes = out_ref.shape[2]
    rows = jnp.concatenate([total[:, :lanes], total[:, lanes:]], 0)
    out_ref[...] = jnp.broadcast_to(rows.astype(jnp.bfloat16)[None], out_ref.shape)


def add_z_kernel(scale, in_ref, *refs):
    out_ref = refs[-1]
    total = jnp.sum(in_ref[...].astype(jnp.float32), axis=0) * scale
    out_ref[...] = jnp.broadcast_to(total.astype(jnp.bfloat16)[None], out_ref.shape)


def place_kernel(own_ref, other_ref, in_weight_ref, out_weight_ref):
    width, lanes = out_weight_ref.shape[0], own_ref.shape[2]
    core = lax.axis_index("core")
    order = channel_order(
        lambda zh, x, c, zl, y: ((c ^ core) * 4 + y) * 32 + (zh * 16 + x * 4 + zl)
    )
    contract_first = (((0,), (1,)), ((), ()))
    for kind in range(4):
        for half in range(2):
            stacked = jnp.concatenate(
                [
                    ref[kind * 4 + y, half * 32 : (half + 1) * 32, :]
                    for ref in (own_ref, other_ref)
                    for y in range(4)
                ],
                0,
            )
            if kind == 0:
                out_weight_ref[:, half * lanes : (half + 1) * lanes] = bf16_dot(order, stacked)
            else:
                in_weight_ref[
                    half * lanes : (half + 1) * lanes, (kind - 1) * width : kind * width
                ] = lax.dot_general(
                    stacked, order, contract_first, preferred_element_type=jnp.float32
                )


def call(kernel, out_shape, scratch=(), limit=vmem_limit, **options):
    return pl.pallas_call(
        kernel,
        out_shape=out_shape,
        scratch_shapes=list(scratch),
        compiler_params=pltpu.CompilerParams(vmem_limit_bytes=limit),
        **options,
    )


def specs(*spaces):
    return [pl.BlockSpec(memory_space=space) for space in spaces]


def exchange(x, axes):
    return lax.all_to_all(x, axes, split_axis=0, concat_axis=0, tiled=True)


def swap_core(x):
    return lax.ppermute(x, "core", [(0, 1), (1, 0)])


def ring(x, axis, distance):
    axes = ("x", "core") if axis == "x" else ("core", "y")
    route = []
    for core, turn in ((0, distance), (1, -distance)):
        for i in range(4):
            j = (i + turn) % 4
            pair = (i * 2 + core, j * 2 + core) if axis == "x" else (core * 4 + i, core * 4 + j)
            route.append(pair)
    return lax.ppermute(x, axes, route)


def per_device(inputs, in_weight, short_kernel, filter_one, filter_two, out_weight, out_grad):
    width = out_weight.shape[0]
    rows = inputs.shape[1]
    devices = lax.axis_size(everyone)
    scale = 1.0 / math.sqrt(devices * rows)
    shape = jax.ShapeDtypeStruct
    f32, bf16 = jnp.float32, jnp.bfloat16
    packed, both = call(
        pack_kernel,
        (shape((width, 2, 3 * rows), bf16), shape((rows, 2 * width), bf16)),
        [pltpu.VMEM((3, 2 * width, rows), f32)],
        limit=56 * 1024 * 1024,
    )(inputs, in_weight, filter_one, filter_two, out_weight, out_grad)
    received = exchange(packed, everyone)
    gathered = [both] + [ring(both, "y", distance) for distance in (1, 2, 3)]
    gathered += [swap_core(x) for x in gathered]
    tables = [jnp.asarray(t) for t in transform_tables(devices // 2, rows)]
    back = call(
        convolve_kernel,
        shape((32, 7, 8, rows), bf16),
        [pltpu.VMEM((3, 2 * devices, rows), f32)],
        in_specs=specs(*[pltpu.VMEM] * (2 + len(tables)), *[pl.ANY] * 2),
    )(received, short_kernel, *tables, gathered[1], gathered[3])
    halfway = exchange(back, ("zh", "x", "zl"))
    found = call(
        part_kernel,
        (shape((32, width), f32),) * 4 + (shape((2, 7 * 32, rows), bf16),) * 4,
        [pltpu.VMEM((32 * 7 * 8, rows), f32), pltpu.VMEM((4, 32, width), f32)],
    )(halfway, *gathered)
    part = [found[0]] + [ring(found[distance], "x", distance) for distance in (1, 2, 3)]
    far = ring(found[6], "y", 2)
    part, *leaving = call(
        add_x_kernel,
        (shape((8, 64, rows), bf16),) + (shape(found[5].shape, bf16),) * 2,
        in_specs=specs(*[pltpu.VMEM] * 4, *[pl.ANY] * 3),
        out_specs=specs(pltpu.VMEM, *[pl.ANY] * 2),
        input_output_aliases={5: 1, 6: 2},
    )(*part, far, found[5], found[7])
    arrived = [found[4], ring(leaving[0], "y", 1), far, ring(leaving[1], "y", 3)]
    part = exchange(part, ("zh", "zl"))
    part = call(
        functools.partial(add_z_kernel, scale),
        shape((16, 64, rows), bf16),
        in_specs=specs(pltpu.VMEM, *[pl.ANY] * 2),
    )(part, arrived[1], arrived[3])
    arrived += [swap_core(x) for x in arrived]
    part = exchange(part, ("x", "y"))
    outputs, grad_inputs, grad_short, grad_one, grad_two = call(
        finish_kernel,
        (
            shape((1, rows, width), bf16),
            shape((1, rows, width), bf16),
            shape((3, 3 * width), f32),
            shape((rows, width), f32),
            shape((rows, width), f32),
        ),
    )(*arrived, in_weight, out_weight)
    part, grad_short = lax.optimization_barrier((part, grad_short))
    grad_in_weight, grad_out_weight = call(
        place_kernel, (shape((width, 3 * width), f32), shape((width, width), f32))
    )(part, swap_core(part))
    return (
        outputs,
        grad_inputs,
        grad_in_weight,
        grad_short,
        grad_one,
        grad_two,
        grad_out_weight,
    )


def solution(mesh):
    mesh = Mesh(mesh.devices.reshape(2, 4, 2, 4, 4), everyone)
    positions = ("x", "core", "zl", "y")
    split_rows, split_filter = P("zh", positions, None), P(positions, None)
    return jax.shard_map(
        per_device,
        mesh=mesh,
        in_specs=(split_rows, P(), P(), split_filter, split_filter, P(), split_rows),
        out_specs=(split_rows, split_rows, P(), P(), split_filter, split_filter, P()),
        check_vma=False,
    )
```

```python
import functools
import math

import jax
import jax.numpy as jnp
import numpy as np
from jax import lax
from jax.experimental import pallas as pl
from jax.experimental.pallas import tpu as pltpu
from jax.sharding import Mesh
from jax.sharding import PartitionSpec as P

everyone = ("zh", "x", "core", "zl", "y")
vmem_limit = 16 * 1024 * 1024


def two_terms(table):
    high = table.astype(np.float32).astype(jnp.bfloat16)
    low = (table - high.astype(np.float64)).astype(np.float32).astype(jnp.bfloat16)
    return high, low


def left_table(table):
    high, low = two_terms(table)
    return np.concatenate([high, low, high], 1)


def right_table(table):
    high, low = two_terms(table)
    return np.concatenate([high, low, high], 0)


def transform_tables(blocks, rows):
    length = 2 * blocks * rows
    outer = np.arange(blocks) + 0.5
    step = 2.0 * math.pi * np.outer(outer, np.arange(blocks)) / (2 * blocks)
    turn = 2.0 * math.pi * np.outer(outer, np.arange(rows)) / length
    inner = 2.0 * math.pi * np.outer(np.arange(rows), np.arange(rows)) / rows
    first = np.concatenate([np.cos(step), -np.sin(step)], 0)
    c, s = np.cos(inner), np.sin(inner)
    second = np.block([[c, -s], [s, c]])
    second_back = np.block([[c, s], [-s, c]])
    first_back = np.concatenate([np.cos(step).T, -np.sin(step).T], 1) * (2.0 / length)
    return [
        left_table(first),
        right_table(second),
        right_table(second_back),
        left_table(first_back),
        np.cos(turn).astype(np.float32),
        np.sin(turn).astype(np.float32),
    ]


def bf16_dot(a, b):
    return jnp.dot(a, b, preferred_element_type=jnp.float32)


def split(x):
    high = x.astype(jnp.bfloat16)
    low = (x - high.astype(jnp.float32)).astype(jnp.bfloat16)
    return high, low


def table_left(table, x):
    x_high, x_low = split(x)
    return bf16_dot(table, jnp.concatenate([x_high, x_high, x_low], 0))


def table_right(x, table):
    x_high, x_low = split(x)
    return bf16_dot(jnp.concatenate([x_high, x_high, x_low], 1), table)


def pack_kernel(seq_ref, in_weight_ref, one_ref, two_ref, out_weight_ref, grad_ref, out_ref, both_ref, rows_ref):
    width = out_weight_ref.shape[0]
    lanes = rows_ref.shape[2]
    contract_first = (((0,), (1,)), ((), ()))
    contract_last = (((1,), (1,)), ((), ()))
    seq = seq_ref[0]

    def put(index, x):
        rows_ref[index // 2, pl.ds(index % 2, width, stride=2), :] = x

    for group in range(3):
        weight = in_weight_ref[:, group * width : (group + 1) * width]
        put(
            group,
            lax.dot_general(weight, seq, contract_first, preferred_element_type=jnp.float32),
        )
    put(
        3,
        lax.dot_general(
            out_weight_ref[...], grad_ref[0], contract_last, preferred_element_type=jnp.float32
        ),
    )
    chosen = jnp.where(lax.axis_index("zh") == 0, one_ref[...], two_ref[...]).T
    high = chosen.astype(jnp.bfloat16).astype(jnp.float32)
    put(4, high)
    put(5, chosen - high)
    both_ref[:, :width] = seq
    both_ref[:, width:] = grad_ref[0]
    for pair in range(3):
        out_ref[:, :, pair * lanes : (pair + 1) * lanes] = (
            rows_ref[pair].reshape(width, 2, lanes).astype(jnp.bfloat16)
        )


def convolve_kernel(
    in_ref,
    short_ref,
    first_ref,
    second_ref,
    second_back_ref,
    first_back_ref,
    turn_cos_ref,
    turn_sin_ref,
    *rest,
):
    out_ref, rows_ref = rest[-2:]
    sources, rows = in_ref.shape[0], in_ref.shape[2] // 3
    blocks = sources // 2
    width = short_ref.shape[1] // 3
    scale = 1.0 / math.sqrt(sources * rows)
    turn_cos = turn_cos_ref[...]
    turn_sin = turn_sin_ref[...]
    lane = lax.broadcasted_iota(jnp.int32, (blocks, rows), 1)
    block = lax.broadcasted_iota(jnp.int32, (blocks, rows), 0)

    for pair in range(3):
        rows_ref[pair] = (
            in_ref[:, :, pair * rows : (pair + 1) * rows]
            .astype(jnp.float32)
            .reshape(sources * 2, rows)
        )

    def row(member, index):
        return rows_ref[index // 2, pl.ds(member * sources + index % 2, blocks, stride=2), :]

    def later(x, distance):
        moved = pltpu.roll(x, distance, 1)
        carried = jnp.where(block == 0, 0.0, pltpu.roll(moved, 1, 0))
        return jnp.where(lane < distance, carried, moved)

    def earlier(x, distance):
        moved = pltpu.roll(x, rows - distance, 1)
        carried = jnp.where(block == blocks - 1, 0.0, pltpu.roll(moved, blocks - 1, 0))
        return jnp.where(lane >= rows - distance, carried, moved)

    def forward(signals):
        outer = table_left(first_ref[...], jnp.concatenate(signals, 1))
        turned = []
        for i in range(len(signals)):
            re = outer[:blocks, i * rows : (i + 1) * rows]
            im = outer[blocks:, i * rows : (i + 1) * rows]
            turned.append(
                jnp.concatenate(
                    [re * turn_cos + im * turn_sin, im * turn_cos - re * turn_sin], 1
                )
            )
        inner = table_right(jnp.concatenate(turned, 0), second_ref[...])
        return [
            (inner[i * blocks : (i + 1) * blocks, :rows], inner[i * blocks : (i + 1) * blocks, rows:])
            for i in range(len(signals))
        ]

    def backward(spectra):
        stacked = jnp.concatenate([jnp.concatenate(pair, 1) for pair in spectra], 0)
        inner = table_right(stacked, second_back_ref[...])
        turned = []
        for i in range(len(spectra)):
            re = inner[i * blocks : (i + 1) * blocks, :rows]
            im = inner[i * blocks : (i + 1) * blocks, rows:]
            turned.append(
                jnp.concatenate(
                    [re * turn_cos - im * turn_sin, im * turn_cos + re * turn_sin], 0
                )
            )
        outer = table_left(first_back_ref[...], jnp.concatenate(turned, 1))
        return [outer[:, i * rows : (i + 1) * rows] for i in range(len(spectra))]

    def times(a, b):
        return a[0] * b[0] - a[1] * b[1], a[0] * b[1] + a[1] * b[0]

    def conj_times(a, b):
        return a[0] * b[0] + a[1] * b[1], a[0] * b[1] - a[1] * b[0]

    def added(a, b):
        return a[0] + b[0], a[1] + b[1]

    mesh_place = lax.axis_index(everyone)
    short = short_ref[...]
    short_lane = lax.broadcasted_iota(jnp.int32, short.shape, 1)
    taps = []
    for group in range(3):
        column = jnp.sum(
            jnp.where(short_lane == mesh_place + group * width, short, 0.0), axis=1, keepdims=True
        )
        taps.append([column[tap : tap + 1, :] for tap in range(3)])

    projected, lagged_one, lagged_two, mixed, pre = [], [], [], [], []
    for member in range(2):
        now = [row(member, group) for group in range(3)]
        one = [later(x, 1) for x in now]
        two = [later(x, 2) for x in now]
        projected.append(now)
        lagged_one.append(one)
        lagged_two.append(two)
        mixed.append(
            [
                taps[g][0] * now[g] + taps[g][1] * one[g] + taps[g][2] * two[g]
                for g in range(3)
            ]
        )
        pre.append(row(member, 3))
    members = range(2)
    grad_conv_two = [pre[m] * mixed[m][2] for m in members]
    spectra = forward(
        [row(m, 4) + row(m, 5) for m in members] + [mixed[m][0] for m in members] + grad_conv_two
    )
    one_spec, two_spec = spectra[0], spectra[1]
    value_spec, conv_two_spec = spectra[2:4], spectra[4:6]
    found = backward(
        [times(one_spec, value_spec[m]) for m in members]
        + [conj_times(two_spec, conv_two_spec[m]) for m in members]
    )
    conv_one, grad_gated = found[:2], found[2:]
    spectra = forward(
        [mixed[m][1] * conv_one[m] for m in members]
        + [mixed[m][1] * grad_gated[m] for m in members]
    )
    gated_spec, conv_one_spec = spectra[:2], spectra[2:]
    found = backward(
        [times(two_spec, gated_spec[m]) for m in members]
        + [conj_times(one_spec, conv_one_spec[m]) for m in members]
        + [
            added(*[conj_times(value_spec[m], conv_one_spec[m]) for m in members]),
            added(*[conj_times(gated_spec[m], conv_two_spec[m]) for m in members]),
        ]
    )
    conv_two, grad_value = found[:2], found[2:4]
    grad_filters = [found[4] * scale, found[5] * scale]

    new = lax.broadcasted_iota(jnp.int32, (blocks, blocks), 0)
    old = lax.broadcasted_iota(jnp.int32, (blocks, blocks), 1)
    wanted = (new & 99) | (((new >> 2) & 1) << 4) | (((new >> 3) & 3) << 2)
    reorder = jnp.where(old == wanted, 1.0, 0.0).astype(jnp.bfloat16)
    sums = [[0.0] * 3 for _ in range(3)]
    for m in members:
        sent = [mixed[m][2] * conv_two[m]]
        grads = [grad_value[m], grad_gated[m] * conv_one[m], pre[m] * conv_two[m]]
        for g in range(3):
            sent.append(
                taps[g][0] * grads[g]
                + taps[g][1] * earlier(grads[g], 1)
                + taps[g][2] * earlier(grads[g], 2)
            )
            for tap, lagged in enumerate((projected, lagged_one, lagged_two)):
                sums[g][tap] = sums[g][tap] + jnp.sum(
                    jnp.sum(grads[g] * lagged[m][g], axis=0, keepdims=True), axis=1, keepdims=True
                )
        sent.extend(grad_filters)
        turned = bf16_dot(reorder, jnp.concatenate(sent, 1).astype(jnp.bfloat16))
        half = out_ref.shape[0] // 2
        for index in range(len(sent)):
            out_ref[m * half : (m + 1) * half, index] = (
                turned[:, index * rows : (index + 1) * rows]
                .reshape(half, blocks // half, rows)
                .astype(jnp.bfloat16)
            )
    shape = (blocks // half, rows)
    sum_lane = lax.broadcasted_iota(jnp.int32, shape, 1)
    line = jnp.zeros(shape, jnp.float32)
    for g in range(3):
        for tap in range(3):
            total = sums[g][tap] * scale
            high = total.astype(jnp.bfloat16).astype(jnp.float32)
            line = jnp.where(sum_lane == g * 3 + tap, high, line)
            line = jnp.where(sum_lane == 16 + g * 3 + tap, total - high, line)
    out_ref[:, 6] = jnp.broadcast_to(line[None], (2 * half,) + shape).astype(jnp.bfloat16)


def channel_order(place_of):
    channel = lax.broadcasted_iota(jnp.int32, (256, 256), 0)
    row = lax.broadcasted_iota(jnp.int32, (256, 256), 1)
    zh, x, core = channel >> 7, (channel >> 5) & 3, (channel >> 4) & 1
    zl, y = (channel >> 2) & 3, channel & 3
    return jnp.where(row == place_of(zh, x, core, zl, y), 1.0, 0.0).astype(jnp.bfloat16)


def part_kernel(in_ref, *refs):
    both_refs, part_ref, send_refs = refs[:8], refs[8], refs[9:13]
    rows_ref, sums_ref = refs[13:]
    sources, kinds, blocks, rows = in_ref.shape
    width = both_refs[0].shape[1] // 2
    core, y = lax.axis_index("core"), lax.axis_index("y")
    turn = 1 - 2 * core
    rows_ref[...] = in_ref[...].astype(jnp.float32).reshape(sources * kinds * blocks, rows)
    out_part = jnp.zeros((sources, width), jnp.float32)
    in_part = jnp.zeros((3 * sources, width), jnp.float32)
    for other in range(2):
        for ahead in range(4):
            block = (core ^ other) * 4 + ((y + turn * ahead) & 3)
            kept = jnp.concatenate(
                [
                    rows_ref[pl.ds(kind * blocks + block, sources, stride=kinds * blocks), :]
                    for kind in range(kinds)
                ],
                0,
            ).astype(jnp.bfloat16)
            send_refs[ahead][other] = kept
            both_ref = both_refs[4 + ahead if other else (4 - ahead) % 4]
            out_part += bf16_dot(kept[:sources], both_ref[:, width:])
            in_part += bf16_dot(kept[sources : 4 * sources], both_ref[:, :width])
    lanes = sums_ref.shape[1]
    for kind in range(4):
        part = out_part if kind == 0 else in_part[(kind - 1) * sources : kind * sources]
        for half in range(2):
            sums_ref[pl.ds(kind * 2 + half, sources, stride=8), :] = part[
                :, half * lanes : (half + 1) * lanes
            ]
    part_ref[...] = sums_ref[...].reshape(part_ref.shape).astype(jnp.bfloat16)


def finish_kernel(*refs):
    held = refs[:8]
    in_weight_ref, out_weight_ref, outputs_ref, grad_inputs_ref, short_ref = refs[8:13]
    one_ref, two_ref = refs[13:]
    width = out_weight_ref.shape[0]
    count = width // 8
    core, y = lax.axis_index("core"), lax.axis_index("y")
    turn = 1 - 2 * core

    def row_of(zh, x, c, zl, v):
        other = c ^ core
        step = (turn * (1 - 2 * other) * (y - v)) & 3
        return (other * 4 + step) * 32 + (zh * 16 + x * 4 + zl)

    order = channel_order(row_of)
    contract_first = (((0,), (1,)), ((), ()))
    contract_last = (((1,), (1,)), ((), ()))

    def stacked_rows(kind):
        return jnp.concatenate(
            [held[i][i // 4, kind * count : (kind + 1) * count, :] for i in range(8)], 0
        )

    def natural(kind):
        stacked = stacked_rows(kind)
        return lax.dot_general(
            stacked, order, contract_first, preferred_element_type=jnp.float32
        )

    outputs_ref[0] = bf16_dot(natural(0).astype(jnp.bfloat16), out_weight_ref[...]).astype(
        jnp.bfloat16
    )
    total = None
    for group in range(3):
        term = lax.dot_general(
            natural(1 + group).astype(jnp.bfloat16),
            in_weight_ref[:, group * width : (group + 1) * width],
            contract_last,
            preferred_element_type=jnp.float32,
        )
        total = term if total is None else total + term
    grad_inputs_ref[0] = total.astype(jnp.bfloat16)
    one_ref[...] = natural(4)
    two_ref[...] = natural(5)
    sums = lax.dot_general(
        stacked_rows(6), order, contract_first, preferred_element_type=jnp.float32
    )
    for group in range(3):
        short_ref[:, group * width : (group + 1) * width] = (
            sums[group * 3 : group * 3 + 3, :] + sums[16 + group * 3 : 19 + group * 3, :]
        )


def add_kernel(scale, in_ref, *refs):
    out_ref = refs[3]
    total = jnp.sum(in_ref[...].astype(jnp.float32), axis=0) * scale
    out_ref[...] = jnp.broadcast_to(total.astype(jnp.bfloat16)[None], out_ref.shape)


def place_kernel(own_ref, other_ref, in_weight_ref, out_weight_ref, rows_ref):
    width, lanes = out_weight_ref.shape[0], own_ref.shape[2]
    chips, slots = own_ref.shape[0], own_ref.shape[1]
    core = lax.axis_index("core")
    order = channel_order(
        lambda zh, x, c, zl, y: (c ^ core) * 128 + (zh * 4 + x) * 16 + zl * 4 + y
    )
    contract_first = (((0,), (1,)), ((), ()))
    for other, ref in enumerate((own_ref, other_ref)):
        rows_ref[other] = ref[...].astype(jnp.float32).reshape(chips * slots, lanes)
    for kind in range(4):
        for half in range(2):
            stacked = jnp.concatenate(
                [
                    rows_ref[other, pl.ds(kind * 2 + half, chips, stride=slots), :]
                    for other in range(2)
                ],
                0,
            ).astype(jnp.bfloat16)
            if kind == 0:
                out_weight_ref[:, half * lanes : (half + 1) * lanes] = bf16_dot(order, stacked)
            else:
                in_weight_ref[
                    half * lanes : (half + 1) * lanes, (kind - 1) * width : kind * width
                ] = lax.dot_general(
                    stacked, order, contract_first, preferred_element_type=jnp.float32
                )


def call(kernel, out_shape, scratch=(), limit=vmem_limit, **options):
    return pl.pallas_call(
        kernel,
        out_shape=out_shape,
        scratch_shapes=list(scratch),
        compiler_params=pltpu.CompilerParams(vmem_limit_bytes=limit),
        **options,
    )


def specs(*spaces):
    return [pl.BlockSpec(memory_space=space) for space in spaces]


def exchange(x, axes):
    return lax.all_to_all(x, axes, split_axis=0, concat_axis=0, tiled=True)


def swap_core(x):
    return lax.ppermute(x, "core", [(0, 1), (1, 0)])


def ring(x, distance):
    route = [(i, (i + distance) % 4) for i in range(4)]
    route += [(4 + i, 4 + (i - distance) % 4) for i in range(4)]
    return lax.ppermute(x, ("core", "y"), route)


def per_device(inputs, in_weight, short_kernel, filter_one, filter_two, out_weight, out_grad):
    width = out_weight.shape[0]
    rows = inputs.shape[1]
    devices = lax.axis_size(everyone)
    scale = 1.0 / math.sqrt(devices * rows)
    shape = jax.ShapeDtypeStruct
    f32, bf16 = jnp.float32, jnp.bfloat16
    packed, both = call(
        pack_kernel,
        (shape((width, 2, 3 * rows), bf16), shape((rows, 2 * width), bf16)),
        [pltpu.VMEM((3, 2 * width, rows), f32)],
        limit=56 * 1024 * 1024,
    )(inputs, in_weight, filter_one, filter_two, out_weight, out_grad)
    received = exchange(packed, everyone)
    gathered = [both] + [ring(both, distance) for distance in (1, 2, 3)]
    gathered += [swap_core(x) for x in gathered]
    tables = [jnp.asarray(t) for t in transform_tables(devices // 2, rows)]
    back = call(
        convolve_kernel,
        shape((32, 7, 8, rows), bf16),
        [pltpu.VMEM((3, 2 * devices, rows), f32)],
        in_specs=specs(*[pltpu.VMEM] * (2 + len(tables)), *[pl.ANY] * 2),
    )(received, short_kernel, *tables, gathered[1], gathered[3])
    halfway = exchange(back, ("zh", "x", "zl"))
    part, *leaving = call(
        part_kernel,
        (shape((32, 8, rows), bf16),) + (shape((2, 7 * 32, rows), bf16),) * 4,
        [pltpu.VMEM((32 * 7 * 8, rows), f32), pltpu.VMEM((32 * 8, rows), f32)],
    )(halfway, *gathered)
    part = exchange(part, ("zh", "x", "zl"))
    part, *leaving[1:] = call(
        functools.partial(add_kernel, scale),
        (shape((devices // 2, 8, rows), bf16),) + (shape(leaving[0].shape, bf16),) * 3,
        in_specs=specs(pltpu.VMEM, *[pl.ANY] * 3),
        out_specs=specs(pltpu.VMEM, *[pl.ANY] * 3),
        input_output_aliases={1: 1, 2: 2, 3: 3},
    )(part, *leaving[1:])
    arrived = [leaving[0]] + [ring(leaving[i], i) for i in (1, 2, 3)]
    arrived += [swap_core(x) for x in arrived]
    part = exchange(part, ("zh", "x", "zl", "y"))
    outputs, grad_inputs, grad_short, grad_one, grad_two = call(
        finish_kernel,
        (
            shape((1, rows, width), bf16),
            shape((1, rows, width), bf16),
            shape((3, 3 * width), f32),
            shape((rows, width), f32),
            shape((rows, width), f32),
        ),
    )(*arrived, in_weight, out_weight)
    part, grad_short = lax.optimization_barrier((part, grad_short))
    grad_in_weight, grad_out_weight = call(
        place_kernel,
        (shape((width, 3 * width), f32), shape((width, width), f32)),
        [pltpu.VMEM((2, devices * 4, rows), f32)],
    )(part, swap_core(part))
    return (
        outputs,
        grad_inputs,
        grad_in_weight,
        grad_short,
        grad_one,
        grad_two,
        grad_out_weight,
    )


def solution(mesh):
    mesh = Mesh(mesh.devices.reshape(2, 4, 2, 4, 4), everyone)
    positions = ("x", "core", "zl", "y")
    split_rows, split_filter = P("zh", positions, None), P(positions, None)
    return jax.shard_map(
        per_device,
        mesh=mesh,
        in_specs=(split_rows, P(), P(), split_filter, split_filter, P(), split_rows),
        out_specs=(split_rows, split_rows, P(), P(), split_filter, split_filter, P()),
        check_vma=False,
    )
```

```python
import functools
import math

import jax
import jax.numpy as jnp
import numpy as np
from jax import lax
from jax.experimental import pallas as pl
from jax.experimental.pallas import tpu as pltpu
from jax.sharding import Mesh
from jax.sharding import PartitionSpec as P

everyone = ("zh", "x", "core", "zl", "y")
vmem_limit = 16 * 1024 * 1024


def two_terms(table):
    high = table.astype(np.float32).astype(jnp.bfloat16)
    low = (table - high.astype(np.float64)).astype(np.float32).astype(jnp.bfloat16)
    return high, low


def left_table(table):
    high, low = two_terms(table)
    return np.concatenate([high, low, high], 1)


def right_table(table):
    high, low = two_terms(table)
    return np.concatenate([high, low, high], 0)


def transform_tables(blocks, rows):
    length = 2 * blocks * rows
    outer = np.arange(blocks) + 0.5
    step = 2.0 * math.pi * np.outer(outer, np.arange(blocks)) / (2 * blocks)
    turn = 2.0 * math.pi * np.outer(outer, np.arange(rows)) / length
    inner = 2.0 * math.pi * np.outer(np.arange(rows), np.arange(rows)) / rows
    first = np.concatenate([np.cos(step), -np.sin(step)], 0)
    c, s = np.cos(inner), np.sin(inner)
    second = np.block([[c, -s], [s, c]])
    second_back = np.block([[c, s], [-s, c]])
    first_back = np.concatenate([np.cos(step).T, -np.sin(step).T], 1) * (2.0 / length)
    return [
        left_table(first),
        right_table(second),
        right_table(second_back),
        left_table(first_back),
        np.cos(turn).astype(np.float32),
        np.sin(turn).astype(np.float32),
    ]


def bf16_dot(a, b):
    return jnp.dot(a, b, preferred_element_type=jnp.float32)


def split(x):
    high = x.astype(jnp.bfloat16)
    low = (x - high.astype(jnp.float32)).astype(jnp.bfloat16)
    return high, low


def table_left(table, x):
    x_high, x_low = split(x)
    return bf16_dot(table, jnp.concatenate([x_high, x_high, x_low], 0))


def table_right(x, table):
    x_high, x_low = split(x)
    return bf16_dot(jnp.concatenate([x_high, x_high, x_low], 1), table)


def pack_kernel(seq_ref, in_weight_ref, one_ref, two_ref, out_weight_ref, grad_ref, out_ref, both_ref, rows_ref):
    width = out_weight_ref.shape[0]
    lanes = rows_ref.shape[2]
    contract_first = (((0,), (1,)), ((), ()))
    contract_last = (((1,), (1,)), ((), ()))
    seq = seq_ref[0]

    def put(index, x):
        rows_ref[index // 2, pl.ds(index % 2, width, stride=2), :] = x

    for group in range(3):
        weight = in_weight_ref[:, group * width : (group + 1) * width]
        put(
            group,
            lax.dot_general(weight, seq, contract_first, preferred_element_type=jnp.float32),
        )
    put(
        3,
        lax.dot_general(
            out_weight_ref[...], grad_ref[0], contract_last, preferred_element_type=jnp.float32
        ),
    )
    chosen = jnp.where(lax.axis_index("zh") == 0, one_ref[...], two_ref[...]).T
    high = chosen.astype(jnp.bfloat16).astype(jnp.float32)
    put(4, high)
    put(5, chosen - high)
    both_ref[:, :width] = seq
    both_ref[:, width:] = grad_ref[0]
    for pair in range(3):
        out_ref[:, :, pair * lanes : (pair + 1) * lanes] = (
            rows_ref[pair].reshape(width, 2, lanes).astype(jnp.bfloat16)
        )


def convolve_kernel(
    in_ref,
    short_ref,
    first_ref,
    second_ref,
    second_back_ref,
    first_back_ref,
    turn_cos_ref,
    turn_sin_ref,
    *rest,
):
    out_ref, rows_ref = rest[-2:]
    sources, rows = in_ref.shape[0], in_ref.shape[2] // 3
    blocks = sources // 2
    width = short_ref.shape[1] // 3
    scale = 1.0 / math.sqrt(sources * rows)
    turn_cos = turn_cos_ref[...]
    turn_sin = turn_sin_ref[...]
    lane = lax.broadcasted_iota(jnp.int32, (blocks, rows), 1)
    block = lax.broadcasted_iota(jnp.int32, (blocks, rows), 0)

    for pair in range(3):
        rows_ref[pair] = (
            in_ref[:, :, pair * rows : (pair + 1) * rows]
            .astype(jnp.float32)
            .reshape(sources * 2, rows)
        )

    def row(member, index):
        return rows_ref[index // 2, pl.ds(member * sources + index % 2, blocks, stride=2), :]

    def later(x, distance):
        moved = pltpu.roll(x, distance, 1)
        carried = jnp.where(block == 0, 0.0, pltpu.roll(moved, 1, 0))
        return jnp.where(lane < distance, carried, moved)

    def earlier(x, distance):
        moved = pltpu.roll(x, rows - distance, 1)
        carried = jnp.where(block == blocks - 1, 0.0, pltpu.roll(moved, blocks - 1, 0))
        return jnp.where(lane >= rows - distance, carried, moved)

    def forward(signals):
        outer = table_left(first_ref[...], jnp.concatenate(signals, 1))
        turned = []
        for i in range(len(signals)):
            re = outer[:blocks, i * rows : (i + 1) * rows]
            im = outer[blocks:, i * rows : (i + 1) * rows]
            turned.append(
                jnp.concatenate(
                    [re * turn_cos + im * turn_sin, im * turn_cos - re * turn_sin], 1
                )
            )
        inner = table_right(jnp.concatenate(turned, 0), second_ref[...])
        return [
            (inner[i * blocks : (i + 1) * blocks, :rows], inner[i * blocks : (i + 1) * blocks, rows:])
            for i in range(len(signals))
        ]

    def backward(spectra):
        stacked = jnp.concatenate([jnp.concatenate(pair, 1) for pair in spectra], 0)
        inner = table_right(stacked, second_back_ref[...])
        turned = []
        for i in range(len(spectra)):
            re = inner[i * blocks : (i + 1) * blocks, :rows]
            im = inner[i * blocks : (i + 1) * blocks, rows:]
            turned.append(
                jnp.concatenate(
                    [re * turn_cos - im * turn_sin, im * turn_cos + re * turn_sin], 0
                )
            )
        outer = table_left(first_back_ref[...], jnp.concatenate(turned, 1))
        return [outer[:, i * rows : (i + 1) * rows] for i in range(len(spectra))]

    def times(a, b):
        return a[0] * b[0] - a[1] * b[1], a[0] * b[1] + a[1] * b[0]

    def conj_times(a, b):
        return a[0] * b[0] + a[1] * b[1], a[0] * b[1] - a[1] * b[0]

    def added(a, b):
        return a[0] + b[0], a[1] + b[1]

    mesh_place = lax.axis_index(everyone)
    short = short_ref[...]
    short_lane = lax.broadcasted_iota(jnp.int32, short.shape, 1)
    taps = []
    for group in range(3):
        column = jnp.sum(
            jnp.where(short_lane == mesh_place + group * width, short, 0.0), axis=1, keepdims=True
        )
        taps.append([column[tap : tap + 1, :] for tap in range(3)])

    projected, lagged_one, lagged_two, mixed, pre = [], [], [], [], []
    for member in range(2):
        now = [row(member, group) for group in range(3)]
        one = [later(x, 1) for x in now]
        two = [later(x, 2) for x in now]
        projected.append(now)
        lagged_one.append(one)
        lagged_two.append(two)
        mixed.append(
            [
                taps[g][0] * now[g] + taps[g][1] * one[g] + taps[g][2] * two[g]
                for g in range(3)
            ]
        )
        pre.append(row(member, 3))
    members = range(2)
    grad_conv_two = [pre[m] * mixed[m][2] for m in members]
    spectra = forward(
        [row(m, 4) + row(m, 5) for m in members] + [mixed[m][0] for m in members] + grad_conv_two
    )
    one_spec, two_spec = spectra[0], spectra[1]
    value_spec, conv_two_spec = spectra[2:4], spectra[4:6]
    found = backward(
        [times(one_spec, value_spec[m]) for m in members]
        + [conj_times(two_spec, conv_two_spec[m]) for m in members]
    )
    conv_one, grad_gated = found[:2], found[2:]
    spectra = forward(
        [mixed[m][1] * conv_one[m] for m in members]
        + [mixed[m][1] * grad_gated[m] for m in members]
    )
    gated_spec, conv_one_spec = spectra[:2], spectra[2:]
    found = backward(
        [times(two_spec, gated_spec[m]) for m in members]
        + [conj_times(one_spec, conv_one_spec[m]) for m in members]
        + [
            added(*[conj_times(value_spec[m], conv_one_spec[m]) for m in members]),
            added(*[conj_times(gated_spec[m], conv_two_spec[m]) for m in members]),
        ]
    )
    conv_two, grad_value = found[:2], found[2:4]
    grad_filters = [found[4] * scale, found[5] * scale]

    new = lax.broadcasted_iota(jnp.int32, (blocks, blocks), 0)
    old = lax.broadcasted_iota(jnp.int32, (blocks, blocks), 1)
    wanted = (new & 99) | (((new >> 2) & 1) << 4) | (((new >> 3) & 3) << 2)
    reorder = jnp.where(old == wanted, 1.0, 0.0).astype(jnp.bfloat16)
    sums = [[0.0] * 3 for _ in range(3)]
    for m in members:
        sent = [mixed[m][2] * conv_two[m]]
        grads = [grad_value[m], grad_gated[m] * conv_one[m], pre[m] * conv_two[m]]
        for g in range(3):
            sent.append(
                taps[g][0] * grads[g]
                + taps[g][1] * earlier(grads[g], 1)
                + taps[g][2] * earlier(grads[g], 2)
            )
            for tap, lagged in enumerate((projected, lagged_one, lagged_two)):
                sums[g][tap] = sums[g][tap] + jnp.sum(
                    jnp.sum(grads[g] * lagged[m][g], axis=0, keepdims=True), axis=1, keepdims=True
                )
        sent.extend(grad_filters)
        turned = bf16_dot(reorder, jnp.concatenate(sent, 1).astype(jnp.bfloat16))
        half = out_ref.shape[0] // 2
        for index in range(len(sent)):
            out_ref[m * half : (m + 1) * half, index] = (
                turned[:, index * rows : (index + 1) * rows]
                .reshape(half, blocks // half, rows)
                .astype(jnp.bfloat16)
            )
    shape = (blocks // half, rows)
    sum_lane = lax.broadcasted_iota(jnp.int32, shape, 1)
    line = jnp.zeros(shape, jnp.float32)
    for g in range(3):
        for tap in range(3):
            total = sums[g][tap] * scale
            high = total.astype(jnp.bfloat16).astype(jnp.float32)
            line = jnp.where(sum_lane == g * 3 + tap, high, line)
            line = jnp.where(sum_lane == 16 + g * 3 + tap, total - high, line)
    out_ref[:, 6] = jnp.broadcast_to(line[None], (2 * half,) + shape).astype(jnp.bfloat16)


def channel_order(place_of):
    channel = lax.broadcasted_iota(jnp.int32, (256, 256), 0)
    row = lax.broadcasted_iota(jnp.int32, (256, 256), 1)
    zh, x, core = channel >> 7, (channel >> 5) & 3, (channel >> 4) & 1
    zl, y = (channel >> 2) & 3, channel & 3
    return jnp.where(row == place_of(zh, x, core, zl, y), 1.0, 0.0).astype(jnp.bfloat16)


def part_kernel(in_ref, *refs):
    both_refs, part_ref, send_refs = refs[:8], refs[8], refs[9:13]
    rows_ref, sums_ref = refs[13:]
    sources, kinds, blocks, rows = in_ref.shape
    width = both_refs[0].shape[1] // 2
    core, y = lax.axis_index("core"), lax.axis_index("y")
    turn = 1 - 2 * core
    rows_ref[...] = in_ref[...].astype(jnp.float32).reshape(sources * kinds * blocks, rows)
    out_part = jnp.zeros((sources, width), jnp.float32)
    in_part = jnp.zeros((3 * sources, width), jnp.float32)
    for other in range(2):
        for ahead in range(4):
            block = (core ^ other) * 4 + ((y + turn * ahead) & 3)
            kept = jnp.concatenate(
                [
                    rows_ref[pl.ds(kind * blocks + block, sources, stride=kinds * blocks), :]
                    for kind in range(kinds)
                ],
                0,
            ).astype(jnp.bfloat16)
            send_refs[ahead][other] = kept
            both_ref = both_refs[4 + ahead if other else (4 - ahead) % 4]
            out_part += bf16_dot(kept[:sources], both_ref[:, width:])
            in_part += bf16_dot(kept[sources : 4 * sources], both_ref[:, :width])
    lanes = sums_ref.shape[1]
    for kind in range(4):
        part = out_part if kind == 0 else in_part[(kind - 1) * sources : kind * sources]
        for half in range(2):
            sums_ref[pl.ds(kind * 2 + half, sources, stride=8), :] = part[
                :, half * lanes : (half + 1) * lanes
            ]
    part_ref[...] = sums_ref[...].reshape(part_ref.shape).astype(jnp.bfloat16)


def finish_kernel(*refs):
    held = refs[:8]
    in_weight_ref, out_weight_ref, outputs_ref, grad_inputs_ref, short_ref = refs[8:13]
    one_ref, two_ref = refs[13:]
    width = out_weight_ref.shape[0]
    count = width // 8
    core, y = lax.axis_index("core"), lax.axis_index("y")
    turn = 1 - 2 * core

    def row_of(zh, x, c, zl, v):
        other = c ^ core
        step = (turn * (1 - 2 * other) * (y - v)) & 3
        return (other * 4 + step) * 32 + (zh * 16 + x * 4 + zl)

    order = channel_order(row_of)
    contract_first = (((0,), (1,)), ((), ()))
    contract_last = (((1,), (1,)), ((), ()))

    def stacked_rows(kind):
        return jnp.concatenate(
            [held[i][i // 4, kind * count : (kind + 1) * count, :] for i in range(8)], 0
        )

    def natural(kind):
        stacked = stacked_rows(kind)
        return lax.dot_general(
            stacked, order, contract_first, preferred_element_type=jnp.float32
        )

    outputs_ref[0] = bf16_dot(natural(0).astype(jnp.bfloat16), out_weight_ref[...]).astype(
        jnp.bfloat16
    )
    total = None
    for group in range(3):
        term = lax.dot_general(
            natural(1 + group).astype(jnp.bfloat16),
            in_weight_ref[:, group * width : (group + 1) * width],
            contract_last,
            preferred_element_type=jnp.float32,
        )
        total = term if total is None else total + term
    grad_inputs_ref[0] = total.astype(jnp.bfloat16)
    one_ref[...] = natural(4)
    two_ref[...] = natural(5)
    sums = lax.dot_general(
        stacked_rows(6), order, contract_first, preferred_element_type=jnp.float32
    )
    for group in range(3):
        short_ref[:, group * width : (group + 1) * width] = (
            sums[group * 3 : group * 3 + 3, :] + sums[16 + group * 3 : 19 + group * 3, :]
        )


def add_kernel(scale, in_ref, *refs):
    out_ref = refs[3]
    total = jnp.sum(in_ref[...].astype(jnp.float32), axis=0) * scale
    out_ref[...] = jnp.broadcast_to(total.astype(jnp.bfloat16)[None], out_ref.shape)


def place_kernel(own_ref, other_ref, in_weight_ref, out_weight_ref, rows_ref):
    width, lanes = out_weight_ref.shape[0], own_ref.shape[2]
    chips, slots = own_ref.shape[0], own_ref.shape[1]
    core = lax.axis_index("core")
    order = channel_order(
        lambda zh, x, c, zl, y: (c ^ core) * 128 + (zh * 4 + x) * 16 + zl * 4 + y
    )
    contract_first = (((0,), (1,)), ((), ()))
    for other, ref in enumerate((own_ref, other_ref)):
        rows_ref[other] = ref[...].astype(jnp.float32).reshape(chips * slots, lanes)
    for kind in range(4):
        for half in range(2):
            stacked = jnp.concatenate(
                [
                    rows_ref[other, pl.ds(kind * 2 + half, chips, stride=slots), :]
                    for other in range(2)
                ],
                0,
            ).astype(jnp.bfloat16)
            if kind == 0:
                out_weight_ref[:, half * lanes : (half + 1) * lanes] = bf16_dot(order, stacked)
            else:
                in_weight_ref[
                    half * lanes : (half + 1) * lanes, (kind - 1) * width : kind * width
                ] = lax.dot_general(
                    stacked, order, contract_first, preferred_element_type=jnp.float32
                )


def call(kernel, out_shape, scratch=(), limit=vmem_limit, **options):
    return pl.pallas_call(
        kernel,
        out_shape=out_shape,
        scratch_shapes=list(scratch),
        compiler_params=pltpu.CompilerParams(vmem_limit_bytes=limit),
        **options,
    )


def specs(*spaces):
    return [pl.BlockSpec(memory_space=space) for space in spaces]


def exchange(x, axes):
    return lax.all_to_all(x, axes, split_axis=0, concat_axis=0, tiled=True)


def swap_core(x):
    return lax.ppermute(x, "core", [(0, 1), (1, 0)])


def ring(x, distance):
    route = [(i, (i + distance) % 4) for i in range(4)]
    route += [(4 + i, 4 + (i - distance) % 4) for i in range(4)]
    return lax.ppermute(x, ("core", "y"), route)


def per_device(inputs, in_weight, short_kernel, filter_one, filter_two, out_weight, out_grad):
    width = out_weight.shape[0]
    rows = inputs.shape[1]
    devices = lax.axis_size(everyone)
    scale = 1.0 / math.sqrt(devices * rows)
    shape = jax.ShapeDtypeStruct
    f32, bf16 = jnp.float32, jnp.bfloat16
    packed, both = call(
        pack_kernel,
        (shape((width, 2, 3 * rows), bf16), shape((rows, 2 * width), bf16)),
        [pltpu.VMEM((3, 2 * width, rows), f32)],
        limit=56 * 1024 * 1024,
    )(inputs, in_weight, filter_one, filter_two, out_weight, out_grad)
    received = exchange(packed, everyone)
    gathered = [both] + [ring(both, distance) for distance in (1, 2, 3)]
    gathered += [swap_core(x) for x in gathered]
    tables = [jnp.asarray(t) for t in transform_tables(devices // 2, rows)]
    back = call(
        convolve_kernel,
        shape((32, 7, 8, rows), bf16),
        [pltpu.VMEM((3, 2 * devices, rows), f32)],
        in_specs=specs(*[pltpu.VMEM] * (2 + len(tables)), *[pl.ANY] * 2),
    )(received, short_kernel, *tables, gathered[1], gathered[3])
    halfway = exchange(back, ("zh", "x", "zl"))
    part, *leaving = call(
        part_kernel,
        (shape((32, 8, rows), bf16),) + (shape((2, 7 * 32, rows), bf16),) * 4,
        [pltpu.VMEM((32 * 7 * 8, rows), f32), pltpu.VMEM((32 * 8, rows), f32)],
    )(halfway, *gathered)
    part = exchange(part, ("zh", "x", "zl"))
    near = [ring(leaving[1], 1), ring(leaving[3], 3)]
    part, far = call(
        functools.partial(add_kernel, scale),
        (shape((devices // 2, 8, rows), bf16), shape(leaving[2].shape, bf16)),
        in_specs=specs(pltpu.VMEM, *[pl.ANY] * 3),
        out_specs=specs(pltpu.VMEM, pl.ANY),
        input_output_aliases={3: 1},
    )(part, *near, leaving[2])
    arrived = [leaving[0], near[0], ring(far, 2), near[1]]
    arrived += [swap_core(x) for x in arrived]
    part = exchange(part, ("zh", "x", "zl", "y"))
    outputs, grad_inputs, grad_short, grad_one, grad_two = call(
        finish_kernel,
        (
            shape((1, rows, width), bf16),
            shape((1, rows, width), bf16),
            shape((3, 3 * width), f32),
            shape((rows, width), f32),
            shape((rows, width), f32),
        ),
    )(*arrived, in_weight, out_weight)
    part, grad_short = lax.optimization_barrier((part, grad_short))
    grad_in_weight, grad_out_weight = call(
        place_kernel,
        (shape((width, 3 * width), f32), shape((width, width), f32)),
        [pltpu.VMEM((2, devices * 4, rows), f32)],
    )(part, swap_core(part))
    return (
        outputs,
        grad_inputs,
        grad_in_weight,
        grad_short,
        grad_one,
        grad_two,
        grad_out_weight,
    )


def solution(mesh):
    mesh = Mesh(mesh.devices.reshape(2, 4, 2, 4, 4), everyone)
    positions = ("x", "core", "zl", "y")
    split_rows, split_filter = P("zh", positions, None), P(positions, None)
    return jax.shard_map(
        per_device,
        mesh=mesh,
        in_specs=(split_rows, P(), P(), split_filter, split_filter, P(), split_rows),
        out_specs=(split_rows, split_rows, P(), P(), split_filter, split_filter, P()),
        check_vma=False,
    )
```

```python
import functools
import math

import jax
import jax.numpy as jnp
import numpy as np
from jax import lax
from jax.experimental import pallas as pl
from jax.experimental.pallas import tpu as pltpu
from jax.sharding import Mesh
from jax.sharding import PartitionSpec as P

everyone = ("zh", "x", "core", "zl", "y")
vmem_limit = 16 * 1024 * 1024


def two_terms(table):
    high = table.astype(np.float32).astype(jnp.bfloat16)
    low = (table - high.astype(np.float64)).astype(np.float32).astype(jnp.bfloat16)
    return high, low


def left_table(table):
    high, low = two_terms(table)
    return np.concatenate([high, low, high], 1)


def right_table(table):
    high, low = two_terms(table)
    return np.concatenate([high, low, high], 0)


def transform_tables(blocks, rows):
    length = 2 * blocks * rows
    outer = np.arange(blocks) + 0.5
    step = 2.0 * math.pi * np.outer(outer, np.arange(blocks)) / (2 * blocks)
    turn = 2.0 * math.pi * np.outer(outer, np.arange(rows)) / length
    inner = 2.0 * math.pi * np.outer(np.arange(rows), np.arange(rows)) / rows
    first = np.concatenate([np.cos(step), -np.sin(step)], 0)
    c, s = np.cos(inner), np.sin(inner)
    second = np.block([[c, -s], [s, c]])
    second_back = np.block([[c, s], [-s, c]])
    first_back = np.concatenate([np.cos(step).T, -np.sin(step).T], 1) * (2.0 / length)
    return [
        left_table(first),
        right_table(second),
        right_table(second_back),
        left_table(first_back),
        np.cos(turn).astype(np.float32),
        np.sin(turn).astype(np.float32),
    ]


def bf16_dot(a, b):
    return jnp.dot(a, b, preferred_element_type=jnp.float32)


def split(x):
    high = x.astype(jnp.bfloat16)
    low = (x - high.astype(jnp.float32)).astype(jnp.bfloat16)
    return high, low


def table_left(table, x):
    x_high, x_low = split(x)
    return bf16_dot(table, jnp.concatenate([x_high, x_high, x_low], 0))


def table_right(x, table):
    x_high, x_low = split(x)
    return bf16_dot(jnp.concatenate([x_high, x_high, x_low], 1), table)


def pack_kernel(seq_ref, in_weight_ref, one_ref, two_ref, out_weight_ref, grad_ref, out_ref, both_ref, rows_ref):
    width = out_weight_ref.shape[0]
    lanes = rows_ref.shape[2]
    contract_first = (((0,), (1,)), ((), ()))
    contract_last = (((1,), (1,)), ((), ()))
    seq = seq_ref[0]

    def put(index, x):
        rows_ref[index // 2, pl.ds(index % 2, width, stride=2), :] = x

    for group in range(3):
        weight = in_weight_ref[:, group * width : (group + 1) * width]
        put(
            group,
            lax.dot_general(weight, seq, contract_first, preferred_element_type=jnp.float32),
        )
    put(
        3,
        lax.dot_general(
            out_weight_ref[...], grad_ref[0], contract_last, preferred_element_type=jnp.float32
        ),
    )
    chosen = jnp.where(lax.axis_index("zh") == 0, one_ref[...], two_ref[...]).T
    high = chosen.astype(jnp.bfloat16).astype(jnp.float32)
    put(4, high)
    put(5, chosen - high)
    both_ref[:, :width] = seq
    both_ref[:, width:] = grad_ref[0]
    for pair in range(3):
        out_ref[:, :, pair * lanes : (pair + 1) * lanes] = (
            rows_ref[pair].reshape(width, 2, lanes).astype(jnp.bfloat16)
        )


def convolve_kernel(
    in_ref,
    short_ref,
    first_ref,
    second_ref,
    second_back_ref,
    first_back_ref,
    turn_cos_ref,
    turn_sin_ref,
    *rest,
):
    out_ref, rows_ref = rest[-2:]
    sources, rows = in_ref.shape[0], in_ref.shape[2] // 3
    blocks = sources // 2
    width = short_ref.shape[1] // 3
    scale = 1.0 / math.sqrt(sources * rows)
    turn_cos = turn_cos_ref[...]
    turn_sin = turn_sin_ref[...]
    lane = lax.broadcasted_iota(jnp.int32, (blocks, rows), 1)
    block = lax.broadcasted_iota(jnp.int32, (blocks, rows), 0)

    for pair in range(3):
        rows_ref[pair] = (
            in_ref[:, :, pair * rows : (pair + 1) * rows]
            .astype(jnp.float32)
            .reshape(sources * 2, rows)
        )

    def row(member, index):
        return rows_ref[index // 2, pl.ds(member * sources + index % 2, blocks, stride=2), :]

    def later(x, distance):
        moved = pltpu.roll(x, distance, 1)
        carried = jnp.where(block == 0, 0.0, pltpu.roll(moved, 1, 0))
        return jnp.where(lane < distance, carried, moved)

    def earlier(x, distance):
        moved = pltpu.roll(x, rows - distance, 1)
        carried = jnp.where(block == blocks - 1, 0.0, pltpu.roll(moved, blocks - 1, 0))
        return jnp.where(lane >= rows - distance, carried, moved)

    def forward(signals):
        outer = table_left(first_ref[...], jnp.concatenate(signals, 1))
        turned = []
        for i in range(len(signals)):
            re = outer[:blocks, i * rows : (i + 1) * rows]
            im = outer[blocks:, i * rows : (i + 1) * rows]
            turned.append(
                jnp.concatenate(
                    [re * turn_cos + im * turn_sin, im * turn_cos - re * turn_sin], 1
                )
            )
        inner = table_right(jnp.concatenate(turned, 0), second_ref[...])
        return [
            (inner[i * blocks : (i + 1) * blocks, :rows], inner[i * blocks : (i + 1) * blocks, rows:])
            for i in range(len(signals))
        ]

    def backward(spectra):
        stacked = jnp.concatenate([jnp.concatenate(pair, 1) for pair in spectra], 0)
        inner = table_right(stacked, second_back_ref[...])
        turned = []
        for i in range(len(spectra)):
            re = inner[i * blocks : (i + 1) * blocks, :rows]
            im = inner[i * blocks : (i + 1) * blocks, rows:]
            turned.append(
                jnp.concatenate(
                    [re * turn_cos - im * turn_sin, im * turn_cos + re * turn_sin], 0
                )
            )
        outer = table_left(first_back_ref[...], jnp.concatenate(turned, 1))
        return [outer[:, i * rows : (i + 1) * rows] for i in range(len(spectra))]

    def times(a, b):
        return a[0] * b[0] - a[1] * b[1], a[0] * b[1] + a[1] * b[0]

    def conj_times(a, b):
        return a[0] * b[0] + a[1] * b[1], a[0] * b[1] - a[1] * b[0]

    def added(a, b):
        return a[0] + b[0], a[1] + b[1]

    mesh_place = lax.axis_index(everyone)
    short = short_ref[...]
    short_lane = lax.broadcasted_iota(jnp.int32, short.shape, 1)
    taps = []
    for group in range(3):
        column = jnp.sum(
            jnp.where(short_lane == mesh_place + group * width, short, 0.0), axis=1, keepdims=True
        )
        taps.append([column[tap : tap + 1, :] for tap in range(3)])

    projected, lagged_one, lagged_two, mixed, pre = [], [], [], [], []
    for member in range(2):
        now = [row(member, group) for group in range(3)]
        one = [later(x, 1) for x in now]
        two = [later(x, 2) for x in now]
        projected.append(now)
        lagged_one.append(one)
        lagged_two.append(two)
        mixed.append(
            [
                taps[g][0] * now[g] + taps[g][1] * one[g] + taps[g][2] * two[g]
                for g in range(3)
            ]
        )
        pre.append(row(member, 3))
    members = range(2)
    grad_conv_two = [pre[m] * mixed[m][2] for m in members]
    spectra = forward(
        [row(m, 4) + row(m, 5) for m in members] + [mixed[m][0] for m in members] + grad_conv_two
    )
    one_spec, two_spec = spectra[0], spectra[1]
    value_spec, conv_two_spec = spectra[2:4], spectra[4:6]
    found = backward(
        [times(one_spec, value_spec[m]) for m in members]
        + [conj_times(two_spec, conv_two_spec[m]) for m in members]
    )
    conv_one, grad_gated = found[:2], found[2:]
    spectra = forward(
        [mixed[m][1] * conv_one[m] for m in members]
        + [mixed[m][1] * grad_gated[m] for m in members]
    )
    gated_spec, conv_one_spec = spectra[:2], spectra[2:]
    found = backward(
        [times(two_spec, gated_spec[m]) for m in members]
        + [conj_times(one_spec, conv_one_spec[m]) for m in members]
        + [
            added(*[conj_times(value_spec[m], conv_one_spec[m]) for m in members]),
            added(*[conj_times(gated_spec[m], conv_two_spec[m]) for m in members]),
        ]
    )
    conv_two, grad_value = found[:2], found[2:4]
    grad_filters = [found[4] * scale, found[5] * scale]

    new = lax.broadcasted_iota(jnp.int32, (blocks, blocks), 0)
    old = lax.broadcasted_iota(jnp.int32, (blocks, blocks), 1)
    wanted = (new & 99) | (((new >> 2) & 1) << 4) | (((new >> 3) & 3) << 2)
    reorder = jnp.where(old == wanted, 1.0, 0.0).astype(jnp.bfloat16)
    sums = [[0.0] * 3 for _ in range(3)]
    for m in members:
        sent = [mixed[m][2] * conv_two[m]]
        grads = [grad_value[m], grad_gated[m] * conv_one[m], pre[m] * conv_two[m]]
        for g in range(3):
            sent.append(
                taps[g][0] * grads[g]
                + taps[g][1] * earlier(grads[g], 1)
                + taps[g][2] * earlier(grads[g], 2)
            )
            for tap, lagged in enumerate((projected, lagged_one, lagged_two)):
                sums[g][tap] = sums[g][tap] + jnp.sum(
                    jnp.sum(grads[g] * lagged[m][g], axis=0, keepdims=True), axis=1, keepdims=True
                )
        sent.extend(grad_filters)
        turned = bf16_dot(reorder, jnp.concatenate(sent, 1).astype(jnp.bfloat16))
        half = out_ref.shape[0] // 2
        for index in range(len(sent)):
            out_ref[m * half : (m + 1) * half, index] = (
                turned[:, index * rows : (index + 1) * rows]
                .reshape(half, blocks // half, rows)
                .astype(jnp.bfloat16)
            )
    shape = (blocks // half, rows)
    sum_lane = lax.broadcasted_iota(jnp.int32, shape, 1)
    line = jnp.zeros(shape, jnp.float32)
    for g in range(3):
        for tap in range(3):
            total = sums[g][tap] * scale
            high = total.astype(jnp.bfloat16).astype(jnp.float32)
            line = jnp.where(sum_lane == g * 3 + tap, high, line)
            line = jnp.where(sum_lane == 16 + g * 3 + tap, total - high, line)
    out_ref[:, 6] = jnp.broadcast_to(line[None], (2 * half,) + shape).astype(jnp.bfloat16)


def channel_order(place_of):
    channel = lax.broadcasted_iota(jnp.int32, (256, 256), 0)
    row = lax.broadcasted_iota(jnp.int32, (256, 256), 1)
    zh, x, core = channel >> 7, (channel >> 5) & 3, (channel >> 4) & 1
    zl, y = (channel >> 2) & 3, channel & 3
    return jnp.where(row == place_of(zh, x, core, zl, y), 1.0, 0.0).astype(jnp.bfloat16)


def part_kernel(in_ref, *refs):
    both_refs, part_refs, send_refs = refs[:8], refs[8:12], refs[12:16]
    rows_ref, sums_ref = refs[16:]
    sources, kinds, blocks, rows = in_ref.shape
    width = both_refs[0].shape[1] // 2
    x, core, y = lax.axis_index("x"), lax.axis_index("core"), lax.axis_index("y")
    turn = 1 - 2 * core
    rows_ref[...] = in_ref[...].astype(jnp.float32).reshape(sources * kinds * blocks, rows)
    out_part = jnp.zeros((sources, width), jnp.float32)
    in_part = jnp.zeros((3 * sources, width), jnp.float32)
    for other in range(2):
        for ahead in range(4):
            block = (core ^ other) * 4 + ((y + turn * ahead) & 3)
            kept = jnp.concatenate(
                [
                    rows_ref[pl.ds(kind * blocks + block, sources, stride=kinds * blocks), :]
                    for kind in range(kinds)
                ],
                0,
            ).astype(jnp.bfloat16)
            send_refs[ahead][other] = kept
            both_ref = both_refs[4 + ahead if other else (4 - ahead) % 4]
            out_part += bf16_dot(kept[:sources], both_ref[:, width:])
            in_part += bf16_dot(kept[sources : 4 * sources], both_ref[:, :width])
    sums_ref[0] = out_part
    for group in range(3):
        sums_ref[1 + group] = in_part[group * sources : (group + 1) * sources]
    for ahead in range(4):
        part_refs[ahead][...] = sums_ref[(x + turn * ahead) & 3]


def finish_kernel(*refs):
    held = refs[:8]
    in_weight_ref, out_weight_ref, outputs_ref, grad_inputs_ref, short_ref = refs[8:13]
    one_ref, two_ref = refs[13:]
    width = out_weight_ref.shape[0]
    count = width // 8
    core, y = lax.axis_index("core"), lax.axis_index("y")
    turn = 1 - 2 * core

    def row_of(zh, x, c, zl, v):
        other = c ^ core
        step = (turn * (1 - 2 * other) * (y - v)) & 3
        return (other * 4 + step) * 32 + (zh * 16 + x * 4 + zl)

    order = channel_order(row_of)
    contract_first = (((0,), (1,)), ((), ()))
    contract_last = (((1,), (1,)), ((), ()))

    def stacked_rows(kind):
        return jnp.concatenate(
            [held[i][i // 4, kind * count : (kind + 1) * count, :] for i in range(8)], 0
        )

    def natural(kind):
        stacked = stacked_rows(kind)
        return lax.dot_general(
            stacked, order, contract_first, preferred_element_type=jnp.float32
        )

    outputs_ref[0] = bf16_dot(natural(0).astype(jnp.bfloat16), out_weight_ref[...]).astype(
        jnp.bfloat16
    )
    total = None
    for group in range(3):
        term = lax.dot_general(
            natural(1 + group).astype(jnp.bfloat16),
            in_weight_ref[:, group * width : (group + 1) * width],
            contract_last,
            preferred_element_type=jnp.float32,
        )
        total = term if total is None else total + term
    grad_inputs_ref[0] = total.astype(jnp.bfloat16)
    one_ref[...] = natural(4)
    two_ref[...] = natural(5)
    sums = lax.dot_general(
        stacked_rows(6), order, contract_first, preferred_element_type=jnp.float32
    )
    for group in range(3):
        short_ref[:, group * width : (group + 1) * width] = (
            sums[group * 3 : group * 3 + 3, :] + sums[16 + group * 3 : 19 + group * 3, :]
        )


def add_x_kernel(*refs):
    out_ref = refs[4]
    total = refs[0][...] + refs[1][...] + refs[2][...] + refs[3][...]
    lanes = out_ref.shape[2]
    rows = jnp.concatenate([total[:, :lanes], total[:, lanes:]], 0)
    out_ref[...] = jnp.broadcast_to(rows.astype(jnp.bfloat16)[None], out_ref.shape)


def add_z_kernel(scale, in_ref, *refs):
    out_ref = refs[-1]
    total = jnp.sum(in_ref[...].astype(jnp.float32), axis=0) * scale
    out_ref[...] = jnp.broadcast_to(total.astype(jnp.bfloat16)[None], out_ref.shape)


def place_kernel(own_ref, other_ref, in_weight_ref, out_weight_ref):
    width, lanes = out_weight_ref.shape[0], own_ref.shape[2]
    core = lax.axis_index("core")
    order = channel_order(
        lambda zh, x, c, zl, y: ((c ^ core) * 4 + y) * 32 + (zh * 16 + x * 4 + zl)
    )
    contract_first = (((0,), (1,)), ((), ()))
    for kind in range(4):
        for half in range(2):
            stacked = jnp.concatenate(
                [
                    ref[kind * 4 + y, half * 32 : (half + 1) * 32, :]
                    for ref in (own_ref, other_ref)
                    for y in range(4)
                ],
                0,
            )
            if kind == 0:
                out_weight_ref[:, half * lanes : (half + 1) * lanes] = bf16_dot(order, stacked)
            else:
                in_weight_ref[
                    half * lanes : (half + 1) * lanes, (kind - 1) * width : kind * width
                ] = lax.dot_general(
                    stacked, order, contract_first, preferred_element_type=jnp.float32
                )


def call(kernel, out_shape, scratch=(), limit=vmem_limit, **options):
    return pl.pallas_call(
        kernel,
        out_shape=out_shape,
        scratch_shapes=list(scratch),
        compiler_params=pltpu.CompilerParams(vmem_limit_bytes=limit),
        **options,
    )


def specs(*spaces):
    return [pl.BlockSpec(memory_space=space) for space in spaces]


def exchange(x, axes):
    return lax.all_to_all(x, axes, split_axis=0, concat_axis=0, tiled=True)


def swap_core(x):
    return lax.ppermute(x, "core", [(0, 1), (1, 0)])


def ring(x, axis, distance):
    axes = ("x", "core") if axis == "x" else ("core", "y")
    route = []
    for core, turn in ((0, distance), (1, -distance)):
        for i in range(4):
            j = (i + turn) % 4
            pair = (i * 2 + core, j * 2 + core) if axis == "x" else (core * 4 + i, core * 4 + j)
            route.append(pair)
    return lax.ppermute(x, axes, route)


def per_device(inputs, in_weight, short_kernel, filter_one, filter_two, out_weight, out_grad):
    width = out_weight.shape[0]
    rows = inputs.shape[1]
    devices = lax.axis_size(everyone)
    scale = 1.0 / math.sqrt(devices * rows)
    shape = jax.ShapeDtypeStruct
    f32, bf16 = jnp.float32, jnp.bfloat16
    packed, both = call(
        pack_kernel,
        (shape((width, 2, 3 * rows), bf16), shape((rows, 2 * width), bf16)),
        [pltpu.VMEM((3, 2 * width, rows), f32)],
        limit=56 * 1024 * 1024,
    )(inputs, in_weight, filter_one, filter_two, out_weight, out_grad)
    received = exchange(packed, everyone)
    gathered = [both] + [ring(both, "y", distance) for distance in (1, 2, 3)]
    gathered += [swap_core(x) for x in gathered]
    tables = [jnp.asarray(t) for t in transform_tables(devices // 2, rows)]
    back = call(
        convolve_kernel,
        shape((32, 7, 8, rows), bf16),
        [pltpu.VMEM((3, 2 * devices, rows), f32)],
        in_specs=specs(*[pltpu.VMEM] * (2 + len(tables)), *[pl.ANY] * 2),
    )(received, short_kernel, *tables, gathered[1], gathered[3])
    halfway = exchange(back, ("zh", "x", "zl"))
    found = call(
        part_kernel,
        (shape((32, width), f32),) * 4 + (shape((2, 7 * 32, rows), bf16),) * 4,
        [pltpu.VMEM((32 * 7 * 8, rows), f32), pltpu.VMEM((4, 32, width), f32)],
    )(halfway, *gathered)
    part = [found[0]] + [ring(found[distance], "x", distance) for distance in (1, 2, 3)]
    arrived = [found[4]] + [ring(found[4 + i], "y", i) for i in (1, 2, 3)]
    arrived += [swap_core(x) for x in arrived]
    part = call(add_x_kernel, shape((8, 64, rows), bf16))(*part)
    part = exchange(part, ("zh", "zl"))
    part = call(
        functools.partial(add_z_kernel, scale),
        shape((16, 64, rows), bf16),
        in_specs=specs(pltpu.VMEM, *[pl.ANY] * 4),
    )(part, *arrived[4:])
    part = exchange(part, ("x", "y"))
    outputs, grad_inputs, grad_short, grad_one, grad_two = call(
        finish_kernel,
        (
            shape((1, rows, width), bf16),
            shape((1, rows, width), bf16),
            shape((3, 3 * width), f32),
            shape((rows, width), f32),
            shape((rows, width), f32),
        ),
    )(*arrived, in_weight, out_weight)
    part, grad_short = lax.optimization_barrier((part, grad_short))
    grad_in_weight, grad_out_weight = call(
        place_kernel, (shape((width, 3 * width), f32), shape((width, width), f32))
    )(part, swap_core(part))
    return (
        outputs,
        grad_inputs,
        grad_in_weight,
        grad_short,
        grad_one,
        grad_two,
        grad_out_weight,
    )


def solution(mesh):
    mesh = Mesh(mesh.devices.reshape(2, 4, 2, 4, 4), everyone)
    positions = ("x", "core", "zl", "y")
    split_rows, split_filter = P("zh", positions, None), P(positions, None)
    return jax.shard_map(
        per_device,
        mesh=mesh,
        in_specs=(split_rows, P(), P(), split_filter, split_filter, P(), split_rows),
        out_specs=(split_rows, split_rows, P(), P(), split_filter, split_filter, P()),
        check_vma=False,
    )
```

```python
import functools
import math

import jax
import jax.numpy as jnp
import numpy as np
from jax import lax
from jax.experimental import pallas as pl
from jax.experimental.pallas import tpu as pltpu
from jax.sharding import Mesh
from jax.sharding import PartitionSpec as P

everyone = ("zh", "x", "core", "zl", "y")
vmem_limit = 16 * 1024 * 1024


def two_terms(table):
    high = table.astype(np.float32).astype(jnp.bfloat16)
    low = (table - high.astype(np.float64)).astype(np.float32).astype(jnp.bfloat16)
    return high, low


def left_table(table):
    high, low = two_terms(table)
    return np.concatenate([high, low, high], 1)


def right_table(table):
    high, low = two_terms(table)
    return np.concatenate([high, low, high], 0)


def transform_tables(blocks, rows):
    length = 2 * blocks * rows
    outer = np.arange(blocks) + 0.5
    step = 2.0 * math.pi * np.outer(outer, np.arange(blocks)) / (2 * blocks)
    turn = 2.0 * math.pi * np.outer(outer, np.arange(rows)) / length
    inner = 2.0 * math.pi * np.outer(np.arange(rows), np.arange(rows)) / rows
    first = np.concatenate([np.cos(step), -np.sin(step)], 0)
    c, s = np.cos(inner), np.sin(inner)
    second = np.block([[c, -s], [s, c]])
    second_back = np.block([[c, s], [-s, c]])
    first_back = np.concatenate([np.cos(step).T, -np.sin(step).T], 1) * (2.0 / length)
    return [
        left_table(first),
        right_table(second),
        right_table(second_back),
        left_table(first_back),
        np.cos(turn).astype(np.float32),
        np.sin(turn).astype(np.float32),
    ]


def bf16_dot(a, b):
    return jnp.dot(a, b, preferred_element_type=jnp.float32)


def split(x):
    high = x.astype(jnp.bfloat16)
    low = (x - high.astype(jnp.float32)).astype(jnp.bfloat16)
    return high, low


def table_left(table, x):
    x_high, x_low = split(x)
    return bf16_dot(table, jnp.concatenate([x_high, x_high, x_low], 0))


def table_right(x, table):
    x_high, x_low = split(x)
    return bf16_dot(jnp.concatenate([x_high, x_high, x_low], 1), table)


def pack_kernel(seq_ref, in_weight_ref, one_ref, two_ref, out_weight_ref, grad_ref, out_ref, both_ref, rows_ref):
    width = out_weight_ref.shape[0]
    lanes = rows_ref.shape[2]
    contract_first = (((0,), (1,)), ((), ()))
    contract_last = (((1,), (1,)), ((), ()))
    seq = seq_ref[0]

    def put(index, x):
        rows_ref[index // 2, pl.ds(index % 2, width, stride=2), :] = x

    for group in range(3):
        weight = in_weight_ref[:, group * width : (group + 1) * width]
        put(
            group,
            lax.dot_general(weight, seq, contract_first, preferred_element_type=jnp.float32),
        )
    put(
        3,
        lax.dot_general(
            out_weight_ref[...], grad_ref[0], contract_last, preferred_element_type=jnp.float32
        ),
    )
    chosen = jnp.where(lax.axis_index("zh") == 0, one_ref[...], two_ref[...]).T
    high = chosen.astype(jnp.bfloat16).astype(jnp.float32)
    put(4, high)
    put(5, chosen - high)
    both_ref[:, :width] = seq
    both_ref[:, width:] = grad_ref[0]
    for pair in range(3):
        out_ref[:, :, pair * lanes : (pair + 1) * lanes] = (
            rows_ref[pair].reshape(width, 2, lanes).astype(jnp.bfloat16)
        )


def convolve_kernel(
    in_ref,
    short_ref,
    first_ref,
    second_ref,
    second_back_ref,
    first_back_ref,
    turn_cos_ref,
    turn_sin_ref,
    *rest,
):
    out_ref, rows_ref = rest[-2:]
    sources, rows = in_ref.shape[0], in_ref.shape[2] // 3
    blocks = sources // 2
    width = short_ref.shape[1] // 3
    scale = 1.0 / math.sqrt(sources * rows)
    turn_cos = turn_cos_ref[...]
    turn_sin = turn_sin_ref[...]
    lane = lax.broadcasted_iota(jnp.int32, (blocks, rows), 1)
    block = lax.broadcasted_iota(jnp.int32, (blocks, rows), 0)

    for pair in range(3):
        rows_ref[pair] = (
            in_ref[:, :, pair * rows : (pair + 1) * rows]
            .astype(jnp.float32)
            .reshape(sources * 2, rows)
        )

    def row(member, index):
        return rows_ref[index // 2, pl.ds(member * sources + index % 2, blocks, stride=2), :]

    def later(x, distance):
        moved = pltpu.roll(x, distance, 1)
        carried = jnp.where(block == 0, 0.0, pltpu.roll(moved, 1, 0))
        return jnp.where(lane < distance, carried, moved)

    def earlier(x, distance):
        moved = pltpu.roll(x, rows - distance, 1)
        carried = jnp.where(block == blocks - 1, 0.0, pltpu.roll(moved, blocks - 1, 0))
        return jnp.where(lane >= rows - distance, carried, moved)

    def forward(signals):
        outer = table_left(first_ref[...], jnp.concatenate(signals, 1))
        turned = []
        for i in range(len(signals)):
            re = outer[:blocks, i * rows : (i + 1) * rows]
            im = outer[blocks:, i * rows : (i + 1) * rows]
            turned.append(
                jnp.concatenate(
                    [re * turn_cos + im * turn_sin, im * turn_cos - re * turn_sin], 1
                )
            )
        inner = table_right(jnp.concatenate(turned, 0), second_ref[...])
        return [
            (inner[i * blocks : (i + 1) * blocks, :rows], inner[i * blocks : (i + 1) * blocks, rows:])
            for i in range(len(signals))
        ]

    def backward(spectra):
        stacked = jnp.concatenate([jnp.concatenate(pair, 1) for pair in spectra], 0)
        inner = table_right(stacked, second_back_ref[...])
        turned = []
        for i in range(len(spectra)):
            re = inner[i * blocks : (i + 1) * blocks, :rows]
            im = inner[i * blocks : (i + 1) * blocks, rows:]
            turned.append(
                jnp.concatenate(
                    [re * turn_cos - im * turn_sin, im * turn_cos + re * turn_sin], 0
                )
            )
        outer = table_left(first_back_ref[...], jnp.concatenate(turned, 1))
        return [outer[:, i * rows : (i + 1) * rows] for i in range(len(spectra))]

    def times(a, b):
        return a[0] * b[0] - a[1] * b[1], a[0] * b[1] + a[1] * b[0]

    def conj_times(a, b):
        return a[0] * b[0] + a[1] * b[1], a[0] * b[1] - a[1] * b[0]

    def added(a, b):
        return a[0] + b[0], a[1] + b[1]

    mesh_place = lax.axis_index(everyone)
    short = short_ref[...]
    short_lane = lax.broadcasted_iota(jnp.int32, short.shape, 1)
    taps = []
    for group in range(3):
        column = jnp.sum(
            jnp.where(short_lane == mesh_place + group * width, short, 0.0), axis=1, keepdims=True
        )
        taps.append([column[tap : tap + 1, :] for tap in range(3)])

    projected, lagged_one, lagged_two, mixed, pre = [], [], [], [], []
    for member in range(2):
        now = [row(member, group) for group in range(3)]
        one = [later(x, 1) for x in now]
        two = [later(x, 2) for x in now]
        projected.append(now)
        lagged_one.append(one)
        lagged_two.append(two)
        mixed.append(
            [
                taps[g][0] * now[g] + taps[g][1] * one[g] + taps[g][2] * two[g]
                for g in range(3)
            ]
        )
        pre.append(row(member, 3))
    members = range(2)
    grad_conv_two = [pre[m] * mixed[m][2] for m in members]
    spectra = forward(
        [row(m, 4) + row(m, 5) for m in members] + [mixed[m][0] for m in members] + grad_conv_two
    )
    one_spec, two_spec = spectra[0], spectra[1]
    value_spec, conv_two_spec = spectra[2:4], spectra[4:6]
    found = backward(
        [times(one_spec, value_spec[m]) for m in members]
        + [conj_times(two_spec, conv_two_spec[m]) for m in members]
    )
    conv_one, grad_gated = found[:2], found[2:]
    spectra = forward(
        [mixed[m][1] * conv_one[m] for m in members]
        + [mixed[m][1] * grad_gated[m] for m in members]
    )
    gated_spec, conv_one_spec = spectra[:2], spectra[2:]
    found = backward(
        [times(two_spec, gated_spec[m]) for m in members]
        + [conj_times(one_spec, conv_one_spec[m]) for m in members]
        + [
            added(*[conj_times(value_spec[m], conv_one_spec[m]) for m in members]),
            added(*[conj_times(gated_spec[m], conv_two_spec[m]) for m in members]),
        ]
    )
    conv_two, grad_value = found[:2], found[2:4]
    grad_filters = [found[4] * scale, found[5] * scale]

    new = lax.broadcasted_iota(jnp.int32, (blocks, blocks), 0)
    old = lax.broadcasted_iota(jnp.int32, (blocks, blocks), 1)
    wanted = (((new >> 3) & 3) << 5) | (((new >> 6) & 1) << 4) | (((new >> 1) & 3) << 2)
    wanted = wanted | (((new >> 5) & 1) << 1) | (new & 1)
    reorder = jnp.where(old == wanted, 1.0, 0.0).astype(jnp.bfloat16)
    sums = [[0.0] * 3 for _ in range(3)]
    for m in members:
        sent = [mixed[m][2] * conv_two[m]]
        grads = [grad_value[m], grad_gated[m] * conv_one[m], pre[m] * conv_two[m]]
        for g in range(3):
            sent.append(
                taps[g][0] * grads[g]
                + taps[g][1] * earlier(grads[g], 1)
                + taps[g][2] * earlier(grads[g], 2)
            )
            for tap, lagged in enumerate((projected, lagged_one, lagged_two)):
                sums[g][tap] = sums[g][tap] + jnp.sum(
                    jnp.sum(grads[g] * lagged[m][g], axis=0, keepdims=True), axis=1, keepdims=True
                )
        sent.extend(grad_filters)
        turned = bf16_dot(reorder, jnp.concatenate(sent, 1).astype(jnp.bfloat16))
        half = out_ref.shape[0] // 2
        count = 2 * half
        for index in range(len(sent)):
            for pair in range(4):
                place = (index * 4 + pair) * rows
                out_ref[m * half : (m + 1) * half, :, place : place + rows] = (
                    turned[pair * count : (pair + 1) * count, index * rows : (index + 1) * rows]
                    .reshape(half, 2, rows)
                    .astype(jnp.bfloat16)
                )
    shape = (2, rows)
    sum_lane = lax.broadcasted_iota(jnp.int32, shape, 1)
    line = jnp.zeros(shape, jnp.float32)
    for g in range(3):
        for tap in range(3):
            total = sums[g][tap] * scale
            high = total.astype(jnp.bfloat16).astype(jnp.float32)
            line = jnp.where(sum_lane == g * 3 + tap, high, line)
            line = jnp.where(sum_lane == 16 + g * 3 + tap, total - high, line)
    out_ref[:, :, 24 * rows :] = jnp.broadcast_to(line[None], (2 * half,) + shape).astype(
        jnp.bfloat16
    )


def channel_order(place_of):
    channel = lax.broadcasted_iota(jnp.int32, (256, 256), 0)
    row = lax.broadcasted_iota(jnp.int32, (256, 256), 1)
    zh, x, core = channel >> 7, (channel >> 5) & 3, (channel >> 4) & 1
    zl, y = (channel >> 2) & 3, channel & 3
    return jnp.where(row == place_of(zh, x, core, zl, y), 1.0, 0.0).astype(jnp.bfloat16)


def part_kernel(in_ref, *refs):
    both_refs, part_refs, send_refs = refs[:8], refs[8:12], refs[12:16]
    rows_ref, sums_ref = refs[16:]
    tiles, rows = rows_ref.shape[0], rows_ref.shape[2]
    sources = in_ref.shape[0]
    width = both_refs[0].shape[1] // 2
    x, core, y = lax.axis_index("x"), lax.axis_index("core"), lax.axis_index("y")
    turn = 1 - 2 * core
    for tile in range(tiles):
        rows_ref[tile] = (
            in_ref[:, :, tile * rows : (tile + 1) * rows]
            .astype(jnp.float32)
            .reshape(sources * 2, rows)
        )
    sums = rows_ref[tiles - 1, pl.ds(0, sources, stride=2), :]
    out_part = jnp.zeros((sources, width), jnp.float32)
    in_part = jnp.zeros((3 * sources, width), jnp.float32)
    for other in range(2):
        for ahead in range(4):
            block = (core ^ other) * 4 + ((y + turn * ahead) & 3)
            kept = [
                rows_ref[kind * 4 + (block >> 1), pl.ds(block & 1, sources, stride=2), :]
                for kind in range(6)
            ]
            kept = jnp.concatenate(kept + [sums], 0).astype(jnp.bfloat16)
            send_refs[ahead][other] = kept
            both_ref = both_refs[4 + ahead if other else (4 - ahead) % 4]
            out_part += bf16_dot(kept[:sources], both_ref[:, width:])
            in_part += bf16_dot(kept[sources : 4 * sources], both_ref[:, :width])
    sums_ref[0] = out_part
    for group in range(3):
        sums_ref[1 + group] = in_part[group * sources : (group + 1) * sources]
    for ahead in range(4):
        part_refs[ahead][...] = sums_ref[(x + turn * ahead) & 3]


def finish_kernel(*refs):
    held = refs[:8]
    in_weight_ref, out_weight_ref, outputs_ref, grad_inputs_ref, short_ref = refs[8:13]
    one_ref, two_ref = refs[13:]
    width = out_weight_ref.shape[0]
    count = width // 8
    core, y = lax.axis_index("core"), lax.axis_index("y")
    turn = 1 - 2 * core

    def row_of(zh, x, c, zl, v):
        other = c ^ core
        step = (turn * (1 - 2 * other) * (y - v)) & 3
        return (other * 4 + step) * 32 + (zh * 16 + x * 4 + zl)

    order = channel_order(row_of)
    contract_first = (((0,), (1,)), ((), ()))
    contract_last = (((1,), (1,)), ((), ()))

    def stacked_rows(kind):
        return jnp.concatenate(
            [held[i][i // 4, kind * count : (kind + 1) * count, :] for i in range(8)], 0
        )

    def natural(kind):
        stacked = stacked_rows(kind)
        return lax.dot_general(
            stacked, order, contract_first, preferred_element_type=jnp.float32
        )

    outputs_ref[0] = bf16_dot(natural(0).astype(jnp.bfloat16), out_weight_ref[...]).astype(
        jnp.bfloat16
    )
    total = None
    for group in range(3):
        term = lax.dot_general(
            natural(1 + group).astype(jnp.bfloat16),
            in_weight_ref[:, group * width : (group + 1) * width],
            contract_last,
            preferred_element_type=jnp.float32,
        )
        total = term if total is None else total + term
    grad_inputs_ref[0] = total.astype(jnp.bfloat16)
    one_ref[...] = natural(4)
    two_ref[...] = natural(5)
    sums = lax.dot_general(
        stacked_rows(6), order, contract_first, preferred_element_type=jnp.float32
    )
    for group in range(3):
        short_ref[:, group * width : (group + 1) * width] = (
            sums[group * 3 : group * 3 + 3, :] + sums[16 + group * 3 : 19 + group * 3, :]
        )


def add_x_kernel(*refs):
    out_ref = refs[4]
    total = refs[0][...] + refs[1][...] + refs[2][...] + refs[3][...]
    lanes = out_ref.shape[2]
    rows = jnp.concatenate([total[:, :lanes], total[:, lanes:]], 0)
    out_ref[...] = jnp.broadcast_to(rows.astype(jnp.bfloat16)[None], out_ref.shape)


def add_z_kernel(scale, in_ref, *refs):
    out_ref = refs[-1]
    total = jnp.sum(in_ref[...].astype(jnp.float32), axis=0) * scale
    out_ref[...] = jnp.broadcast_to(total.astype(jnp.bfloat16)[None], out_ref.shape)


def place_kernel(own_ref, other_ref, in_weight_ref, out_weight_ref):
    width, lanes = out_weight_ref.shape[0], own_ref.shape[2]
    core = lax.axis_index("core")
    order = channel_order(
        lambda zh, x, c, zl, y: ((c ^ core) * 4 + y) * 32 + (zh * 16 + x * 4 + zl)
    )
    contract_first = (((0,), (1,)), ((), ()))
    for kind in range(4):
        for half in range(2):
            stacked = jnp.concatenate(
                [
                    ref[kind * 4 + y, half * 32 : (half + 1) * 32, :]
                    for ref in (own_ref, other_ref)
                    for y in range(4)
                ],
                0,
            )
            if kind == 0:
                out_weight_ref[:, half * lanes : (half + 1) * lanes] = bf16_dot(order, stacked)
            else:
                in_weight_ref[
                    half * lanes : (half + 1) * lanes, (kind - 1) * width : kind * width
                ] = lax.dot_general(
                    stacked, order, contract_first, preferred_element_type=jnp.float32
                )


def call(kernel, out_shape, scratch=(), limit=vmem_limit, **options):
    return pl.pallas_call(
        kernel,
        out_shape=out_shape,
        scratch_shapes=list(scratch),
        compiler_params=pltpu.CompilerParams(vmem_limit_bytes=limit),
        **options,
    )


def specs(*spaces):
    return [pl.BlockSpec(memory_space=space) for space in spaces]


def exchange(x, axes):
    return lax.all_to_all(x, axes, split_axis=0, concat_axis=0, tiled=True)


def swap_core(x):
    return lax.ppermute(x, "core", [(0, 1), (1, 0)])


def ring(x, axis, distance):
    axes = ("x", "core") if axis == "x" else ("core", "y")
    route = []
    for core, turn in ((0, distance), (1, -distance)):
        for i in range(4):
            j = (i + turn) % 4
            pair = (i * 2 + core, j * 2 + core) if axis == "x" else (core * 4 + i, core * 4 + j)
            route.append(pair)
    return lax.ppermute(x, axes, route)


def per_device(inputs, in_weight, short_kernel, filter_one, filter_two, out_weight, out_grad):
    width = out_weight.shape[0]
    rows = inputs.shape[1]
    devices = lax.axis_size(everyone)
    scale = 1.0 / math.sqrt(devices * rows)
    shape = jax.ShapeDtypeStruct
    f32, bf16 = jnp.float32, jnp.bfloat16
    packed, both = call(
        pack_kernel,
        (shape((width, 2, 3 * rows), bf16), shape((rows, 2 * width), bf16)),
        [pltpu.VMEM((3, 2 * width, rows), f32)],
        limit=56 * 1024 * 1024,
    )(inputs, in_weight, filter_one, filter_two, out_weight, out_grad)
    received = exchange(packed, everyone)
    gathered = [both] + [ring(both, "y", distance) for distance in (1, 2, 3)]
    gathered += [swap_core(x) for x in gathered]
    tables = [jnp.asarray(t) for t in transform_tables(devices // 2, rows)]
    back = call(
        convolve_kernel,
        shape((32, 2, 25 * rows), bf16),
        [pltpu.VMEM((3, 2 * devices, rows), f32)],
        in_specs=specs(*[pltpu.VMEM] * (2 + len(tables)), *[pl.ANY] * 2),
    )(received, short_kernel, *tables, gathered[1], gathered[3])
    halfway = exchange(back, ("zh", "x", "zl"))
    found = call(
        part_kernel,
        (shape((32, width), f32),) * 4 + (shape((2, 7 * 32, rows), bf16),) * 4,
        [pltpu.VMEM((25, 64, rows), f32), pltpu.VMEM((4, 32, width), f32)],
    )(halfway, *gathered)
    part = [found[0]] + [ring(found[distance], "x", distance) for distance in (1, 2, 3)]
    arrived = [found[4]] + [ring(found[4 + i], "y", i) for i in (1, 2, 3)]
    arrived += [swap_core(x) for x in arrived]
    part = call(add_x_kernel, shape((8, 64, rows), bf16))(*part)
    part = exchange(part, ("zh", "zl"))
    part = call(
        functools.partial(add_z_kernel, scale),
        shape((16, 64, rows), bf16),
        in_specs=specs(pltpu.VMEM, *[pl.ANY] * 4),
    )(part, *arrived[4:])
    part = exchange(part, ("x", "y"))
    outputs, grad_inputs, grad_short, grad_one, grad_two = call(
        finish_kernel,
        (
            shape((1, rows, width), bf16),
            shape((1, rows, width), bf16),
            shape((3, 3 * width), f32),
            shape((rows, width), f32),
            shape((rows, width), f32),
        ),
    )(*arrived, in_weight, out_weight)
    part, grad_short = lax.optimization_barrier((part, grad_short))
    grad_in_weight, grad_out_weight = call(
        place_kernel, (shape((width, 3 * width), f32), shape((width, width), f32))
    )(part, swap_core(part))
    return (
        outputs,
        grad_inputs,
        grad_in_weight,
        grad_short,
        grad_one,
        grad_two,
        grad_out_weight,
    )


def solution(mesh):
    mesh = Mesh(mesh.devices.reshape(2, 4, 2, 4, 4), everyone)
    positions = ("x", "core", "zl", "y")
    split_rows, split_filter = P("zh", positions, None), P(positions, None)
    return jax.shard_map(
        per_device,
        mesh=mesh,
        in_specs=(split_rows, P(), P(), split_filter, split_filter, P(), split_rows),
        out_specs=(split_rows, split_rows, P(), P(), split_filter, split_filter, P()),
        check_vma=False,
    )
```

```python
import functools
import math

import jax
import jax.numpy as jnp
import numpy as np
from jax import lax
from jax.experimental import pallas as pl
from jax.experimental.pallas import tpu as pltpu
from jax.sharding import Mesh
from jax.sharding import PartitionSpec as P

everyone = ("zh", "x", "core", "zl", "y")
vmem_limit = 16 * 1024 * 1024


def two_terms(table):
    high = table.astype(np.float32).astype(jnp.bfloat16)
    low = (table - high.astype(np.float64)).astype(np.float32).astype(jnp.bfloat16)
    return high, low


def left_table(table):
    high, low = two_terms(table)
    return np.concatenate([high, low, high], 1)


def right_table(table):
    high, low = two_terms(table)
    return np.concatenate([high, low, high], 0)


def transform_tables(blocks, rows):
    length = 2 * blocks * rows
    outer = np.arange(blocks) + 0.5
    step = 2.0 * math.pi * np.outer(outer, np.arange(blocks)) / (2 * blocks)
    turn = 2.0 * math.pi * np.outer(outer, np.arange(rows)) / length
    inner = 2.0 * math.pi * np.outer(np.arange(rows), np.arange(rows)) / rows
    first = np.concatenate([np.cos(step), -np.sin(step)], 0)
    c, s = np.cos(inner), np.sin(inner)
    second = np.block([[c, -s], [s, c]])
    second_back = np.block([[c, s], [-s, c]])
    first_back = np.concatenate([np.cos(step).T, -np.sin(step).T], 1) * (2.0 / length)
    return [
        left_table(first),
        right_table(second),
        right_table(second_back),
        left_table(first_back),
        np.cos(turn).astype(np.float32),
        np.sin(turn).astype(np.float32),
    ]


def bf16_dot(a, b):
    return jnp.dot(a, b, preferred_element_type=jnp.float32)


def split(x):
    high = x.astype(jnp.bfloat16)
    low = (x - high.astype(jnp.float32)).astype(jnp.bfloat16)
    return high, low


def table_left(table, x):
    x_high, x_low = split(x)
    return bf16_dot(table, jnp.concatenate([x_high, x_high, x_low], 0))


def table_right(x, table):
    x_high, x_low = split(x)
    return bf16_dot(jnp.concatenate([x_high, x_high, x_low], 1), table)


def pack_kernel(seq_ref, in_weight_ref, one_ref, two_ref, out_weight_ref, grad_ref, out_ref, both_ref, rows_ref):
    width = out_weight_ref.shape[0]
    lanes = rows_ref.shape[2]
    contract_first = (((0,), (1,)), ((), ()))
    contract_last = (((1,), (1,)), ((), ()))
    seq = seq_ref[0]

    def put(index, x):
        rows_ref[index // 2, pl.ds(index % 2, width, stride=2), :] = x

    for group in range(3):
        weight = in_weight_ref[:, group * width : (group + 1) * width]
        put(
            group,
            lax.dot_general(weight, seq, contract_first, preferred_element_type=jnp.float32),
        )
    put(
        3,
        lax.dot_general(
            out_weight_ref[...], grad_ref[0], contract_last, preferred_element_type=jnp.float32
        ),
    )
    chosen = jnp.where(lax.axis_index("zh") == 0, one_ref[...], two_ref[...]).T
    high = chosen.astype(jnp.bfloat16).astype(jnp.float32)
    put(4, high)
    put(5, chosen - high)
    both_ref[:, :width] = seq
    both_ref[:, width:] = grad_ref[0]
    for pair in range(3):
        out_ref[:, :, pair * lanes : (pair + 1) * lanes] = (
            rows_ref[pair].reshape(width, 2, lanes).astype(jnp.bfloat16)
        )


def convolve_kernel(
    in_ref,
    short_ref,
    first_ref,
    second_ref,
    second_back_ref,
    first_back_ref,
    turn_cos_ref,
    turn_sin_ref,
    *rest,
):
    out_ref, rows_ref = rest[-2:]
    sources, rows = in_ref.shape[0], in_ref.shape[2] // 3
    blocks = sources // 2
    width = short_ref.shape[1] // 3
    scale = 1.0 / math.sqrt(sources * rows)
    turn_cos = turn_cos_ref[...]
    turn_sin = turn_sin_ref[...]
    lane = lax.broadcasted_iota(jnp.int32, (blocks, rows), 1)
    block = lax.broadcasted_iota(jnp.int32, (blocks, rows), 0)

    for pair in range(3):
        rows_ref[pair] = (
            in_ref[:, :, pair * rows : (pair + 1) * rows]
            .astype(jnp.float32)
            .reshape(sources * 2, rows)
        )

    def row(member, index):
        return rows_ref[index // 2, pl.ds(member * sources + index % 2, blocks, stride=2), :]

    def later(x, distance):
        moved = pltpu.roll(x, distance, 1)
        carried = jnp.where(block == 0, 0.0, pltpu.roll(moved, 1, 0))
        return jnp.where(lane < distance, carried, moved)

    def earlier(x, distance):
        moved = pltpu.roll(x, rows - distance, 1)
        carried = jnp.where(block == blocks - 1, 0.0, pltpu.roll(moved, blocks - 1, 0))
        return jnp.where(lane >= rows - distance, carried, moved)

    def forward(signals):
        outer = table_left(first_ref[...], jnp.concatenate(signals, 1))
        turned = []
        for i in range(len(signals)):
            re = outer[:blocks, i * rows : (i + 1) * rows]
            im = outer[blocks:, i * rows : (i + 1) * rows]
            turned.append(
                jnp.concatenate(
                    [re * turn_cos + im * turn_sin, im * turn_cos - re * turn_sin], 1
                )
            )
        inner = table_right(jnp.concatenate(turned, 0), second_ref[...])
        return [
            (inner[i * blocks : (i + 1) * blocks, :rows], inner[i * blocks : (i + 1) * blocks, rows:])
            for i in range(len(signals))
        ]

    def backward(spectra):
        stacked = jnp.concatenate([jnp.concatenate(pair, 1) for pair in spectra], 0)
        inner = table_right(stacked, second_back_ref[...])
        turned = []
        for i in range(len(spectra)):
            re = inner[i * blocks : (i + 1) * blocks, :rows]
            im = inner[i * blocks : (i + 1) * blocks, rows:]
            turned.append(
                jnp.concatenate(
                    [re * turn_cos - im * turn_sin, im * turn_cos + re * turn_sin], 0
                )
            )
        outer = table_left(first_back_ref[...], jnp.concatenate(turned, 1))
        return [outer[:, i * rows : (i + 1) * rows] for i in range(len(spectra))]

    def times(a, b):
        return a[0] * b[0] - a[1] * b[1], a[0] * b[1] + a[1] * b[0]

    def conj_times(a, b):
        return a[0] * b[0] + a[1] * b[1], a[0] * b[1] - a[1] * b[0]

    def added(a, b):
        return a[0] + b[0], a[1] + b[1]

    mesh_place = lax.axis_index(everyone)
    short = short_ref[...]
    short_lane = lax.broadcasted_iota(jnp.int32, short.shape, 1)
    taps = []
    for group in range(3):
        column = jnp.sum(
            jnp.where(short_lane == mesh_place + group * width, short, 0.0), axis=1, keepdims=True
        )
        taps.append([column[tap : tap + 1, :] for tap in range(3)])

    projected, lagged_one, lagged_two, mixed, pre = [], [], [], [], []
    for member in range(2):
        now = [row(member, group) for group in range(3)]
        one = [later(x, 1) for x in now]
        two = [later(x, 2) for x in now]
        projected.append(now)
        lagged_one.append(one)
        lagged_two.append(two)
        mixed.append(
            [
                taps[g][0] * now[g] + taps[g][1] * one[g] + taps[g][2] * two[g]
                for g in range(3)
            ]
        )
        pre.append(row(member, 3))
    members = range(2)
    grad_conv_two = [pre[m] * mixed[m][2] for m in members]
    spectra = forward(
        [row(m, 4) + row(m, 5) for m in members] + [mixed[m][0] for m in members] + grad_conv_two
    )
    one_spec, two_spec = spectra[0], spectra[1]
    value_spec, conv_two_spec = spectra[2:4], spectra[4:6]
    found = backward(
        [times(one_spec, value_spec[m]) for m in members]
        + [conj_times(two_spec, conv_two_spec[m]) for m in members]
    )
    conv_one, grad_gated = found[:2], found[2:]
    spectra = forward(
        [mixed[m][1] * conv_one[m] for m in members]
        + [mixed[m][1] * grad_gated[m] for m in members]
    )
    gated_spec, conv_one_spec = spectra[:2], spectra[2:]
    found = backward(
        [times(two_spec, gated_spec[m]) for m in members]
        + [conj_times(one_spec, conv_one_spec[m]) for m in members]
        + [
            added(*[conj_times(value_spec[m], conv_one_spec[m]) for m in members]),
            added(*[conj_times(gated_spec[m], conv_two_spec[m]) for m in members]),
        ]
    )
    conv_two, grad_value = found[:2], found[2:4]
    grad_filters = [found[4] * scale, found[5] * scale]

    new = lax.broadcasted_iota(jnp.int32, (blocks, blocks), 0)
    old = lax.broadcasted_iota(jnp.int32, (blocks, blocks), 1)
    wanted = (((new >> 3) & 3) << 5) | (((new >> 6) & 1) << 4) | (((new >> 1) & 3) << 2)
    wanted = wanted | (((new >> 5) & 1) << 1) | (new & 1)
    reorder = jnp.where(old == wanted, 1.0, 0.0).astype(jnp.bfloat16)
    sums = [[0.0] * 3 for _ in range(3)]
    for m in members:
        sent = [mixed[m][2] * conv_two[m]]
        grads = [grad_value[m], grad_gated[m] * conv_one[m], pre[m] * conv_two[m]]
        for g in range(3):
            sent.append(
                taps[g][0] * grads[g]
                + taps[g][1] * earlier(grads[g], 1)
                + taps[g][2] * earlier(grads[g], 2)
            )
            for tap, lagged in enumerate((projected, lagged_one, lagged_two)):
                sums[g][tap] = sums[g][tap] + jnp.sum(
                    jnp.sum(grads[g] * lagged[m][g], axis=0, keepdims=True), axis=1, keepdims=True
                )
        sent.extend(grad_filters)
        turned = bf16_dot(reorder, jnp.concatenate(sent, 1).astype(jnp.bfloat16))
        half = out_ref.shape[0] // 2
        count = 2 * half
        for index in range(len(sent)):
            for pair in range(4):
                place = (index * 4 + pair) * rows
                out_ref[m * half : (m + 1) * half, :, place : place + rows] = (
                    turned[pair * count : (pair + 1) * count, index * rows : (index + 1) * rows]
                    .reshape(half, 2, rows)
                    .astype(jnp.bfloat16)
                )
    shape = (2, rows)
    sum_lane = lax.broadcasted_iota(jnp.int32, shape, 1)
    line = jnp.zeros(shape, jnp.float32)
    for g in range(3):
        for tap in range(3):
            total = sums[g][tap] * scale
            high = total.astype(jnp.bfloat16).astype(jnp.float32)
            line = jnp.where(sum_lane == g * 3 + tap, high, line)
            line = jnp.where(sum_lane == 16 + g * 3 + tap, total - high, line)
    out_ref[:, :, 24 * rows :] = jnp.broadcast_to(line[None], (2 * half,) + shape).astype(
        jnp.bfloat16
    )


def channel_order(place_of):
    channel = lax.broadcasted_iota(jnp.int32, (256, 256), 0)
    row = lax.broadcasted_iota(jnp.int32, (256, 256), 1)
    zh, x, core = channel >> 7, (channel >> 5) & 3, (channel >> 4) & 1
    zl, y = (channel >> 2) & 3, channel & 3
    return jnp.where(row == place_of(zh, x, core, zl, y), 1.0, 0.0).astype(jnp.bfloat16)


def part_kernel(in_ref, *refs):
    both_refs, part_refs, send_refs = refs[:8], refs[8:12], refs[12:16]
    rows_ref, sums_ref = refs[16:]
    tiles, rows = rows_ref.shape[0], rows_ref.shape[2]
    sources = in_ref.shape[0]
    width = both_refs[0].shape[1] // 2
    x, core, y = lax.axis_index("x"), lax.axis_index("core"), lax.axis_index("y")
    turn = 1 - 2 * core
    for tile in range(tiles):
        rows_ref[tile] = (
            in_ref[:, :, tile * rows : (tile + 1) * rows]
            .astype(jnp.float32)
            .reshape(sources * 2, rows)
        )
    sums = rows_ref[tiles - 1, pl.ds(0, sources, stride=2), :]
    out_part = jnp.zeros((sources, width), jnp.float32)
    in_part = jnp.zeros((3 * sources, width), jnp.float32)
    for other in range(2):
        for ahead in range(4):
            block = (core ^ other) * 4 + ((y + turn * ahead) & 3)
            kept = [
                rows_ref[kind * 4 + (block >> 1), pl.ds(block & 1, sources, stride=2), :]
                for kind in range(6)
            ]
            kept = jnp.concatenate(kept + [sums], 0).astype(jnp.bfloat16)
            send_refs[ahead][other] = kept
            both_ref = both_refs[4 + ahead if other else (4 - ahead) % 4]
            out_part += bf16_dot(kept[:sources], both_ref[:, width:])
            in_part += bf16_dot(kept[sources : 4 * sources], both_ref[:, :width])
    sums_ref[0] = out_part
    for group in range(3):
        sums_ref[1 + group] = in_part[group * sources : (group + 1) * sources]
    for ahead in range(4):
        part_refs[ahead][...] = sums_ref[(x + turn * ahead) & 3]


def finish_kernel(*refs):
    held = refs[:8]
    in_weight_ref, out_weight_ref, outputs_ref, grad_inputs_ref, short_ref = refs[8:13]
    one_ref, two_ref = refs[13:]
    width = out_weight_ref.shape[0]
    count = width // 8
    core, y = lax.axis_index("core"), lax.axis_index("y")
    turn = 1 - 2 * core

    def row_of(zh, x, c, zl, v):
        other = c ^ core
        step = (turn * (1 - 2 * other) * (y - v)) & 3
        return (other * 4 + step) * 32 + (zh * 16 + x * 4 + zl)

    order = channel_order(row_of)
    contract_first = (((0,), (1,)), ((), ()))
    contract_last = (((1,), (1,)), ((), ()))

    def stacked_rows(kind):
        return jnp.concatenate(
            [held[i][i // 4, kind * count : (kind + 1) * count, :] for i in range(8)], 0
        )

    def natural(kind):
        stacked = stacked_rows(kind)
        return lax.dot_general(
            stacked, order, contract_first, preferred_element_type=jnp.float32
        )

    outputs_ref[0] = bf16_dot(natural(0).astype(jnp.bfloat16), out_weight_ref[...]).astype(
        jnp.bfloat16
    )
    total = None
    for group in range(3):
        term = lax.dot_general(
            natural(1 + group).astype(jnp.bfloat16),
            in_weight_ref[:, group * width : (group + 1) * width],
            contract_last,
            preferred_element_type=jnp.float32,
        )
        total = term if total is None else total + term
    grad_inputs_ref[0] = total.astype(jnp.bfloat16)
    one_ref[...] = natural(4)
    two_ref[...] = natural(5)
    sums = lax.dot_general(
        stacked_rows(6), order, contract_first, preferred_element_type=jnp.float32
    )
    for group in range(3):
        short_ref[:, group * width : (group + 1) * width] = (
            sums[group * 3 : group * 3 + 3, :] + sums[16 + group * 3 : 19 + group * 3, :]
        )


def add_x_kernel(*refs):
    out_ref = refs[7]
    total = refs[0][...] + refs[1][...] + refs[2][...] + refs[3][...]
    lanes = out_ref.shape[2]
    rows = jnp.concatenate([total[:, :lanes], total[:, lanes:]], 0)
    out_ref[...] = jnp.broadcast_to(rows.astype(jnp.bfloat16)[None], out_ref.shape)


def add_z_kernel(scale, in_ref, *refs):
    out_ref = refs[-1]
    total = jnp.sum(in_ref[...].astype(jnp.float32), axis=0) * scale
    out_ref[...] = jnp.broadcast_to(total.astype(jnp.bfloat16)[None], out_ref.shape)


def place_kernel(own_ref, other_ref, in_weight_ref, out_weight_ref):
    width, lanes = out_weight_ref.shape[0], own_ref.shape[2]
    core = lax.axis_index("core")
    order = channel_order(
        lambda zh, x, c, zl, y: ((c ^ core) * 4 + y) * 32 + (zh * 16 + x * 4 + zl)
    )
    contract_first = (((0,), (1,)), ((), ()))
    for kind in range(4):
        for half in range(2):
            stacked = jnp.concatenate(
                [
                    ref[kind * 4 + y, half * 32 : (half + 1) * 32, :]
                    for ref in (own_ref, other_ref)
                    for y in range(4)
                ],
                0,
            )
            if kind == 0:
                out_weight_ref[:, half * lanes : (half + 1) * lanes] = bf16_dot(order, stacked)
            else:
                in_weight_ref[
                    half * lanes : (half + 1) * lanes, (kind - 1) * width : kind * width
                ] = lax.dot_general(
                    stacked, order, contract_first, preferred_element_type=jnp.float32
                )


def call(kernel, out_shape, scratch=(), limit=vmem_limit, **options):
    return pl.pallas_call(
        kernel,
        out_shape=out_shape,
        scratch_shapes=list(scratch),
        compiler_params=pltpu.CompilerParams(vmem_limit_bytes=limit),
        **options,
    )


def specs(*spaces):
    return [pl.BlockSpec(memory_space=space) for space in spaces]


def exchange(x, axes):
    return lax.all_to_all(x, axes, split_axis=0, concat_axis=0, tiled=True)


def swap_core(x):
    return lax.ppermute(x, "core", [(0, 1), (1, 0)])


def ring(x, axis, distance):
    axes = ("x", "core") if axis == "x" else ("core", "y")
    route = []
    for core, turn in ((0, distance), (1, -distance)):
        for i in range(4):
            j = (i + turn) % 4
            pair = (i * 2 + core, j * 2 + core) if axis == "x" else (core * 4 + i, core * 4 + j)
            route.append(pair)
    return lax.ppermute(x, axes, route)


def per_device(inputs, in_weight, short_kernel, filter_one, filter_two, out_weight, out_grad):
    width = out_weight.shape[0]
    rows = inputs.shape[1]
    devices = lax.axis_size(everyone)
    scale = 1.0 / math.sqrt(devices * rows)
    shape = jax.ShapeDtypeStruct
    f32, bf16 = jnp.float32, jnp.bfloat16
    packed, both = call(
        pack_kernel,
        (shape((width, 2, 3 * rows), bf16), shape((rows, 2 * width), bf16)),
        [pltpu.VMEM((3, 2 * width, rows), f32)],
        limit=56 * 1024 * 1024,
    )(inputs, in_weight, filter_one, filter_two, out_weight, out_grad)
    received = exchange(packed, everyone)
    gathered = [both] + [ring(both, "y", distance) for distance in (1, 2, 3)]
    gathered += [swap_core(x) for x in gathered]
    tables = [jnp.asarray(t) for t in transform_tables(devices // 2, rows)]
    back = call(
        convolve_kernel,
        shape((32, 2, 25 * rows), bf16),
        [pltpu.VMEM((3, 2 * devices, rows), f32)],
        in_specs=specs(*[pltpu.VMEM] * (2 + len(tables)), *[pl.ANY] * 2),
    )(received, short_kernel, *tables, gathered[1], gathered[3])
    halfway = exchange(back, ("zh", "x", "zl"))
    found = call(
        part_kernel,
        (shape((32, width), f32),) * 4 + (shape((2, 7 * 32, rows), bf16),) * 4,
        [pltpu.VMEM((25, 64, rows), f32), pltpu.VMEM((4, 32, width), f32)],
    )(halfway, *gathered)
    part = [found[0]] + [ring(found[distance], "x", distance) for distance in (1, 2, 3)]
    leaving = found[5:]
    part, *leaving = call(
        add_x_kernel,
        (shape((8, 64, rows), bf16),) + (shape(leaving[0].shape, bf16),) * 3,
        in_specs=specs(*[pltpu.VMEM] * 4, *[pl.ANY] * 3),
        out_specs=specs(pltpu.VMEM, *[pl.ANY] * 3),
        input_output_aliases={4: 1, 5: 2, 6: 3},
    )(*part, *leaving)
    arrived = [found[4]] + [ring(x, "y", 1 + i) for i, x in enumerate(leaving)]
    part = exchange(part, ("zh", "zl"))
    part = call(
        functools.partial(add_z_kernel, scale),
        shape((16, 64, rows), bf16),
        in_specs=specs(pltpu.VMEM, *[pl.ANY] * 3),
    )(part, *arrived[1:])
    arrived += [swap_core(x) for x in arrived]
    part = exchange(part, ("x", "y"))
    outputs, grad_inputs, grad_short, grad_one, grad_two = call(
        finish_kernel,
        (
            shape((1, rows, width), bf16),
            shape((1, rows, width), bf16),
            shape((3, 3 * width), f32),
            shape((rows, width), f32),
            shape((rows, width), f32),
        ),
    )(*arrived, in_weight, out_weight)
    part, grad_short = lax.optimization_barrier((part, grad_short))
    grad_in_weight, grad_out_weight = call(
        place_kernel, (shape((width, 3 * width), f32), shape((width, width), f32))
    )(part, swap_core(part))
    return (
        outputs,
        grad_inputs,
        grad_in_weight,
        grad_short,
        grad_one,
        grad_two,
        grad_out_weight,
    )


def solution(mesh):
    mesh = Mesh(mesh.devices.reshape(2, 4, 2, 4, 4), everyone)
    positions = ("x", "core", "zl", "y")
    split_rows, split_filter = P("zh", positions, None), P(positions, None)
    return jax.shard_map(
        per_device,
        mesh=mesh,
        in_specs=(split_rows, P(), P(), split_filter, split_filter, P(), split_rows),
        out_specs=(split_rows, split_rows, P(), P(), split_filter, split_filter, P()),
        check_vma=False,
    )
```

```python
import functools
import math

import jax
import jax.numpy as jnp
import numpy as np
from jax import lax
from jax.experimental import pallas as pl
from jax.experimental.pallas import tpu as pltpu
from jax.sharding import Mesh
from jax.sharding import PartitionSpec as P

everyone = ("zh", "x", "core", "zl", "y")
vmem_limit = 16 * 1024 * 1024


def two_terms(table):
    high = table.astype(np.float32).astype(jnp.bfloat16)
    low = (table - high.astype(np.float64)).astype(np.float32).astype(jnp.bfloat16)
    return high, low


def left_table(table):
    high, low = two_terms(table)
    return np.concatenate([high, low, high], 1)


def right_table(table):
    high, low = two_terms(table)
    return np.concatenate([high, low, high], 0)


def transform_tables(blocks, rows):
    length = 2 * blocks * rows
    outer = np.arange(blocks) + 0.5
    step = 2.0 * math.pi * np.outer(outer, np.arange(blocks)) / (2 * blocks)
    turn = 2.0 * math.pi * np.outer(outer, np.arange(rows)) / length
    inner = 2.0 * math.pi * np.outer(np.arange(rows), np.arange(rows)) / rows
    first = np.concatenate([np.cos(step), -np.sin(step)], 0)
    c, s = np.cos(inner), np.sin(inner)
    second = np.block([[c, -s], [s, c]])
    second_back = np.block([[c, s], [-s, c]])
    first_back = np.concatenate([np.cos(step).T, -np.sin(step).T], 1) * (2.0 / length)
    return [
        left_table(first),
        right_table(second),
        right_table(second_back),
        left_table(first_back),
        np.cos(turn).astype(np.float32),
        np.sin(turn).astype(np.float32),
    ]


def bf16_dot(a, b):
    return jnp.dot(a, b, preferred_element_type=jnp.float32)


def split(x):
    high = x.astype(jnp.bfloat16)
    low = (x - high.astype(jnp.float32)).astype(jnp.bfloat16)
    return high, low


def table_left(table, x):
    x_high, x_low = split(x)
    return bf16_dot(table, jnp.concatenate([x_high, x_high, x_low], 0))


def table_right(x, table):
    x_high, x_low = split(x)
    return bf16_dot(jnp.concatenate([x_high, x_high, x_low], 1), table)


def pack_kernel(seq_ref, in_weight_ref, one_ref, two_ref, out_weight_ref, grad_ref, out_ref, both_ref, rows_ref):
    width = out_weight_ref.shape[0]
    lanes = rows_ref.shape[2]
    contract_first = (((0,), (1,)), ((), ()))
    contract_last = (((1,), (1,)), ((), ()))
    seq = seq_ref[0]

    def put(index, x):
        rows_ref[index // 2, pl.ds(index % 2, width, stride=2), :] = x

    for group in range(3):
        weight = in_weight_ref[:, group * width : (group + 1) * width]
        put(
            group,
            lax.dot_general(weight, seq, contract_first, preferred_element_type=jnp.float32),
        )
    put(
        3,
        lax.dot_general(
            out_weight_ref[...], grad_ref[0], contract_last, preferred_element_type=jnp.float32
        ),
    )
    chosen = jnp.where(lax.axis_index("zh") == 0, one_ref[...], two_ref[...]).T
    high = chosen.astype(jnp.bfloat16).astype(jnp.float32)
    put(4, high)
    put(5, chosen - high)
    both_ref[:, :width] = seq
    both_ref[:, width:] = grad_ref[0]
    for pair in range(3):
        out_ref[:, :, pair * lanes : (pair + 1) * lanes] = (
            rows_ref[pair].reshape(width, 2, lanes).astype(jnp.bfloat16)
        )


def convolve_kernel(
    in_ref,
    short_ref,
    first_ref,
    second_ref,
    second_back_ref,
    first_back_ref,
    turn_cos_ref,
    turn_sin_ref,
    *rest,
):
    out_ref, rows_ref = rest[-2:]
    sources, rows = in_ref.shape[0], in_ref.shape[2] // 3
    blocks = sources // 2
    width = short_ref.shape[1] // 3
    scale = 1.0 / math.sqrt(sources * rows)
    turn_cos = turn_cos_ref[...]
    turn_sin = turn_sin_ref[...]
    lane = lax.broadcasted_iota(jnp.int32, (blocks, rows), 1)
    block = lax.broadcasted_iota(jnp.int32, (blocks, rows), 0)

    for pair in range(3):
        rows_ref[pair] = (
            in_ref[:, :, pair * rows : (pair + 1) * rows]
            .astype(jnp.float32)
            .reshape(sources * 2, rows)
        )

    def row(member, index):
        return rows_ref[index // 2, pl.ds(member * sources + index % 2, blocks, stride=2), :]

    def later(x, distance):
        moved = pltpu.roll(x, distance, 1)
        carried = jnp.where(block == 0, 0.0, pltpu.roll(moved, 1, 0))
        return jnp.where(lane < distance, carried, moved)

    def earlier(x, distance):
        moved = pltpu.roll(x, rows - distance, 1)
        carried = jnp.where(block == blocks - 1, 0.0, pltpu.roll(moved, blocks - 1, 0))
        return jnp.where(lane >= rows - distance, carried, moved)

    def forward(signals):
        outer = table_left(first_ref[...], jnp.concatenate(signals, 1))
        turned = []
        for i in range(len(signals)):
            re = outer[:blocks, i * rows : (i + 1) * rows]
            im = outer[blocks:, i * rows : (i + 1) * rows]
            turned.append(
                jnp.concatenate(
                    [re * turn_cos + im * turn_sin, im * turn_cos - re * turn_sin], 1
                )
            )
        inner = table_right(jnp.concatenate(turned, 0), second_ref[...])
        return [
            (inner[i * blocks : (i + 1) * blocks, :rows], inner[i * blocks : (i + 1) * blocks, rows:])
            for i in range(len(signals))
        ]

    def backward(spectra):
        stacked = jnp.concatenate([jnp.concatenate(pair, 1) for pair in spectra], 0)
        inner = table_right(stacked, second_back_ref[...])
        turned = []
        for i in range(len(spectra)):
            re = inner[i * blocks : (i + 1) * blocks, :rows]
            im = inner[i * blocks : (i + 1) * blocks, rows:]
            turned.append(
                jnp.concatenate(
                    [re * turn_cos - im * turn_sin, im * turn_cos + re * turn_sin], 0
                )
            )
        outer = table_left(first_back_ref[...], jnp.concatenate(turned, 1))
        return [outer[:, i * rows : (i + 1) * rows] for i in range(len(spectra))]

    def times(a, b):
        return a[0] * b[0] - a[1] * b[1], a[0] * b[1] + a[1] * b[0]

    def conj_times(a, b):
        return a[0] * b[0] + a[1] * b[1], a[0] * b[1] - a[1] * b[0]

    def added(a, b):
        return a[0] + b[0], a[1] + b[1]

    mesh_place = lax.axis_index(everyone)
    short = short_ref[...]
    short_lane = lax.broadcasted_iota(jnp.int32, short.shape, 1)
    taps = []
    for group in range(3):
        column = jnp.sum(
            jnp.where(short_lane == mesh_place + group * width, short, 0.0), axis=1, keepdims=True
        )
        taps.append([column[tap : tap + 1, :] for tap in range(3)])

    projected, lagged_one, lagged_two, mixed, pre = [], [], [], [], []
    for member in range(2):
        now = [row(member, group) for group in range(3)]
        one = [later(x, 1) for x in now]
        two = [later(x, 2) for x in now]
        projected.append(now)
        lagged_one.append(one)
        lagged_two.append(two)
        mixed.append(
            [
                taps[g][0] * now[g] + taps[g][1] * one[g] + taps[g][2] * two[g]
                for g in range(3)
            ]
        )
        pre.append(row(member, 3))
    members = range(2)
    grad_conv_two = [pre[m] * mixed[m][2] for m in members]
    spectra = forward(
        [row(m, 4) + row(m, 5) for m in members] + [mixed[m][0] for m in members] + grad_conv_two
    )
    one_spec, two_spec = spectra[0], spectra[1]
    value_spec, conv_two_spec = spectra[2:4], spectra[4:6]
    found = backward(
        [times(one_spec, value_spec[m]) for m in members]
        + [conj_times(two_spec, conv_two_spec[m]) for m in members]
    )
    conv_one, grad_gated = found[:2], found[2:]
    spectra = forward(
        [mixed[m][1] * conv_one[m] for m in members]
        + [mixed[m][1] * grad_gated[m] for m in members]
    )
    gated_spec, conv_one_spec = spectra[:2], spectra[2:]
    found = backward(
        [times(two_spec, gated_spec[m]) for m in members]
        + [conj_times(one_spec, conv_one_spec[m]) for m in members]
        + [
            added(*[conj_times(value_spec[m], conv_one_spec[m]) for m in members]),
            added(*[conj_times(gated_spec[m], conv_two_spec[m]) for m in members]),
        ]
    )
    conv_two, grad_value = found[:2], found[2:4]
    grad_filters = [found[4] * scale, found[5] * scale]

    new = lax.broadcasted_iota(jnp.int32, (blocks, blocks), 0)
    old = lax.broadcasted_iota(jnp.int32, (blocks, blocks), 1)
    wanted = (((new >> 3) & 3) << 5) | (((new >> 6) & 1) << 4) | (((new >> 1) & 3) << 2)
    wanted = wanted | (((new >> 5) & 1) << 1) | (new & 1)
    reorder = jnp.where(old == wanted, 1.0, 0.0).astype(jnp.bfloat16)
    sums = [[0.0] * 3 for _ in range(3)]
    for m in members:
        sent = [mixed[m][2] * conv_two[m]]
        grads = [grad_value[m], grad_gated[m] * conv_one[m], pre[m] * conv_two[m]]
        for g in range(3):
            sent.append(
                taps[g][0] * grads[g]
                + taps[g][1] * earlier(grads[g], 1)
                + taps[g][2] * earlier(grads[g], 2)
            )
            for tap, lagged in enumerate((projected, lagged_one, lagged_two)):
                sums[g][tap] = sums[g][tap] + jnp.sum(
                    jnp.sum(grads[g] * lagged[m][g], axis=0, keepdims=True), axis=1, keepdims=True
                )
        sent.extend(grad_filters)
        turned = bf16_dot(reorder, jnp.concatenate(sent, 1).astype(jnp.bfloat16))
        half = out_ref.shape[0] // 2
        count = 2 * half
        for index in range(len(sent)):
            for pair in range(4):
                place = (index * 4 + pair) * rows
                out_ref[m * half : (m + 1) * half, :, place : place + rows] = (
                    turned[pair * count : (pair + 1) * count, index * rows : (index + 1) * rows]
                    .reshape(half, 2, rows)
                    .astype(jnp.bfloat16)
                )
    shape = (2, rows)
    sum_lane = lax.broadcasted_iota(jnp.int32, shape, 1)
    line = jnp.zeros(shape, jnp.float32)
    for g in range(3):
        for tap in range(3):
            total = sums[g][tap] * scale
            high = total.astype(jnp.bfloat16).astype(jnp.float32)
            line = jnp.where(sum_lane == g * 3 + tap, high, line)
            line = jnp.where(sum_lane == 16 + g * 3 + tap, total - high, line)
    out_ref[:, :, 24 * rows :] = jnp.broadcast_to(line[None], (2 * half,) + shape).astype(
        jnp.bfloat16
    )


def channel_order(place_of):
    channel = lax.broadcasted_iota(jnp.int32, (256, 256), 0)
    row = lax.broadcasted_iota(jnp.int32, (256, 256), 1)
    zh, x, core = channel >> 7, (channel >> 5) & 3, (channel >> 4) & 1
    zl, y = (channel >> 2) & 3, channel & 3
    return jnp.where(row == place_of(zh, x, core, zl, y), 1.0, 0.0).astype(jnp.bfloat16)


def part_kernel(in_ref, *refs):
    both_refs, part_refs, send_refs = refs[:8], refs[8:12], refs[12:16]
    rows_ref, sums_ref = refs[16:]
    tiles, rows = rows_ref.shape[0], rows_ref.shape[2]
    sources = in_ref.shape[0]
    width = both_refs[0].shape[1] // 2
    x, core, y = lax.axis_index("x"), lax.axis_index("core"), lax.axis_index("y")
    turn = 1 - 2 * core
    for tile in range(tiles):
        rows_ref[tile] = (
            in_ref[:, :, tile * rows : (tile + 1) * rows]
            .astype(jnp.float32)
            .reshape(sources * 2, rows)
        )
    sums = rows_ref[tiles - 1, pl.ds(0, sources, stride=2), :]
    out_part = jnp.zeros((sources, width), jnp.float32)
    in_part = jnp.zeros((3 * sources, width), jnp.float32)
    for other in range(2):
        for ahead in range(4):
            block = (core ^ other) * 4 + ((y + turn * ahead) & 3)
            kept = [
                rows_ref[kind * 4 + (block >> 1), pl.ds(block & 1, sources, stride=2), :]
                for kind in range(6)
            ]
            kept = jnp.concatenate(kept + [sums], 0).astype(jnp.bfloat16)
            send_refs[ahead][other] = kept
            both_ref = both_refs[4 + ahead if other else (4 - ahead) % 4]
            out_part += bf16_dot(kept[:sources], both_ref[:, width:])
            in_part += bf16_dot(kept[sources : 4 * sources], both_ref[:, :width])
    sums_ref[0] = out_part
    for group in range(3):
        sums_ref[1 + group] = in_part[group * sources : (group + 1) * sources]
    for ahead in range(4):
        part_refs[ahead][...] = sums_ref[(x + turn * ahead) & 3]


def finish_kernel(*refs):
    held = refs[:8]
    in_weight_ref, out_weight_ref, outputs_ref, grad_inputs_ref, short_ref = refs[8:13]
    one_ref, two_ref = refs[13:]
    width = out_weight_ref.shape[0]
    count = width // 8
    core, y = lax.axis_index("core"), lax.axis_index("y")
    turn = 1 - 2 * core

    def row_of(zh, x, c, zl, v):
        other = c ^ core
        step = (turn * (1 - 2 * other) * (y - v)) & 3
        return (other * 4 + step) * 32 + (zh * 16 + x * 4 + zl)

    order = channel_order(row_of)
    contract_first = (((0,), (1,)), ((), ()))
    contract_last = (((1,), (1,)), ((), ()))

    def stacked_rows(kind):
        return jnp.concatenate(
            [held[i][i // 4, kind * count : (kind + 1) * count, :] for i in range(8)], 0
        )

    def natural(kind):
        stacked = stacked_rows(kind)
        return lax.dot_general(
            stacked, order, contract_first, preferred_element_type=jnp.float32
        )

    outputs_ref[0] = bf16_dot(natural(0).astype(jnp.bfloat16), out_weight_ref[...]).astype(
        jnp.bfloat16
    )
    total = None
    for group in range(3):
        term = lax.dot_general(
            natural(1 + group).astype(jnp.bfloat16),
            in_weight_ref[:, group * width : (group + 1) * width],
            contract_last,
            preferred_element_type=jnp.float32,
        )
        total = term if total is None else total + term
    grad_inputs_ref[0] = total.astype(jnp.bfloat16)
    one_ref[...] = natural(4)
    two_ref[...] = natural(5)
    sums = lax.dot_general(
        stacked_rows(6), order, contract_first, preferred_element_type=jnp.float32
    )
    for group in range(3):
        short_ref[:, group * width : (group + 1) * width] = (
            sums[group * 3 : group * 3 + 3, :] + sums[16 + group * 3 : 19 + group * 3, :]
        )


def add_x_kernel(*refs):
    out_ref = refs[6]
    total = refs[0][...] + refs[1][...] + refs[2][...] + refs[3][...]
    lanes = out_ref.shape[2]
    rows = jnp.concatenate([total[:, :lanes], total[:, lanes:]], 0)
    out_ref[...] = jnp.broadcast_to(rows.astype(jnp.bfloat16)[None], out_ref.shape)


def add_z_kernel(scale, in_ref, *refs):
    out_ref = refs[-1]
    total = jnp.sum(in_ref[...].astype(jnp.float32), axis=0) * scale
    out_ref[...] = jnp.broadcast_to(total.astype(jnp.bfloat16)[None], out_ref.shape)


def place_kernel(own_ref, other_ref, in_weight_ref, out_weight_ref):
    width, lanes = out_weight_ref.shape[0], own_ref.shape[2]
    core = lax.axis_index("core")
    order = channel_order(
        lambda zh, x, c, zl, y: ((c ^ core) * 4 + y) * 32 + (zh * 16 + x * 4 + zl)
    )
    contract_first = (((0,), (1,)), ((), ()))
    for kind in range(4):
        for half in range(2):
            stacked = jnp.concatenate(
                [
                    ref[kind * 4 + y, half * 32 : (half + 1) * 32, :]
                    for ref in (own_ref, other_ref)
                    for y in range(4)
                ],
                0,
            )
            if kind == 0:
                out_weight_ref[:, half * lanes : (half + 1) * lanes] = bf16_dot(order, stacked)
            else:
                in_weight_ref[
                    half * lanes : (half + 1) * lanes, (kind - 1) * width : kind * width
                ] = lax.dot_general(
                    stacked, order, contract_first, preferred_element_type=jnp.float32
                )


def call(kernel, out_shape, scratch=(), limit=vmem_limit, **options):
    return pl.pallas_call(
        kernel,
        out_shape=out_shape,
        scratch_shapes=list(scratch),
        compiler_params=pltpu.CompilerParams(vmem_limit_bytes=limit),
        **options,
    )


def specs(*spaces):
    return [pl.BlockSpec(memory_space=space) for space in spaces]


def exchange(x, axes):
    return lax.all_to_all(x, axes, split_axis=0, concat_axis=0, tiled=True)


def swap_core(x):
    return lax.ppermute(x, "core", [(0, 1), (1, 0)])


def ring(x, axis, distance):
    axes = ("x", "core") if axis == "x" else ("core", "y")
    route = []
    for core, turn in ((0, distance), (1, -distance)):
        for i in range(4):
            j = (i + turn) % 4
            pair = (i * 2 + core, j * 2 + core) if axis == "x" else (core * 4 + i, core * 4 + j)
            route.append(pair)
    return lax.ppermute(x, axes, route)


def per_device(inputs, in_weight, short_kernel, filter_one, filter_two, out_weight, out_grad):
    width = out_weight.shape[0]
    rows = inputs.shape[1]
    devices = lax.axis_size(everyone)
    scale = 1.0 / math.sqrt(devices * rows)
    shape = jax.ShapeDtypeStruct
    f32, bf16 = jnp.float32, jnp.bfloat16
    packed, both = call(
        pack_kernel,
        (shape((width, 2, 3 * rows), bf16), shape((rows, 2 * width), bf16)),
        [pltpu.VMEM((3, 2 * width, rows), f32)],
        limit=56 * 1024 * 1024,
    )(inputs, in_weight, filter_one, filter_two, out_weight, out_grad)
    received = exchange(packed, everyone)
    gathered = [both] + [ring(both, "y", distance) for distance in (1, 2, 3)]
    gathered += [swap_core(x) for x in gathered]
    tables = [jnp.asarray(t) for t in transform_tables(devices // 2, rows)]
    back = call(
        convolve_kernel,
        shape((32, 2, 25 * rows), bf16),
        [pltpu.VMEM((3, 2 * devices, rows), f32)],
        in_specs=specs(*[pltpu.VMEM] * (2 + len(tables)), *[pl.ANY] * 2),
    )(received, short_kernel, *tables, gathered[1], gathered[3])
    halfway = exchange(back, ("zh", "x", "zl"))
    found = call(
        part_kernel,
        (shape((32, width), f32),) * 4 + (shape((2, 7 * 32, rows), bf16),) * 4,
        [pltpu.VMEM((25, 64, rows), f32), pltpu.VMEM((4, 32, width), f32)],
    )(halfway, *gathered)
    part = [found[0]] + [ring(found[distance], "x", distance) for distance in (1, 2, 3)]
    far = ring(found[6], "y", 2)
    part, *leaving = call(
        add_x_kernel,
        (shape((8, 64, rows), bf16),) + (shape(found[5].shape, bf16),) * 2,
        in_specs=specs(*[pltpu.VMEM] * 4, *[pl.ANY] * 2),
        out_specs=specs(pltpu.VMEM, *[pl.ANY] * 2),
        input_output_aliases={4: 1, 5: 2},
    )(*part, found[5], found[7])
    arrived = [found[4], ring(leaving[0], "y", 1), far, ring(leaving[1], "y", 3)]
    arrived += [swap_core(x) for x in arrived]
    part = exchange(part, ("zh", "zl"))
    part = call(
        functools.partial(add_z_kernel, scale),
        shape((16, 64, rows), bf16),
        in_specs=specs(pltpu.VMEM, *[pl.ANY] * 3),
    )(part, arrived[1], arrived[3], arrived[6])
    part = exchange(part, ("x", "y"))
    outputs, grad_inputs, grad_short, grad_one, grad_two = call(
        finish_kernel,
        (
            shape((1, rows, width), bf16),
            shape((1, rows, width), bf16),
            shape((3, 3 * width), f32),
            shape((rows, width), f32),
            shape((rows, width), f32),
        ),
    )(*arrived, in_weight, out_weight)
    part, grad_short = lax.optimization_barrier((part, grad_short))
    grad_in_weight, grad_out_weight = call(
        place_kernel, (shape((width, 3 * width), f32), shape((width, width), f32))
    )(part, swap_core(part))
    return (
        outputs,
        grad_inputs,
        grad_in_weight,
        grad_short,
        grad_one,
        grad_two,
        grad_out_weight,
    )


def solution(mesh):
    mesh = Mesh(mesh.devices.reshape(2, 4, 2, 4, 4), everyone)
    positions = ("x", "core", "zl", "y")
    split_rows, split_filter = P("zh", positions, None), P(positions, None)
    return jax.shard_map(
        per_device,
        mesh=mesh,
        in_specs=(split_rows, P(), P(), split_filter, split_filter, P(), split_rows),
        out_specs=(split_rows, split_rows, P(), P(), split_filter, split_filter, P()),
        check_vma=False,
    )
```

```python
import functools
import math

import jax
import jax.numpy as jnp
import numpy as np
from jax import lax
from jax.experimental import pallas as pl
from jax.experimental.pallas import tpu as pltpu
from jax.sharding import Mesh
from jax.sharding import PartitionSpec as P

everyone = ("zh", "x", "core", "zl", "y")
vmem_limit = 16 * 1024 * 1024


def two_terms(table):
    high = table.astype(np.float32).astype(jnp.bfloat16)
    low = (table - high.astype(np.float64)).astype(np.float32).astype(jnp.bfloat16)
    return high, low


def left_table(table):
    high, low = two_terms(table)
    return np.concatenate([high, low, high], 1)


def right_table(table):
    high, low = two_terms(table)
    return np.concatenate([high, low, high], 0)


def transform_tables(blocks, rows):
    length = 2 * blocks * rows
    outer = np.arange(blocks) + 0.5
    step = 2.0 * math.pi * np.outer(outer, np.arange(blocks)) / (2 * blocks)
    turn = 2.0 * math.pi * np.outer(outer, np.arange(rows)) / length
    inner = 2.0 * math.pi * np.outer(np.arange(rows), np.arange(rows)) / rows
    first = np.concatenate([np.cos(step), -np.sin(step)], 0)
    c, s = np.cos(inner), np.sin(inner)
    second = np.block([[c, -s], [s, c]])
    second_back = np.block([[c, s], [-s, c]])
    first_back = np.concatenate([np.cos(step).T, -np.sin(step).T], 1) * (2.0 / length)
    return [
        left_table(first),
        right_table(second),
        right_table(second_back),
        left_table(first_back),
        np.cos(turn).astype(np.float32),
        np.sin(turn).astype(np.float32),
    ]


def bf16_dot(a, b):
    return jnp.dot(a, b, preferred_element_type=jnp.float32)


def split(x):
    high = x.astype(jnp.bfloat16)
    low = (x - high.astype(jnp.float32)).astype(jnp.bfloat16)
    return high, low


def table_left(table, x):
    x_high, x_low = split(x)
    return bf16_dot(table, jnp.concatenate([x_high, x_high, x_low], 0))


def table_right(x, table):
    x_high, x_low = split(x)
    return bf16_dot(jnp.concatenate([x_high, x_high, x_low], 1), table)


def pack_kernel(seq_ref, in_weight_ref, one_ref, two_ref, out_weight_ref, grad_ref, out_ref, both_ref, rows_ref):
    width = out_weight_ref.shape[0]
    lanes = rows_ref.shape[2]
    contract_first = (((0,), (1,)), ((), ()))
    contract_last = (((1,), (1,)), ((), ()))
    seq = seq_ref[0]

    def put(index, x):
        rows_ref[index // 2, pl.ds(index % 2, width, stride=2), :] = x

    for group in range(3):
        weight = in_weight_ref[:, group * width : (group + 1) * width]
        put(
            group,
            lax.dot_general(weight, seq, contract_first, preferred_element_type=jnp.float32),
        )
    put(
        3,
        lax.dot_general(
            out_weight_ref[...], grad_ref[0], contract_last, preferred_element_type=jnp.float32
        ),
    )
    chosen = jnp.where(lax.axis_index("zh") == 0, one_ref[...], two_ref[...]).T
    high = chosen.astype(jnp.bfloat16).astype(jnp.float32)
    put(4, high)
    put(5, chosen - high)
    both_ref[:, :width] = seq
    both_ref[:, width:] = grad_ref[0]
    for pair in range(3):
        out_ref[:, :, pair * lanes : (pair + 1) * lanes] = (
            rows_ref[pair].reshape(width, 2, lanes).astype(jnp.bfloat16)
        )


def convolve_kernel(
    in_ref,
    short_ref,
    first_ref,
    second_ref,
    second_back_ref,
    first_back_ref,
    turn_cos_ref,
    turn_sin_ref,
    *rest,
):
    out_ref, rows_ref = rest[-2:]
    sources, rows = in_ref.shape[0], in_ref.shape[2] // 3
    blocks = sources // 2
    width = short_ref.shape[1] // 3
    scale = 1.0 / math.sqrt(sources * rows)
    turn_cos = turn_cos_ref[...]
    turn_sin = turn_sin_ref[...]
    lane = lax.broadcasted_iota(jnp.int32, (blocks, rows), 1)
    block = lax.broadcasted_iota(jnp.int32, (blocks, rows), 0)

    for pair in range(3):
        rows_ref[pair] = (
            in_ref[:, :, pair * rows : (pair + 1) * rows]
            .astype(jnp.float32)
            .reshape(sources * 2, rows)
        )

    def row(member, index):
        return rows_ref[index // 2, pl.ds(member * sources + index % 2, blocks, stride=2), :]

    def later(x, distance):
        moved = pltpu.roll(x, distance, 1)
        carried = jnp.where(block == 0, 0.0, pltpu.roll(moved, 1, 0))
        return jnp.where(lane < distance, carried, moved)

    def earlier(x, distance):
        moved = pltpu.roll(x, rows - distance, 1)
        carried = jnp.where(block == blocks - 1, 0.0, pltpu.roll(moved, blocks - 1, 0))
        return jnp.where(lane >= rows - distance, carried, moved)

    def forward(signals):
        outer = table_left(first_ref[...], jnp.concatenate(signals, 1))
        turned = []
        for i in range(len(signals)):
            re = outer[:blocks, i * rows : (i + 1) * rows]
            im = outer[blocks:, i * rows : (i + 1) * rows]
            turned.append(
                jnp.concatenate(
                    [re * turn_cos + im * turn_sin, im * turn_cos - re * turn_sin], 1
                )
            )
        inner = table_right(jnp.concatenate(turned, 0), second_ref[...])
        return [
            (inner[i * blocks : (i + 1) * blocks, :rows], inner[i * blocks : (i + 1) * blocks, rows:])
            for i in range(len(signals))
        ]

    def backward(spectra):
        stacked = jnp.concatenate([jnp.concatenate(pair, 1) for pair in spectra], 0)
        inner = table_right(stacked, second_back_ref[...])
        turned = []
        for i in range(len(spectra)):
            re = inner[i * blocks : (i + 1) * blocks, :rows]
            im = inner[i * blocks : (i + 1) * blocks, rows:]
            turned.append(
                jnp.concatenate(
                    [re * turn_cos - im * turn_sin, im * turn_cos + re * turn_sin], 0
                )
            )
        outer = table_left(first_back_ref[...], jnp.concatenate(turned, 1))
        return [outer[:, i * rows : (i + 1) * rows] for i in range(len(spectra))]

    def times(a, b):
        return a[0] * b[0] - a[1] * b[1], a[0] * b[1] + a[1] * b[0]

    def conj_times(a, b):
        return a[0] * b[0] + a[1] * b[1], a[0] * b[1] - a[1] * b[0]

    def added(a, b):
        return a[0] + b[0], a[1] + b[1]

    mesh_place = lax.axis_index(everyone)
    short = short_ref[...]
    short_lane = lax.broadcasted_iota(jnp.int32, short.shape, 1)
    taps = []
    for group in range(3):
        column = jnp.sum(
            jnp.where(short_lane == mesh_place + group * width, short, 0.0), axis=1, keepdims=True
        )
        taps.append([column[tap : tap + 1, :] for tap in range(3)])

    projected, lagged_one, lagged_two, mixed, pre = [], [], [], [], []
    for member in range(2):
        now = [row(member, group) for group in range(3)]
        one = [later(x, 1) for x in now]
        two = [later(x, 2) for x in now]
        projected.append(now)
        lagged_one.append(one)
        lagged_two.append(two)
        mixed.append(
            [
                taps[g][0] * now[g] + taps[g][1] * one[g] + taps[g][2] * two[g]
                for g in range(3)
            ]
        )
        pre.append(row(member, 3))
    members = range(2)
    grad_conv_two = [pre[m] * mixed[m][2] for m in members]
    spectra = forward(
        [row(m, 4) + row(m, 5) for m in members] + [mixed[m][0] for m in members] + grad_conv_two
    )
    one_spec, two_spec = spectra[0], spectra[1]
    value_spec, conv_two_spec = spectra[2:4], spectra[4:6]
    found = backward(
        [times(one_spec, value_spec[m]) for m in members]
        + [conj_times(two_spec, conv_two_spec[m]) for m in members]
    )
    conv_one, grad_gated = found[:2], found[2:]
    spectra = forward(
        [mixed[m][1] * conv_one[m] for m in members]
        + [mixed[m][1] * grad_gated[m] for m in members]
    )
    gated_spec, conv_one_spec = spectra[:2], spectra[2:]
    found = backward(
        [times(two_spec, gated_spec[m]) for m in members]
        + [conj_times(one_spec, conv_one_spec[m]) for m in members]
        + [
            added(*[conj_times(value_spec[m], conv_one_spec[m]) for m in members]),
            added(*[conj_times(gated_spec[m], conv_two_spec[m]) for m in members]),
        ]
    )
    conv_two, grad_value = found[:2], found[2:4]
    grad_filters = [found[4] * scale, found[5] * scale]

    new = lax.broadcasted_iota(jnp.int32, (blocks, blocks), 0)
    old = lax.broadcasted_iota(jnp.int32, (blocks, blocks), 1)
    wanted = (((new >> 3) & 3) << 5) | (((new >> 6) & 1) << 4) | (((new >> 1) & 3) << 2)
    wanted = wanted | (((new >> 5) & 1) << 1) | (new & 1)
    reorder = jnp.where(old == wanted, 1.0, 0.0).astype(jnp.bfloat16)
    sums = [[0.0] * 3 for _ in range(3)]
    for m in members:
        sent = [mixed[m][2] * conv_two[m]]
        grads = [grad_value[m], grad_gated[m] * conv_one[m], pre[m] * conv_two[m]]
        for g in range(3):
            sent.append(
                taps[g][0] * grads[g]
                + taps[g][1] * earlier(grads[g], 1)
                + taps[g][2] * earlier(grads[g], 2)
            )
            for tap, lagged in enumerate((projected, lagged_one, lagged_two)):
                sums[g][tap] = sums[g][tap] + jnp.sum(
                    jnp.sum(grads[g] * lagged[m][g], axis=0, keepdims=True), axis=1, keepdims=True
                )
        sent.extend(grad_filters)
        turned = bf16_dot(reorder, jnp.concatenate(sent, 1).astype(jnp.bfloat16))
        half = out_ref.shape[0] // 2
        count = 2 * half
        for index in range(len(sent)):
            for pair in range(4):
                place = (index * 4 + pair) * rows
                out_ref[m * half : (m + 1) * half, :, place : place + rows] = (
                    turned[pair * count : (pair + 1) * count, index * rows : (index + 1) * rows]
                    .reshape(half, 2, rows)
                    .astype(jnp.bfloat16)
                )
    shape = (2, rows)
    sum_lane = lax.broadcasted_iota(jnp.int32, shape, 1)
    line = jnp.zeros(shape, jnp.float32)
    for g in range(3):
        for tap in range(3):
            total = sums[g][tap] * scale
            high = total.astype(jnp.bfloat16).astype(jnp.float32)
            line = jnp.where(sum_lane == g * 3 + tap, high, line)
            line = jnp.where(sum_lane == 16 + g * 3 + tap, total - high, line)
    out_ref[:, :, 24 * rows :] = jnp.broadcast_to(line[None], (2 * half,) + shape).astype(
        jnp.bfloat16
    )


def channel_order(place_of):
    channel = lax.broadcasted_iota(jnp.int32, (256, 256), 0)
    row = lax.broadcasted_iota(jnp.int32, (256, 256), 1)
    zh, x, core = channel >> 7, (channel >> 5) & 3, (channel >> 4) & 1
    zl, y = (channel >> 2) & 3, channel & 3
    return jnp.where(row == place_of(zh, x, core, zl, y), 1.0, 0.0).astype(jnp.bfloat16)


def part_kernel(in_ref, *refs):
    both_refs, part_refs, send_refs = refs[:8], refs[8:12], refs[12:16]
    rows_ref, sums_ref = refs[16:]
    tiles, rows = rows_ref.shape[0], rows_ref.shape[2]
    sources = in_ref.shape[0]
    width = both_refs[0].shape[1] // 2
    x, core, y = lax.axis_index("x"), lax.axis_index("core"), lax.axis_index("y")
    turn = 2 * core - 1
    for tile in range(tiles):
        rows_ref[tile] = (
            in_ref[:, :, tile * rows : (tile + 1) * rows]
            .astype(jnp.float32)
            .reshape(sources * 2, rows)
        )
    sums = rows_ref[tiles - 1, pl.ds(0, sources, stride=2), :]
    out_part = jnp.zeros((sources, width), jnp.float32)
    in_part = jnp.zeros((3 * sources, width), jnp.float32)
    for other in range(2):
        for ahead in range(4):
            block = (core ^ other) * 4 + ((y + turn * ahead) & 3)
            kept = [
                rows_ref[kind * 4 + (block >> 1), pl.ds(block & 1, sources, stride=2), :]
                for kind in range(6)
            ]
            kept = jnp.concatenate(kept + [sums], 0).astype(jnp.bfloat16)
            send_refs[ahead][other] = kept
            both_ref = both_refs[4 + ahead if other else (4 - ahead) % 4]
            out_part += bf16_dot(kept[:sources], both_ref[:, width:])
            in_part += bf16_dot(kept[sources : 4 * sources], both_ref[:, :width])
    sums_ref[0] = out_part
    for group in range(3):
        sums_ref[1 + group] = in_part[group * sources : (group + 1) * sources]
    for ahead in range(4):
        part_refs[ahead][...] = sums_ref[(x + turn * ahead) & 3]


def finish_kernel(*refs):
    held = refs[:8]
    in_weight_ref, out_weight_ref, outputs_ref, grad_inputs_ref, short_ref = refs[8:13]
    one_ref, two_ref = refs[13:]
    width = out_weight_ref.shape[0]
    count = width // 8
    core, y = lax.axis_index("core"), lax.axis_index("y")
    turn = 2 * core - 1

    def row_of(zh, x, c, zl, v):
        other = c ^ core
        step = (turn * (1 - 2 * other) * (y - v)) & 3
        return (other * 4 + step) * 32 + (zh * 16 + x * 4 + zl)

    order = channel_order(row_of)
    contract_first = (((0,), (1,)), ((), ()))
    contract_last = (((1,), (1,)), ((), ()))

    def stacked_rows(kind):
        return jnp.concatenate(
            [held[i][i // 4, kind * count : (kind + 1) * count, :] for i in range(8)], 0
        )

    def natural(kind):
        stacked = stacked_rows(kind)
        return lax.dot_general(
            stacked, order, contract_first, preferred_element_type=jnp.float32
        )

    outputs_ref[0] = bf16_dot(natural(0).astype(jnp.bfloat16), out_weight_ref[...]).astype(
        jnp.bfloat16
    )
    total = None
    for group in range(3):
        term = lax.dot_general(
            natural(1 + group).astype(jnp.bfloat16),
            in_weight_ref[:, group * width : (group + 1) * width],
            contract_last,
            preferred_element_type=jnp.float32,
        )
        total = term if total is None else total + term
    grad_inputs_ref[0] = total.astype(jnp.bfloat16)
    one_ref[...] = natural(4)
    two_ref[...] = natural(5)
    sums = lax.dot_general(
        stacked_rows(6), order, contract_first, preferred_element_type=jnp.float32
    )
    for group in range(3):
        short_ref[:, group * width : (group + 1) * width] = (
            sums[group * 3 : group * 3 + 3, :] + sums[16 + group * 3 : 19 + group * 3, :]
        )


def add_x_kernel(*refs):
    out_ref = refs[6]
    total = refs[0][...] + refs[1][...] + refs[2][...] + refs[3][...]
    lanes = out_ref.shape[2]
    rows = jnp.concatenate([total[:, :lanes], total[:, lanes:]], 0)
    out_ref[...] = jnp.broadcast_to(rows.astype(jnp.bfloat16)[None], out_ref.shape)


def add_z_kernel(scale, in_ref, *refs):
    out_ref = refs[-1]
    total = jnp.sum(in_ref[...].astype(jnp.float32), axis=0) * scale
    out_ref[...] = jnp.broadcast_to(total.astype(jnp.bfloat16)[None], out_ref.shape)


def place_kernel(own_ref, other_ref, in_weight_ref, out_weight_ref):
    width, lanes = out_weight_ref.shape[0], own_ref.shape[2]
    core = lax.axis_index("core")
    order = channel_order(
        lambda zh, x, c, zl, y: ((c ^ core) * 4 + y) * 32 + (zh * 16 + x * 4 + zl)
    )
    contract_first = (((0,), (1,)), ((), ()))
    for kind in range(4):
        for half in range(2):
            stacked = jnp.concatenate(
                [
                    ref[kind * 4 + y, half * 32 : (half + 1) * 32, :]
                    for ref in (own_ref, other_ref)
                    for y in range(4)
                ],
                0,
            )
            if kind == 0:
                out_weight_ref[:, half * lanes : (half + 1) * lanes] = bf16_dot(order, stacked)
            else:
                in_weight_ref[
                    half * lanes : (half + 1) * lanes, (kind - 1) * width : kind * width
                ] = lax.dot_general(
                    stacked, order, contract_first, preferred_element_type=jnp.float32
                )


def call(kernel, out_shape, scratch=(), limit=vmem_limit, **options):
    return pl.pallas_call(
        kernel,
        out_shape=out_shape,
        scratch_shapes=list(scratch),
        compiler_params=pltpu.CompilerParams(vmem_limit_bytes=limit),
        **options,
    )


def specs(*spaces):
    return [pl.BlockSpec(memory_space=space) for space in spaces]


def exchange(x, axes):
    return lax.all_to_all(x, axes, split_axis=0, concat_axis=0, tiled=True)


def swap_core(x):
    return lax.ppermute(x, "core", [(0, 1), (1, 0)])


def ring(x, axis, distance):
    axes = ("x", "core") if axis == "x" else ("core", "y")
    route = []
    for core, turn in ((0, -distance), (1, distance)):
        for i in range(4):
            j = (i + turn) % 4
            pair = (i * 2 + core, j * 2 + core) if axis == "x" else (core * 4 + i, core * 4 + j)
            route.append(pair)
    return lax.ppermute(x, axes, route)


def per_device(inputs, in_weight, short_kernel, filter_one, filter_two, out_weight, out_grad):
    width = out_weight.shape[0]
    rows = inputs.shape[1]
    devices = lax.axis_size(everyone)
    scale = 1.0 / math.sqrt(devices * rows)
    shape = jax.ShapeDtypeStruct
    f32, bf16 = jnp.float32, jnp.bfloat16
    packed, both = call(
        pack_kernel,
        (shape((width, 2, 3 * rows), bf16), shape((rows, 2 * width), bf16)),
        [pltpu.VMEM((3, 2 * width, rows), f32)],
        limit=56 * 1024 * 1024,
    )(inputs, in_weight, filter_one, filter_two, out_weight, out_grad)
    received = exchange(packed, everyone)
    gathered = [both] + [ring(both, "y", distance) for distance in (1, 2, 3)]
    gathered += [swap_core(x) for x in gathered]
    tables = [jnp.asarray(t) for t in transform_tables(devices // 2, rows)]
    back = call(
        convolve_kernel,
        shape((32, 2, 25 * rows), bf16),
        [pltpu.VMEM((3, 2 * devices, rows), f32)],
        in_specs=specs(*[pltpu.VMEM] * (2 + len(tables)), *[pl.ANY] * 2),
    )(received, short_kernel, *tables, gathered[1], gathered[3])
    halfway = exchange(back, ("zh", "x", "zl"))
    found = call(
        part_kernel,
        (shape((32, width), f32),) * 4 + (shape((2, 7 * 32, rows), bf16),) * 4,
        [pltpu.VMEM((25, 64, rows), f32), pltpu.VMEM((4, 32, width), f32)],
    )(halfway, *gathered)
    part = [found[0]] + [ring(found[distance], "x", distance) for distance in (1, 2, 3)]
    far = ring(found[6], "y", 2)
    part, *leaving = call(
        add_x_kernel,
        (shape((8, 64, rows), bf16),) + (shape(found[5].shape, bf16),) * 2,
        in_specs=specs(*[pltpu.VMEM] * 4, *[pl.ANY] * 2),
        out_specs=specs(pltpu.VMEM, *[pl.ANY] * 2),
        input_output_aliases={4: 1, 5: 2},
    )(*part, found[5], found[7])
    arrived = [found[4], ring(leaving[0], "y", 1), far, ring(leaving[1], "y", 3)]
    arrived += [swap_core(x) for x in arrived]
    part = exchange(part, ("zh", "zl"))
    part = call(
        functools.partial(add_z_kernel, scale),
        shape((16, 64, rows), bf16),
        in_specs=specs(pltpu.VMEM, *[pl.ANY] * 3),
    )(part, arrived[1], arrived[3], arrived[6])
    part = exchange(part, ("x", "y"))
    outputs, grad_inputs, grad_short, grad_one, grad_two = call(
        finish_kernel,
        (
            shape((1, rows, width), bf16),
            shape((1, rows, width), bf16),
            shape((3, 3 * width), f32),
            shape((rows, width), f32),
            shape((rows, width), f32),
        ),
    )(*arrived, in_weight, out_weight)
    part, grad_short = lax.optimization_barrier((part, grad_short))
    grad_in_weight, grad_out_weight = call(
        place_kernel, (shape((width, 3 * width), f32), shape((width, width), f32))
    )(part, swap_core(part))
    return (
        outputs,
        grad_inputs,
        grad_in_weight,
        grad_short,
        grad_one,
        grad_two,
        grad_out_weight,
    )


def solution(mesh):
    mesh = Mesh(mesh.devices.reshape(2, 4, 2, 4, 4), everyone)
    positions = ("x", "core", "zl", "y")
    split_rows, split_filter = P("zh", positions, None), P(positions, None)
    return jax.shard_map(
        per_device,
        mesh=mesh,
        in_specs=(split_rows, P(), P(), split_filter, split_filter, P(), split_rows),
        out_specs=(split_rows, split_rows, P(), P(), split_filter, split_filter, P()),
        check_vma=False,
    )
```
